512 devices in a mesh: dp: 64 (over z, y_lo, core), expert: 8 (over y_hi, x).
Axes of the slice: x: 4, y: 4 (y_hi: 2, y_lo: 2; y = y_hi * 2 + y_lo), z: 16, core: 2. Of those that a mesh axis runs over, the one named last changes fastest.
Arguments:
- tokens: bfloat16 [65536, 2048], P(('dp', 'expert')), may hold values from -24 to 24
- cotangent: bfloat16 [65536, 2048], P(('dp', 'expert')), may hold values from -24 to 24
- expert_ids: int32 [65536, 8], P(('dp', 'expert')), may hold values from 0 to 127, as said below
- route_weights: float32 [65536, 8], P(('dp', 'expert')), may hold values from 0.1 to 1
- join_groups: int32 [64], replicated, may hold values from 0 to 1
- w_gate: bfloat16 [2048, 1024], P('dp', 'expert'), may hold values from -0.125 to 0.125
- w_up: bfloat16 [2048, 1024], P('dp', 'expert'), may hold values from -0.125 to 0.125
- w_down: bfloat16 [2048, 1024], P('dp', 'expert'), may hold values from -0.1875 to 0.1875
Outputs:
- mixed: bfloat16 [65536, 2048], P(('dp', 'expert'))
- grad_gate: bfloat16 [2048, 1024], P('dp', 'expert')
- grad_up: bfloat16 [2048, 1024], P('dp', 'expert')
- grad_down: bfloat16 [2048, 1024], P('dp', 'expert')
The draws below stay inside these ranges and needn't reach their ends.
Inputs may be any that keep to these rules, and one draw needn't show every extreme that they name: `expert_ids`: each row names 8 different experts; the rows of one device name expert 0 at most 16 times, and the rows of some device exactly 16 times.
All inputs are finite; a program needn't handle non-finite values.
Results may differ from the reference program's by a relative error of at most 0.014.
Values may be sent and summed in bfloat16 or wider, within the bound.
No kernel may reach another device: no remote copies, remote signals or barrier semaphores. Data moves between devices by JAX's collectives and lax.ppermute only.
A program may use at most 64 MiB of HBM per device.

```python
import jax
import jax.numpy as jnp
from jax import lax

D = 2048
FF = 1024
NEXP_ALL = 128
TOP = 8
TOK_DEV = 128
CAP = 16
ROWS = 128
TOKENS = 65536
N_DP = 64
N_EXPERT = 8


def draw_expert_ids(key, part):
    key_count, key_pick, key_order, key_rest, key_turn = jax.random.split(key, 5)
    blocks = TOKENS // TOK_DEV
    counts = jax.random.randint(key_count, (blocks,), CAP // 4, CAP + 1)
    special = jax.random.randint(key_pick, (), 0, blocks)
    counts = jnp.where(jnp.arange(blocks) == special, CAP, counts)
    orders = jax.vmap(lambda sub_key: jax.random.permutation(sub_key, TOK_DEV))(jax.random.split(key_order, blocks))
    routed = (orders < counts[:, None]).reshape(TOKENS)
    scores = jax.random.randint(key_rest, (TOKENS, NEXP_ALL - 1), 0, 2 ** 30)
    others = 1 + jnp.argsort(scores, axis=-1)[:, :TOP]
    first = jnp.where(routed, 0, others[:, TOP - 1])
    chosen = jnp.concatenate([first[:, None], others[:, :TOP - 1]], axis=1)
    turns = jax.random.randint(key_turn, (TOKENS, 1), 0, TOP)
    index = (jnp.arange(TOP)[None, :] + turns) % TOP
    return jnp.take_along_axis(chosen, index, axis=1).astype(jnp.int32)


def set_ends(drawn, own_key, least, top_value):
    place = [jax.random.randint(jax.random.fold_in(own_key, axis), (), 0, length) for axis, length in enumerate(drawn.shape)]
    longest = drawn.shape.index(max(drawn.shape))
    next_to = place[:longest] + [(place[longest] + 1) % drawn.shape[longest]] + place[longest + 1:]
    return drawn.at[tuple(place)].set(least).at[tuple(next_to)].set(top_value)


def with_spikes(entries, rng, source, target, parts, factor):
    def block_of(dim):
        return (jnp.arange(entries.shape[dim]) // (entries.shape[dim] // parts)).reshape((-1,) + (1,) * (entries.ndim - 1 - dim))

    near = jax.random.permutation(rng, parts)[block_of(target)]
    second = (block_of(target) + parts // 2) % parts
    return jnp.where((block_of(source) == near) | (block_of(source) == second), factor * entries, entries)


def block_levels(own_key, shape, cuts, least, high):
    loudness, own = 1.0, jax.random.fold_in(own_key, 6)
    for dim, blocks in cuts:
        draws = jnp.exp(jax.random.uniform(jax.random.fold_in(own, dim), (blocks,), jnp.float32, least / len(cuts), high / len(cuts)))
        loudness = loudness * jnp.repeat(draws, shape[dim] // blocks).reshape([-1 if axis == dim else 1 for axis in range(len(shape))])
    return loudness


def scatter_about(key, extent, spread, bound, cuts=(), held_as=jnp.bfloat16):
    drawn = spread * jax.random.normal(key, extent, jnp.float32)
    if cuts:
        drawn = drawn * block_levels(key, extent, cuts, -0.22, 0.18)
    return jnp.clip(drawn, -bound, bound).astype(held_as)


def bell_draw_with(own_key, shape, spread, most, pieces, heavy, kind=jnp.bfloat16):
    values = spread * jax.random.normal(own_key, shape, jnp.float32)
    if pieces:
        values = values * block_levels(own_key, shape, pieces, -0.22, 0.18)
    return jnp.clip(with_spikes(values, jax.random.fold_in(own_key, 3), *heavy), -most, most).astype(kind)


def setup_inputs(seed: int = 0) -> dict:
    key_of = jax.random.split(jax.random.key(seed), 9)
    return {
        "tokens": bell_draw_with(key_of[0], (TOKENS, D), 1.0, 24.0, ((0, 512),), (0, 1, 512, 6.0)),
        "cotangent": bell_draw_with(key_of[1], (TOKENS, D), 1.0, 24.0, ((0, 512),), (0, 1, 512, 6.0)),
        "expert_ids": draw_expert_ids(jax.random.fold_in(key_of[8], 71), 0),
        "route_weights": jnp.clip(0.1 + 0.9 * jax.random.uniform(key_of[3], (TOKENS, TOP), jnp.float32) ** block_levels(key_of[3], (TOKENS, TOP), ((0, 512),), -0.2, 0.2), 0.1, 1.0),
        "join_groups": set_ends(jax.random.randint(key_of[4], (N_DP,), 0, 2), jax.random.fold_in(key_of[4], 1), 0, 1).astype(jnp.int32),
        "w_gate": scatter_about(key_of[5], (D, FF), D ** -0.5, 0.125, ((0, 64), (1, 8))),
        "w_up": scatter_about(key_of[6], (D, FF), D ** -0.5, 0.125, ((0, 64), (1, 8))),
        "w_down": scatter_about(key_of[7], (D, FF), FF ** -0.5, 0.1875, ((0, 64), (1, 8))),
    }


def reference(tokens, cotangent, expert_ids, route_weights, join_groups, w_gate, w_up, w_down):
    expert_count = N_EXPERT
    slice_width = FF // expert_count
    highest = lax.Precision.HIGHEST
    slot_ids = jnp.arange(CAP, dtype=jnp.int32)
    tok_groups = tokens.reshape(N_DP, expert_count, TOK_DEV, D)
    cot_groups = cotangent.reshape(N_DP, expert_count, TOK_DEV, D)
    id_groups = expert_ids.reshape(N_DP, expert_count, TOK_DEV, TOP)
    wt_groups = route_weights.reshape(N_DP, expert_count, TOK_DEV, TOP)

    def group_step(running, member):
        tok_block, cot_block, id_block, wt_block, joined = member
        chosen_mask = id_block == 0
        routed = jnp.any(chosen_mask, -1)
        weight = jnp.sum(jnp.where(chosen_mask, wt_block, 0.0), -1)
        places = jnp.cumsum(routed.astype(jnp.int32), -1) - 1
        chooser = ((places[:, None, :] == slot_ids[None, :, None]) & routed[:, None, :]).astype(jnp.float32)
        picked = jnp.einsum('ect,etd->ecd', chooser, tok_block.astype(jnp.float32), precision=highest)
        picked = picked.astype(jnp.bfloat16).reshape(ROWS, D)
        gate_acts = jnp.dot(picked, w_gate, preferred_element_type=jnp.float32)
        up_acts = jnp.dot(picked, w_up, preferred_element_type=jnp.float32)
        hidden = (jax.nn.silu(gate_acts) * up_acts).astype(jnp.bfloat16)
        partials = jnp.einsum('rjf,djf->jrd', hidden.reshape(ROWS, expert_count, slice_width).astype(jnp.float32),
                              w_down.reshape(D, expert_count, slice_width).astype(jnp.float32), precision=highest)
        out_rows = jnp.sum(partials.astype(jnp.bfloat16).astype(jnp.float32), 0).reshape(expert_count, CAP, D)
        mixed = jnp.einsum('ect,ecd->etd', chooser, out_rows, precision=highest) * weight[..., None]
        mixed = mixed.astype(jnp.bfloat16)
        scaled = cot_block.astype(jnp.float32) * weight[..., None]
        dpicked = jnp.einsum('ect,etd->ecd', chooser, scaled, precision=highest).astype(jnp.bfloat16).reshape(ROWS, D)
        hidden_grad = jnp.dot(dpicked, w_down, preferred_element_type=jnp.float32)
        sigma_gate = jax.nn.sigmoid(gate_acts)
        dgate = (hidden_grad * up_acts * sigma_gate * (1.0 + gate_acts * (1.0 - sigma_gate))).astype(jnp.bfloat16)
        dup = (hidden_grad * gate_acts * sigma_gate).astype(jnp.bfloat16)
        dims = (((0,), (0,)), ((), ()))
        term_gate = lax.dot_general(picked, dgate, dims, preferred_element_type=jnp.float32)
        term_up = lax.dot_general(picked, dup, dims, preferred_element_type=jnp.float32)
        term_down = lax.dot_general(dpicked, hidden, dims, preferred_element_type=jnp.float32)
        active = 1.0 - joined.astype(jnp.float32)
        running = running + active * jnp.stack([term_gate, term_up, term_down])
        return running, mixed

    start = jnp.zeros((3, D, FF), jnp.float32)
    sums, mixed_all = lax.scan(group_step, start, (tok_groups, cot_groups, id_groups, wt_groups, join_groups))
    return (mixed_all.reshape(TOKENS, D), sums[0].astype(jnp.bfloat16),
            sums[1].astype(jnp.bfloat16), sums[2].astype(jnp.bfloat16))
```

```python
import jax
import jax.numpy as jnp
from jax import lax
from jax.experimental import pallas as pl
from jax.experimental.pallas import tpu as pltpu
from jax.sharding import Mesh
from jax.sharding import PartitionSpec as P

AXES = ("z", "y", "c", "h", "x")
PLANE = ("y", "h", "x")
SWAP = ((0, 1), (1, 0))
VMEM_LIMIT = 40 * 1024 * 1024
PARAMS = pltpu.CompilerParams(vmem_limit_bytes=VMEM_LIMIT)
ROW_DIMS = (((0,), (0,)), ((), ()))
LANE_DIMS = (((1,), (1,)), ((), ()))


def whole(n):
    return [pl.BlockSpec(memory_space=pltpu.VMEM) for _ in range(n)]


def lanes(shape):
    return lax.broadcasted_iota(jnp.int32, shape, 1)


def halves_swapped(a):
    half = a.shape[1] // 2
    return pltpu.roll(a.astype(jnp.float32), half, 1)


def route_kernel(ids_ref, share_ref, tokens_ref, cot_ref, both_ref, place_ref, slot_weight_ref):
    count = ids_ref.shape[0]
    slots = both_ref.shape[0] // 2
    chosen = ids_ref[...] == 0
    routed = jnp.max(chosen.astype(jnp.float32), axis=1, keepdims=True)
    weight = jnp.sum(jnp.where(chosen, share_ref[...], 0.0), axis=1, keepdims=True)
    square = (count, count)
    below = lax.broadcasted_iota(jnp.int32, square, 0) >= lanes(square)
    before = jnp.dot(
        below.astype(jnp.bfloat16),
        jnp.broadcast_to(routed, square).astype(jnp.bfloat16),
        preferred_element_type=jnp.float32,
    )
    at_slot = (before - 1.0 == lanes(square).astype(jnp.float32)) & (routed > 0.0)
    place = at_slot.astype(jnp.float32)
    chooser = place.T[:slots].astype(jnp.bfloat16)
    slot_weight = jnp.sum((place * weight).T[:slots], axis=1, keepdims=True)
    picked = jnp.dot(chooser, tokens_ref[...], preferred_element_type=jnp.float32)
    dpicked = jnp.dot(chooser, cot_ref[...], preferred_element_type=jnp.float32) * slot_weight
    both_ref[:slots, :] = picked.astype(jnp.bfloat16)
    both_ref[slots:, :] = dpicked.astype(jnp.bfloat16)
    place_ref[...] = place.astype(jnp.bfloat16)
    slot_weight_ref[...] = jnp.broadcast_to(slot_weight, slot_weight_ref.shape)


def route(ids, share, tokens, cot):
    count, width = tokens.shape
    slots = count // 8
    return pl.pallas_call(
        route_kernel,
        out_shape=(
            jax.ShapeDtypeStruct((2 * slots, width), jnp.bfloat16),
            jax.ShapeDtypeStruct((count, count), jnp.bfloat16),
            jax.ShapeDtypeStruct((slots, 128), jnp.float32),
        ),
        in_specs=whole(4),
        out_specs=tuple(whole(3)),
        compiler_params=PARAMS,
        name="route",
    )(ids, share, tokens, cot)


def half_kernel(gate_ref, up_ref, mine_ref, other_ref):
    gate, up = gate_ref[...].astype(jnp.float32), up_ref[...].astype(jnp.float32)
    low = lanes(gate.shape) < gate.shape[1] // 2
    first = jnp.where(low, gate, halves_swapped(up)).astype(jnp.bfloat16)
    second = jnp.where(low, halves_swapped(gate), up).astype(jnp.bfloat16)
    top = lax.axis_index("y") == 0
    mine_ref[...] = jnp.where(top, first, second)
    other_ref[...] = jnp.where(top, second, first)


def split_columns(gate, up):
    return pl.pallas_call(
        half_kernel,
        out_shape=(jax.ShapeDtypeStruct(gate.shape, gate.dtype),) * 2,
        in_specs=whole(2),
        out_specs=tuple(whole(2)),
        name="split_columns",
    )(gate, up)


def pack_kernel(mine_ref, got_ref, down_ref, packed_ref):
    rows = mine_ref.shape[0]
    top = lax.axis_index("y") == 0
    mine, got = mine_ref[...], got_ref[:rows, :]
    packed_ref[:rows, :] = jnp.where(top, mine, got)
    packed_ref[rows : 2 * rows, :] = jnp.where(top, got, mine)
    down, their_down = down_ref[...].astype(jnp.float32), got_ref[rows:, :].astype(jnp.float32)
    low = lanes(down.shape) < down.shape[1] // 2
    if_top = jnp.where(low, down, halves_swapped(their_down))
    if_not = jnp.where(low, halves_swapped(their_down), down)
    packed_ref[2 * rows :, :] = jnp.where(top, if_top, if_not).astype(jnp.bfloat16)


def pack_shards(mine, got, down):
    rows, width = mine.shape
    return pl.pallas_call(
        pack_kernel,
        out_shape=jax.ShapeDtypeStruct((3 * rows, width), mine.dtype),
        in_specs=whole(3),
        out_specs=whole(1)[0],
        name="pack_shards",
    )(mine, got, down)


def expert_kernel(
    join_ref, both_ref, packed_ref, partial_ref, send_ref, keep_ref, gate_up, down, terms
):
    chips = packed_ref.shape[1]
    rows = packed_ref.shape[2] // 3
    width = packed_ref.shape[3]
    half = width // 2
    peers, slots = both_ref.shape[0], both_ref.shape[1] // 2
    depth = both_ref.shape[2]
    z, c = lax.axis_index("z"), lax.axis_index("c")
    for chip in range(chips):
        for core in range(2):
            block = packed_ref[core, chip, 2 * rows :, :].astype(jnp.float32)
            turned = pltpu.roll(block, half, 1)
            low = lanes(block.shape) < half
            doubled = (jnp.where(low, block, turned), jnp.where(low, turned, block))
            for y in range(2):
                at = ((chip * 2 + y) * 2 + core) * rows
                gate_up[at : at + rows, :] = packed_ref[core, chip, y * rows : (y + 1) * rows, :]
                down[at : at + rows, :] = doubled[y].astype(jnp.bfloat16)
    total = peers * slots
    picked = both_ref[:, :slots, :].reshape(total, depth)
    dpicked = both_ref[:, slots:, :].reshape(total, depth)
    acts = jnp.dot(picked, gate_up[...], preferred_element_type=jnp.float32)
    turned = pltpu.roll(acts, half, 1)
    low = lanes(acts.shape) < half
    gate, up = jnp.where(low, acts, turned), jnp.where(low, turned, acts)
    sigma = jax.nn.sigmoid(gate)
    hidden = gate * sigma * up
    hidden_half = hidden.astype(jnp.bfloat16)
    partial = lax.dot_general(
        jnp.where(low, hidden, 0.0).astype(jnp.bfloat16),
        down[...],
        LANE_DIMS,
        preferred_element_type=jnp.float32,
    )
    partial_ref[...] = partial.astype(jnp.bfloat16).reshape(partial_ref.shape)
    dhidden = jnp.dot(dpicked, down[...], preferred_element_type=jnp.float32)
    dgate = dhidden * up * sigma * (1.0 + gate * (1.0 - sigma))
    dup = dhidden * gate * sigma
    first = 1.0 - join_ref[(z * 2 + 0) * 2 + c].astype(jnp.float32)
    second = 1.0 - join_ref[(z * 2 + 1) * 2 + c].astype(jnp.float32)
    group = lax.broadcasted_iota(jnp.int32, acts.shape, 0) // (total // 2)
    active = jnp.where(group == 0, first, second)
    dacts = (jnp.where(low, dgate, dup) * active).astype(jnp.bfloat16)
    counted = (hidden_half.astype(jnp.float32) * active).astype(jnp.bfloat16)
    terms[0] = lax.dot_general(picked, dacts, ROW_DIMS, preferred_element_type=jnp.float32)
    terms[1] = lax.dot_general(dpicked, counted, ROW_DIMS, preferred_element_type=jnp.float32)
    half_rows = rows // 2
    low = lanes((half_rows, width)) < half
    for chip in range(chips):
        for y in range(2):
            base = (chip * 2 + y) * 2 * rows
            for which, ref in ((c, keep_ref), (1 - c, send_ref)):
                at = pl.multiple_of(base + which * rows, rows)
                ref[chip, y, :rows, :] = terms[0, pl.ds(at, rows), :].astype(ref.dtype)
                packed = jnp.where(
                    low,
                    terms[1, pl.ds(at, half_rows), :],
                    terms[1, pl.ds(at + half_rows, half_rows), :],
                )
                ref[chip, y, rows:, :] = packed.astype(ref.dtype)


def expert(join, both, packed):
    peers, doubled, depth = both.shape
    slots = doubled // 2
    _, chips, rows, width = packed.shape
    chunk = (chips, 2, rows // 2, width)
    return pl.pallas_call(
        expert_kernel,
        out_shape=(
            jax.ShapeDtypeStruct((peers, slots, depth), jnp.bfloat16),
            jax.ShapeDtypeStruct(chunk, jnp.bfloat16),
            jax.ShapeDtypeStruct(chunk, jnp.float32),
        ),
        in_specs=[pl.BlockSpec(memory_space=pltpu.SMEM), *whole(2)],
        out_specs=tuple(whole(3)),
        scratch_shapes=[
            pltpu.VMEM((depth, width), jnp.bfloat16),
            pltpu.VMEM((depth, width), jnp.bfloat16),
            pltpu.VMEM((2, depth, width), jnp.float32),
        ],
        compiler_params=PARAMS,
        name="expert",
    )(join, both, packed)


def mix_kernel(blocks_ref, place_ref, slot_weight_ref, mixed_ref):
    slots = blocks_ref.shape[1]
    total = blocks_ref[0].astype(jnp.float32)
    for k in range(1, blocks_ref.shape[0]):
        total += blocks_ref[k].astype(jnp.float32)
    weighted = (total * slot_weight_ref[:, :1]).astype(jnp.bfloat16)
    mixed_ref[...] = jnp.dot(
        place_ref[:, :slots], weighted, preferred_element_type=jnp.float32
    ).astype(jnp.bfloat16)


def mix(blocks, place, slot_weight):
    return pl.pallas_call(
        mix_kernel,
        out_shape=jax.ShapeDtypeStruct((place.shape[0], blocks.shape[2]), jnp.bfloat16),
        in_specs=whole(3),
        out_specs=whole(1)[0],
        compiler_params=PARAMS,
        name="mix",
    )(blocks, place, slot_weight)


def finish_kernel(blocks_ref, gate_ref, up_ref, down_ref):
    rows, width = gate_ref.shape
    half = width // 2
    sums = [blocks_ref[y].astype(jnp.float32) for y in range(2)]
    for k in range(2, blocks_ref.shape[0], 2):
        for y in range(2):
            sums[y] += blocks_ref[k + y].astype(jnp.float32)
    low = lanes(sums[0].shape) < half
    firsts = jnp.where(low, sums[0], pltpu.roll(sums[1], half, 1)).astype(jnp.bfloat16)
    seconds = jnp.where(low, pltpu.roll(sums[0], half, 1), sums[1]).astype(jnp.bfloat16)
    gate_ref[...] = firsts[:rows]
    up_ref[...] = seconds[:rows]
    down_ref[: rows // 2, :] = firsts[rows:]
    down_ref[rows // 2 :, :] = seconds[rows:]


def finish(blocks):
    _, packed_rows, width = blocks.shape
    shape = jax.ShapeDtypeStruct((packed_rows // 3 * 2, width), jnp.bfloat16)
    return pl.pallas_call(
        finish_kernel,
        out_shape=(shape,) * 3,
        in_specs=whole(1),
        out_specs=tuple(whole(3)),
        name="finish",
    )(blocks)


def per_device(tokens, cotangent, expert_ids, route_weights, join_groups, w_gate, w_up, w_down):
    plane = lax.axis_size(PLANE)
    chips = lax.axis_size("z")
    mine, other = split_columns(w_gate, w_up)
    got = lax.ppermute(jnp.concatenate([other, w_down]), "y", SWAP)
    both, place, slot_weight = route(expert_ids, route_weights, tokens, cotangent)
    packed = pack_shards(mine, got, w_down)
    copies = jnp.broadcast_to(both, (plane, *both.shape))
    rows_in = lax.all_to_all(copies, PLANE, 0, 0, tiled=True)
    along = lax.all_gather(packed, "z", axis=0, tiled=False)
    gathered = lax.all_gather(along, "c", axis=0, tiled=False)
    partial, send, keep = expert(join_groups, rows_in, gathered)
    blocks = lax.all_to_all(partial, PLANE, 0, 0, tiled=True)
    from_core = lax.ppermute(send, "c", SWAP)
    chip_sum = (keep + from_core.astype(jnp.float32)).astype(jnp.bfloat16)
    chip_sum = chip_sum.reshape(chips * 2, *chip_sum.shape[2:])
    pieces = lax.all_to_all(chip_sum, ("z", "y"), 0, 0, tiled=True)
    mixed = mix(blocks, place, slot_weight)
    return (mixed, *finish(pieces))


def solution(mesh):
    experts = mesh.shape["expert"]
    split = Mesh(mesh.devices.reshape(-1, 2, 2, 2, experts // 2), AXES)
    dp = ("z", "y", "c")
    tok, weight = P(AXES, None), P(dp, ("h", "x"))
    return jax.shard_map(
        per_device,
        mesh=split,
        in_specs=(tok, tok, tok, tok, P(), weight, weight, weight),
        out_specs=(tok, weight, weight, weight),
        check_vma=False,
    )
```

```python
import jax
import jax.numpy as jnp
from jax import lax
from jax.experimental import pallas as pl
from jax.experimental.pallas import tpu as pltpu
from jax.sharding import Mesh
from jax.sharding import PartitionSpec as P

AXES = ("z", "y", "c", "h", "x")
RING = ("y", "h")
PLANE = ("y", "h", "x")
HBM = pl.BlockSpec(memory_space=pltpu.HBM)
SWAP = ((0, 1), (1, 0))
ROW_DIMS = (((0,), (0,)), ((), ()))
LANE_DIMS = (((1,), (1,)), ((), ()))


def whole(n):
    return [pl.BlockSpec(memory_space=pltpu.VMEM) for _ in range(n)]


def lanes(shape):
    return lax.broadcasted_iota(jnp.int32, shape, 1)


def halves_swapped(a):
    half = a.shape[1] // 2
    return pltpu.roll(a.astype(jnp.float32), half, 1)


def params(mib):
    return pltpu.CompilerParams(vmem_limit_bytes=mib * 1024 * 1024)


def route_kernel(
    ids_ref, share_ref, tokens_ref, cot_ref, copies_ref, chooser_ref, slot_weight_ref,
    held_tokens, held_cot, both, in_sems, out_sem,
):
    count = ids_ref.shape[1]
    slots = chooser_ref.shape[0]
    reads = [
        pltpu.make_async_copy(tokens_ref, held_tokens, in_sems.at[0]),
        pltpu.make_async_copy(cot_ref, held_cot, in_sems.at[1]),
    ]
    for read in reads:
        read.start()
    chosen = ids_ref[...] == 0
    routed = jnp.max(chosen.astype(jnp.float32), axis=0, keepdims=True)
    weight = jnp.sum(jnp.where(chosen, share_ref[...], 0.0), axis=0, keepdims=True)
    square = (count, count)
    until = lax.broadcasted_iota(jnp.int32, square, 0) <= lanes(square)
    before = jnp.dot(
        jnp.broadcast_to(routed, (slots, count)).astype(jnp.bfloat16),
        until.astype(jnp.bfloat16),
        preferred_element_type=jnp.float32,
    )
    slot = lax.broadcasted_iota(jnp.int32, (slots, count), 0).astype(jnp.float32)
    place = jnp.where((before - 1.0 == slot) & (routed > 0.0), 1.0, 0.0)
    chooser = place.astype(jnp.bfloat16)
    slot_weight = jnp.sum(place * weight, axis=1, keepdims=True)
    chooser_ref[...] = chooser
    slot_weight_ref[...] = jnp.broadcast_to(slot_weight, slot_weight_ref.shape)
    reads[0].wait()
    picked = jnp.dot(chooser, held_tokens[...], preferred_element_type=jnp.float32)
    both[:slots, :] = picked.astype(jnp.bfloat16)
    reads[1].wait()
    dpicked = jnp.dot(chooser, held_cot[...], preferred_element_type=jnp.float32) * slot_weight
    both[slots:, :] = dpicked.astype(jnp.bfloat16)
    writes = [
        pltpu.make_async_copy(both, copies_ref.at[k], out_sem.at[k])
        for k in range(copies_ref.shape[0])
    ]
    for write in writes:
        write.start()
    for write in writes:
        write.wait()


def route(ids, share, tokens, cot, peers):
    count, width = tokens.shape
    slots = count // 8
    return pl.pallas_call(
        route_kernel,
        out_shape=(
            jax.ShapeDtypeStruct((peers, 2 * slots, width), jnp.bfloat16),
            jax.ShapeDtypeStruct((slots, count), jnp.bfloat16),
            jax.ShapeDtypeStruct((slots, 128), jnp.float32),
        ),
        in_specs=[*whole(2), HBM, HBM],
        out_specs=(HBM, *whole(2)),
        scratch_shapes=[
            pltpu.VMEM((count, width), jnp.bfloat16),
            pltpu.VMEM((count, width), jnp.bfloat16),
            pltpu.VMEM((2 * slots, width), jnp.bfloat16),
            pltpu.SemaphoreType.DMA((2,)),
            pltpu.SemaphoreType.DMA((peers,)),
        ],
        compiler_params=params(56),
        name="route",
    )(ids.T, share.T, tokens, cot)


def half_kernel(gate_ref, up_ref, down_ref, mine_ref, other_ref):
    gate, up = gate_ref[...].astype(jnp.float32), up_ref[...].astype(jnp.float32)
    rows = gate.shape[0]
    low = lanes(gate.shape) < gate.shape[1] // 2
    first = jnp.where(low, gate, halves_swapped(up)).astype(jnp.bfloat16)
    second = jnp.where(low, halves_swapped(gate), up).astype(jnp.bfloat16)
    top = lax.axis_index("y") == 0
    mine_ref[:rows, :] = jnp.where(top, first, second)
    mine_ref[rows:, :] = down_ref[...]
    other_ref[:rows, :] = jnp.where(top, second, first)
    other_ref[rows:, :] = down_ref[...]


def split_columns(gate, up, down):
    rows, width = gate.shape
    return pl.pallas_call(
        half_kernel,
        out_shape=(jax.ShapeDtypeStruct((2 * rows, width), gate.dtype),) * 2,
        in_specs=whole(3),
        out_specs=tuple(whole(2)),
        compiler_params=params(56),
        name="split_columns",
    )(gate, up, down)


def pack_kernel(mine_ref, got_ref, packed_ref):
    rows = mine_ref.shape[0] // 2
    top = lax.axis_index("y") == 0
    mine, got = mine_ref[:rows, :], got_ref[:rows, :]
    packed_ref[:rows, :] = jnp.where(top, mine, got)
    packed_ref[rows : 2 * rows, :] = jnp.where(top, got, mine)
    down, their_down = (ref[rows:, :].astype(jnp.float32) for ref in (mine_ref, got_ref))
    low = lanes(down.shape) < down.shape[1] // 2
    if_top = jnp.where(low, down, halves_swapped(their_down))
    if_not = jnp.where(low, halves_swapped(their_down), down)
    packed_ref[2 * rows :, :] = jnp.where(top, if_top, if_not).astype(jnp.bfloat16)


def pack_shards(mine, got):
    rows, width = mine.shape
    return pl.pallas_call(
        pack_kernel,
        out_shape=jax.ShapeDtypeStruct((3 * rows // 2, width), mine.dtype),
        in_specs=whole(2),
        out_specs=whole(1)[0],
        compiler_params=params(56),
        name="pack_shards",
    )(mine, got)


def expert_kernel(
    join_ref, both_ref, packed_ref, partial_0, partial_1, partial_2, partial_3, send_ref, keep_ref,
    gate_up, down, terms, partials,
):
    chips = packed_ref.shape[1]
    rows = packed_ref.shape[2] // 3
    width = packed_ref.shape[3]
    half = width // 2
    peers, slots = both_ref.shape[0], both_ref.shape[1] // 2
    depth = both_ref.shape[2]
    z, c = lax.axis_index("z"), lax.axis_index("c")
    for chip in range(chips):
        for core in range(2):
            block = packed_ref[core, chip, 2 * rows :, :].astype(jnp.float32)
            turned = pltpu.roll(block, half, 1)
            low = lanes(block.shape) < half
            doubled = (jnp.where(low, block, turned), jnp.where(low, turned, block))
            for y in range(2):
                at = ((chip * 2 + y) * 2 + core) * rows
                gate_up[at : at + rows, :] = packed_ref[core, chip, y * rows : (y + 1) * rows, :]
                down[at : at + rows, :] = doubled[y].astype(jnp.bfloat16)
    total = peers * slots
    picked = both_ref[:, :slots, :].reshape(total, depth)
    dpicked = both_ref[:, slots:, :].reshape(total, depth)
    acts = jnp.dot(picked, gate_up[...], preferred_element_type=jnp.float32)
    turned = pltpu.roll(acts, half, 1)
    low = lanes(acts.shape) < half
    gate, up = jnp.where(low, acts, turned), jnp.where(low, turned, acts)
    sigma = jax.nn.sigmoid(gate)
    hidden = gate * sigma * up
    hidden_half = hidden.astype(jnp.bfloat16)
    partial = lax.dot_general(
        jnp.where(low, hidden, 0.0).astype(jnp.bfloat16),
        down[...],
        LANE_DIMS,
        preferred_element_type=jnp.float32,
    )
    partials[...] = partial.reshape(partials.shape)
    x, ring = lax.axis_index("x"), lax.axis_index("h") * 2 + lax.axis_index("y")
    for step, ref in enumerate((partial_0, partial_1, partial_2, partial_3)):
        for turn in range(4):
            place = lax.rem(ring + turn, 4)
            peer = (lax.rem(place, 2) * 2 + place // 2) * 4 + lax.rem(x + step, 4)
            ref[turn] = partials[peer].astype(ref.dtype)
    dhidden = jnp.dot(dpicked, down[...], preferred_element_type=jnp.float32)
    dgate = dhidden * up * sigma * (1.0 + gate * (1.0 - sigma))
    dup = dhidden * gate * sigma
    first = 1.0 - join_ref[(z * 2 + 0) * 2 + c].astype(jnp.float32)
    second = 1.0 - join_ref[(z * 2 + 1) * 2 + c].astype(jnp.float32)
    group = lax.broadcasted_iota(jnp.int32, acts.shape, 0) // (total // 2)
    active = jnp.where(group == 0, first, second)
    dacts = (jnp.where(low, dgate, dup) * active).astype(jnp.bfloat16)
    counted = (hidden_half.astype(jnp.float32) * active).astype(jnp.bfloat16)
    terms[0] = lax.dot_general(picked, dacts, ROW_DIMS, preferred_element_type=jnp.float32)
    terms[1] = lax.dot_general(dpicked, counted, ROW_DIMS, preferred_element_type=jnp.float32)
    half_rows = rows // 2
    low = lanes((half_rows, width)) < half
    for chip in range(chips):
        for y in range(2):
            base = (chip * 2 + y) * 2 * rows
            for which, ref in ((c, keep_ref), (1 - c, send_ref)):
                at = pl.multiple_of(base + which * rows, rows)
                ref[chip, y, :rows, :] = terms[0, pl.ds(at, rows), :].astype(ref.dtype)
                packed = jnp.where(
                    low,
                    terms[1, pl.ds(at, half_rows), :],
                    terms[1, pl.ds(at + half_rows, half_rows), :],
                )
                ref[chip, y, rows:, :] = packed.astype(ref.dtype)


def expert(join, both, packed):
    peers, doubled, depth = both.shape
    slots = doubled // 2
    _, chips, rows, width = packed.shape
    chunk = (chips, 2, rows // 2, width)
    quarter = jax.ShapeDtypeStruct((peers // 4, slots, depth), jnp.bfloat16)
    return pl.pallas_call(
        expert_kernel,
        out_shape=(
            quarter, quarter, quarter, quarter,
            jax.ShapeDtypeStruct(chunk, jnp.bfloat16),
            jax.ShapeDtypeStruct(chunk, jnp.float32),
        ),
        in_specs=[pl.BlockSpec(memory_space=pltpu.SMEM), *whole(2)],
        out_specs=tuple(whole(6)),
        scratch_shapes=[
            pltpu.VMEM((depth, width), jnp.bfloat16),
            pltpu.VMEM((depth, width), jnp.bfloat16),
            pltpu.VMEM((2, depth, width), jnp.float32),
            pltpu.VMEM((peers, slots, depth), jnp.float32),
        ],
        compiler_params=params(24),
        name="expert",
    )(join, both, packed)


def add_kernel(own_ref, *refs):
    total = own_ref[...].astype(jnp.float32)
    for ref in refs[:3]:
        total += ref[...].astype(jnp.float32)
    for k, ref in enumerate(refs[3:]):
        ref[...] = total[k].astype(ref.dtype)


def add_quarters(parts):
    turns, slots, depth = parts[0].shape
    return pl.pallas_call(
        add_kernel,
        out_shape=(jax.ShapeDtypeStruct((slots, depth), jnp.bfloat16),) * turns,
        in_specs=whole(4),
        out_specs=tuple(whole(turns)),
        compiler_params=params(8),
        name="add_quarters",
    )(*parts)


def mix_kernel(own_ref, first_ref, second_ref, third_ref, chooser_ref, slot_weight_ref, mixed_ref):
    total = own_ref[...].astype(jnp.float32)
    for ref in (first_ref, second_ref, third_ref):
        total += ref[...].astype(jnp.float32)
    weighted = (total * slot_weight_ref[:, :1]).astype(jnp.bfloat16)
    mixed_ref[...] = lax.dot_general(
        chooser_ref[...], weighted, ROW_DIMS, preferred_element_type=jnp.float32
    ).astype(jnp.bfloat16)


def mix(parts, chooser, slot_weight):
    return pl.pallas_call(
        mix_kernel,
        out_shape=jax.ShapeDtypeStruct((chooser.shape[1], parts[0].shape[1]), jnp.bfloat16),
        in_specs=whole(6),
        out_specs=whole(1)[0],
        compiler_params=params(8),
        name="mix",
    )(*parts, chooser, slot_weight)


def finish_kernel(blocks_ref, gate_ref, up_ref, down_ref):
    rows, width = gate_ref.shape
    half = width // 2
    sums = [blocks_ref[y].astype(jnp.float32) for y in range(2)]
    for k in range(2, blocks_ref.shape[0], 2):
        for y in range(2):
            sums[y] += blocks_ref[k + y].astype(jnp.float32)
    low = lanes(sums[0].shape) < half
    firsts = jnp.where(low, sums[0], pltpu.roll(sums[1], half, 1)).astype(jnp.bfloat16)
    seconds = jnp.where(low, pltpu.roll(sums[0], half, 1), sums[1]).astype(jnp.bfloat16)
    gate_ref[...] = firsts[:rows]
    up_ref[...] = seconds[:rows]
    down_ref[: rows // 2, :] = firsts[rows:]
    down_ref[rows // 2 :, :] = seconds[rows:]


def finish(blocks):
    _, packed_rows, width = blocks.shape
    shape = jax.ShapeDtypeStruct((packed_rows // 3 * 2, width), jnp.bfloat16)
    return pl.pallas_call(
        finish_kernel,
        out_shape=(shape,) * 3,
        in_specs=whole(1),
        out_specs=tuple(whole(3)),
        compiler_params=params(4),
        name="finish",
    )(blocks)


def spread(parts, axes, ring):
    came = [
        lax.ppermute(part, axes, [(ring[i], ring[(i + k) % 4]) for i in range(4)])
        for k, part in enumerate(parts)
        if k
    ]
    return [parts[0], *came]


def per_device(tokens, cotangent, expert_ids, route_weights, join_groups, w_gate, w_up, w_down):
    plane = lax.axis_size(PLANE)
    chips = lax.axis_size("z")
    mine, other = split_columns(w_gate, w_up, w_down)
    got = lax.ppermute(other, "y", SWAP)
    copies, chooser, slot_weight = route(expert_ids, route_weights, tokens, cotangent, plane)
    packed = pack_shards(mine, got)
    packed, copies = lax.optimization_barrier((packed, copies))
    rows_in = lax.all_to_all(copies, PLANE, 0, 0, tiled=True)
    along = lax.all_gather(packed, "z", axis=0, tiled=False)
    gathered = lax.all_gather(along, "c", axis=0, tiled=False)
    *partials, send, keep = expert(join_groups, rows_in, gathered)
    from_core = lax.ppermute(send, "c", SWAP)
    chip_sum = (keep + from_core.astype(jnp.float32)).astype(jnp.bfloat16)
    chip_sum = chip_sum.reshape(chips * 2, *chip_sum.shape[2:])
    chip_sum, partials = lax.optimization_barrier((chip_sum, partials))
    pieces = lax.all_to_all(chip_sum, ("z", "y"), 0, 0, tiled=True)
    quarters = add_quarters(spread(partials, "x", (0, 1, 2, 3)))
    mixed = mix(spread(quarters, RING, (0, 2, 1, 3)), chooser, slot_weight)
    return (mixed, *finish(pieces))


def solution(mesh):
    experts = mesh.shape["expert"]
    split = Mesh(mesh.devices.reshape(-1, 2, 2, 2, experts // 2), AXES)
    dp = ("z", "y", "c")
    tok, weight = P(AXES, None), P(dp, ("h", "x"))
    return jax.shard_map(
        per_device,
        mesh=split,
        in_specs=(tok, tok, tok, tok, P(), weight, weight, weight),
        out_specs=(tok, weight, weight, weight),
        check_vma=False,
    )
```

```python
import jax
import jax.numpy as jnp
from jax import lax
from jax.experimental import pallas as pl
from jax.experimental.pallas import tpu as pltpu
from jax.sharding import Mesh
from jax.sharding import PartitionSpec as P

AXES = ("z", "y", "c", "h", "x")
RING = ("y", "h")
PLANE = ("y", "h", "x")
HBM = pl.BlockSpec(memory_space=pltpu.HBM)
SWAP = ((0, 1), (1, 0))
ROW_DIMS = (((0,), (0,)), ((), ()))
LANE_DIMS = (((1,), (1,)), ((), ()))


def whole(n):
    return [pl.BlockSpec(memory_space=pltpu.VMEM) for _ in range(n)]


def lanes(shape):
    return lax.broadcasted_iota(jnp.int32, shape, 1)


def halves_swapped(a):
    half = a.shape[1] // 2
    return pltpu.roll(a.astype(jnp.float32), half, 1)


def params(mib):
    return pltpu.CompilerParams(vmem_limit_bytes=mib * 1024 * 1024)


def route_kernel(
    ids_ref, share_ref, tokens_ref, cot_ref, copies_ref, chooser_ref, slot_weight_ref,
    held_ids, held_share, held_tokens, held_cot, both, chooser, weights, in_sems, out_sems, own_sems,
):
    count = ids_ref.shape[1]
    slots = chooser_ref.shape[0]
    peers = copies_ref.shape[0]
    pairs = (
        (ids_ref, held_ids), (share_ref, held_share), (tokens_ref, held_tokens), (cot_ref, held_cot)
    )
    reads = [
        pltpu.make_async_copy(src, dst, in_sems.at[k]) for k, (src, dst) in enumerate(pairs)
    ]
    for read in reads:
        read.start()
    square = (count, count)
    until = lax.broadcasted_iota(jnp.int32, square, 0) <= lanes(square)
    until = until.astype(jnp.bfloat16)
    slot = lax.broadcasted_iota(jnp.int32, (slots, count), 0).astype(jnp.float32)
    reads[0].wait()
    reads[1].wait()
    chosen = held_ids[...] == 0
    routed = jnp.max(chosen.astype(jnp.float32), axis=0, keepdims=True)
    weight = jnp.sum(jnp.where(chosen, held_share[...], 0.0), axis=0, keepdims=True)
    before = jnp.dot(
        jnp.broadcast_to(routed, (slots, count)).astype(jnp.bfloat16),
        until,
        preferred_element_type=jnp.float32,
    )
    place = jnp.where((before - 1.0 == slot) & (routed > 0.0), 1.0, 0.0)
    slot_weight = jnp.sum(place * weight, axis=1, keepdims=True)
    chooser[...] = place.astype(jnp.bfloat16)
    weights[...] = jnp.broadcast_to(slot_weight, weights.shape)
    writes = [
        pltpu.make_async_copy(chooser, chooser_ref, own_sems.at[0]),
        pltpu.make_async_copy(weights, slot_weight_ref, own_sems.at[1]),
    ]
    for write in writes:
        write.start()
    for part, held in enumerate((held_tokens, held_cot)):
        reads[2 + part].wait()
        rows = jnp.dot(chooser[...], held[...], preferred_element_type=jnp.float32)
        both[part] = (rows * slot_weight if part else rows).astype(jnp.bfloat16)
        for k in range(peers):
            writes.append(
                pltpu.make_async_copy(
                    both.at[part],
                    copies_ref.at[k, pl.ds(part * slots, slots), :],
                    out_sems.at[part, k],
                )
            )
            writes[-1].start()
    for write in writes:
        write.wait()


def route(ids, share, tokens, cot, peers):
    count, width = tokens.shape
    slots = count // 8
    top = ids.shape[1]
    return pl.pallas_call(
        route_kernel,
        out_shape=(
            jax.ShapeDtypeStruct((peers, 2 * slots, width), jnp.bfloat16),
            jax.ShapeDtypeStruct((slots, count), jnp.bfloat16),
            jax.ShapeDtypeStruct((slots, 128), jnp.float32),
        ),
        in_specs=[HBM] * 4,
        out_specs=(HBM,) * 3,
        scratch_shapes=[
            pltpu.VMEM((top, count), jnp.int32),
            pltpu.VMEM((top, count), jnp.float32),
            pltpu.VMEM((count, width), jnp.bfloat16),
            pltpu.VMEM((count, width), jnp.bfloat16),
            pltpu.VMEM((2, slots, width), jnp.bfloat16),
            pltpu.VMEM((slots, count), jnp.bfloat16),
            pltpu.VMEM((slots, 128), jnp.float32),
            pltpu.SemaphoreType.DMA((4,)),
            pltpu.SemaphoreType.DMA((2, peers)),
            pltpu.SemaphoreType.DMA((2,)),
        ],
        compiler_params=params(56),
        name="route",
    )(ids.T, share.T, tokens, cot)


def pack_kernel(own_ref, got_ref, packed_ref):
    rows, width = own_ref.shape[1:]
    low = lanes((rows, width)) < width // 2
    top = lax.axis_index("y") == 0

    def half_of(left, right):
        left, right = left.astype(jnp.float32), right.astype(jnp.float32)
        if_top = jnp.where(low, left, halves_swapped(right))
        return jnp.where(top, if_top, jnp.where(low, halves_swapped(left), right)).astype(jnp.bfloat16)

    mine = half_of(own_ref[0], own_ref[1])
    got = half_of(got_ref[0], got_ref[1])
    down, their_down = own_ref[2], got_ref[2]
    packed_ref[:rows, :] = jnp.where(top, mine, got)
    packed_ref[rows : 2 * rows, :] = jnp.where(top, got, mine)
    packed_ref[2 * rows :, :] = half_of(
        jnp.where(top, down, their_down), jnp.where(top, their_down, down)
    )


def pack_shards(own, got):
    _, rows, width = own.shape
    return pl.pallas_call(
        pack_kernel,
        out_shape=jax.ShapeDtypeStruct((3 * rows, width), own.dtype),
        in_specs=whole(2),
        out_specs=whole(1)[0],
        compiler_params=params(2),
        name="pack_shards",
    )(own, got)


def expert_kernel(
    join_ref, both_ref, packed_ref, partial_0, partial_1, partial_2, partial_3, send_ref, keep_ref,
    gate_up, down, terms, partials,
):
    chips = packed_ref.shape[1]
    rows = packed_ref.shape[2] // 3
    width = packed_ref.shape[3]
    half = width // 2
    peers, slots = both_ref.shape[0], both_ref.shape[1] // 2
    depth = both_ref.shape[2]
    z, c = lax.axis_index("z"), lax.axis_index("c")
    for chip in range(chips):
        for core in range(2):
            block = packed_ref[core, chip, 2 * rows :, :].astype(jnp.float32)
            turned = pltpu.roll(block, half, 1)
            low = lanes(block.shape) < half
            doubled = (jnp.where(low, block, turned), jnp.where(low, turned, block))
            for y in range(2):
                at = ((chip * 2 + y) * 2 + core) * rows
                gate_up[at : at + rows, :] = packed_ref[core, chip, y * rows : (y + 1) * rows, :]
                down[at : at + rows, :] = doubled[y].astype(jnp.bfloat16)
    total = peers * slots
    picked = both_ref[:, :slots, :].reshape(total, depth)
    dpicked = both_ref[:, slots:, :].reshape(total, depth)
    acts = jnp.dot(picked, gate_up[...], preferred_element_type=jnp.float32)
    turned = pltpu.roll(acts, half, 1)
    low = lanes(acts.shape) < half
    gate, up = jnp.where(low, acts, turned), jnp.where(low, turned, acts)
    sigma = jax.nn.sigmoid(gate)
    hidden = gate * sigma * up
    hidden_half = hidden.astype(jnp.bfloat16)
    partial = lax.dot_general(
        jnp.where(low, hidden, 0.0).astype(jnp.bfloat16),
        down[...],
        LANE_DIMS,
        preferred_element_type=jnp.float32,
    )
    partials[...] = partial.reshape(partials.shape)
    x, ring = lax.axis_index("x"), lax.axis_index("h") * 2 + lax.axis_index("y")
    for step, ref in enumerate((partial_0, partial_1, partial_2, partial_3)):
        for turn in range(4):
            place = lax.rem(ring + turn, 4)
            peer = (lax.rem(place, 2) * 2 + place // 2) * 4 + lax.rem(x + step, 4)
            ref[turn] = partials[peer].astype(ref.dtype)
    dhidden = jnp.dot(dpicked, down[...], preferred_element_type=jnp.float32)
    dgate = dhidden * up * sigma * (1.0 + gate * (1.0 - sigma))
    dup = dhidden * gate * sigma
    first = 1.0 - join_ref[(z * 2 + 0) * 2 + c].astype(jnp.float32)
    second = 1.0 - join_ref[(z * 2 + 1) * 2 + c].astype(jnp.float32)
    group = lax.broadcasted_iota(jnp.int32, acts.shape, 0) // (total // 2)
    active = jnp.where(group == 0, first, second)
    dacts = (jnp.where(low, dgate, dup) * active).astype(jnp.bfloat16)
    counted = (hidden_half.astype(jnp.float32) * active).astype(jnp.bfloat16)
    terms[0] = lax.dot_general(picked, dacts, ROW_DIMS, preferred_element_type=jnp.float32)
    terms[1] = lax.dot_general(dpicked, counted, ROW_DIMS, preferred_element_type=jnp.float32)
    half_rows = rows // 2
    low = lanes((half_rows, width)) < half
    for chip in range(chips):
        for y in range(2):
            base = (chip * 2 + y) * 2 * rows
            for which, ref in ((c, keep_ref), (1 - c, send_ref)):
                at = pl.multiple_of(base + which * rows, rows)
                ref[chip, y, :rows, :] = terms[0, pl.ds(at, rows), :].astype(ref.dtype)
                packed = jnp.where(
                    low,
                    terms[1, pl.ds(at, half_rows), :],
                    terms[1, pl.ds(at + half_rows, half_rows), :],
                )
                ref[chip, y, rows:, :] = packed.astype(ref.dtype)


def expert(join, both, packed):
    peers, doubled, depth = both.shape
    slots = doubled // 2
    _, chips, rows, width = packed.shape
    chunk = (chips, 2, rows // 2, width)
    quarter = jax.ShapeDtypeStruct((peers // 4, slots, depth), jnp.bfloat16)
    return pl.pallas_call(
        expert_kernel,
        out_shape=(
            quarter, quarter, quarter, quarter,
            jax.ShapeDtypeStruct(chunk, jnp.bfloat16),
            jax.ShapeDtypeStruct(chunk, jnp.float32),
        ),
        in_specs=[pl.BlockSpec(memory_space=pltpu.SMEM), *whole(2)],
        out_specs=tuple(whole(6)),
        scratch_shapes=[
            pltpu.VMEM((depth, width), jnp.bfloat16),
            pltpu.VMEM((depth, width), jnp.bfloat16),
            pltpu.VMEM((2, depth, width), jnp.float32),
            pltpu.VMEM((peers, slots, depth), jnp.float32),
        ],
        compiler_params=params(24),
        name="expert",
    )(join, both, packed)


def add_kernel(own_ref, *refs):
    total = own_ref[...].astype(jnp.float32)
    for ref in refs[:3]:
        total += ref[...].astype(jnp.float32)
    for k, ref in enumerate(refs[3:]):
        ref[...] = total[k].astype(ref.dtype)


def add_quarters(parts):
    turns, slots, depth = parts[0].shape
    return pl.pallas_call(
        add_kernel,
        out_shape=(jax.ShapeDtypeStruct((slots, depth), jnp.bfloat16),) * turns,
        in_specs=whole(4),
        out_specs=tuple(whole(turns)),
        compiler_params=params(8),
        name="add_quarters",
    )(*parts)


def mix_kernel(own_ref, first_ref, second_ref, third_ref, chooser_ref, slot_weight_ref, mixed_ref):
    total = own_ref[...].astype(jnp.float32)
    for ref in (first_ref, second_ref, third_ref):
        total += ref[...].astype(jnp.float32)
    weighted = (total * slot_weight_ref[:, :1]).astype(jnp.bfloat16)
    mixed_ref[...] = lax.dot_general(
        chooser_ref[...], weighted, ROW_DIMS, preferred_element_type=jnp.float32
    ).astype(jnp.bfloat16)


def mix(parts, chooser, slot_weight):
    return pl.pallas_call(
        mix_kernel,
        out_shape=jax.ShapeDtypeStruct((chooser.shape[1], parts[0].shape[1]), jnp.bfloat16),
        in_specs=whole(6),
        out_specs=whole(1)[0],
        compiler_params=params(8),
        name="mix",
    )(*parts, chooser, slot_weight)


def finish_kernel(blocks_ref, gate_ref, up_ref, down_ref):
    rows, width = gate_ref.shape
    half = width // 2
    sums = [blocks_ref[y].astype(jnp.float32) for y in range(2)]
    for k in range(2, blocks_ref.shape[0], 2):
        for y in range(2):
            sums[y] += blocks_ref[k + y].astype(jnp.float32)
    low = lanes(sums[0].shape) < half
    firsts = jnp.where(low, sums[0], pltpu.roll(sums[1], half, 1)).astype(jnp.bfloat16)
    seconds = jnp.where(low, pltpu.roll(sums[0], half, 1), sums[1]).astype(jnp.bfloat16)
    gate_ref[...] = firsts[:rows]
    up_ref[...] = seconds[:rows]
    down_ref[: rows // 2, :] = firsts[rows:]
    down_ref[rows // 2 :, :] = seconds[rows:]


def finish(blocks):
    _, packed_rows, width = blocks.shape
    shape = jax.ShapeDtypeStruct((packed_rows // 3 * 2, width), jnp.bfloat16)
    return pl.pallas_call(
        finish_kernel,
        out_shape=(shape,) * 3,
        in_specs=whole(1),
        out_specs=tuple(whole(3)),
        compiler_params=params(4),
        name="finish",
    )(blocks)


def spread(parts, axes, ring):
    came = [
        lax.ppermute(part, axes, [(ring[i], ring[(i + k) % 4]) for i in range(4)])
        for k, part in enumerate(parts)
        if k
    ]
    return [parts[0], *came]


def per_device(tokens, cotangent, expert_ids, route_weights, join_groups, w_gate, w_up, w_down):
    plane = lax.axis_size(PLANE)
    chips = lax.axis_size("z")
    own = jnp.stack([w_gate, w_up, w_down])
    got = lax.ppermute(own, "y", SWAP)
    copies, chooser, slot_weight = route(expert_ids, route_weights, tokens, cotangent, plane)
    packed = pack_shards(own, got)
    packed, copies = lax.optimization_barrier((packed, copies))
    rows_in = lax.all_to_all(copies, PLANE, 0, 0, tiled=True)
    along = lax.all_gather(packed, "z", axis=0, tiled=False)
    gathered = lax.all_gather(along, "c", axis=0, tiled=False)
    *partials, send, keep = expert(join_groups, rows_in, gathered)
    from_core = lax.ppermute(send, "c", SWAP)
    own, right, across, left = spread(partials, "x", (0, 1, 2, 3))
    chip_sum = (keep + from_core.astype(jnp.float32)).astype(jnp.bfloat16)
    chip_sum = chip_sum.reshape(chips * 2, *chip_sum.shape[2:])
    chip_sum, right, left = lax.optimization_barrier((chip_sum, right, left))
    pieces = lax.all_to_all(chip_sum, ("z", "y"), 0, 0, tiled=True)
    quarters = add_quarters((own, right, across, left))
    mixed = mix(spread(quarters, RING, (0, 2, 1, 3)), chooser, slot_weight)
    return (mixed, *finish(pieces))


def solution(mesh):
    experts = mesh.shape["expert"]
    split = Mesh(mesh.devices.reshape(-1, 2, 2, 2, experts // 2), AXES)
    dp = ("z", "y", "c")
    tok, weight = P(AXES, None), P(dp, ("h", "x"))
    return jax.shard_map(
        per_device,
        mesh=split,
        in_specs=(tok, tok, tok, tok, P(), weight, weight, weight),
        out_specs=(tok, weight, weight, weight),
        check_vma=False,
    )
```

```python
import jax
import jax.numpy as jnp
from jax import lax
from jax.experimental import pallas as pl
from jax.experimental.pallas import tpu as pltpu
from jax.sharding import Mesh
from jax.sharding import PartitionSpec as P

AXES = ("z", "y", "c", "h", "x")
PLANE = ("y", "h", "x")
HBM = pl.BlockSpec(memory_space=pltpu.HBM)
SWAP = ((0, 1), (1, 0))
ROW_DIMS = (((0,), (0,)), ((), ()))
LANE_DIMS = (((1,), (1,)), ((), ()))


def whole(n):
    return [pl.BlockSpec(memory_space=pltpu.VMEM) for _ in range(n)]


def lanes(shape):
    return lax.broadcasted_iota(jnp.int32, shape, 1)


def halves_swapped(a):
    half = a.shape[1] // 2
    return pltpu.roll(a.astype(jnp.float32), half, 1)


def params(mib):
    return pltpu.CompilerParams(vmem_limit_bytes=mib * 1024 * 1024)


def route_kernel(
    ids_ref, share_ref, tokens_ref, cot_ref, copies_ref, chooser_ref, slot_weight_ref,
    held_ids, held_share, held_tokens, held_cot, both, chooser, weights, in_sems, out_sems, own_sems,
):
    count = ids_ref.shape[1]
    slots = chooser_ref.shape[0]
    peers = copies_ref.shape[0]
    pairs = (
        (ids_ref, held_ids), (share_ref, held_share), (tokens_ref, held_tokens), (cot_ref, held_cot)
    )
    reads = [
        pltpu.make_async_copy(src, dst, in_sems.at[k]) for k, (src, dst) in enumerate(pairs)
    ]
    for read in reads:
        read.start()
    square = (count, count)
    until = lax.broadcasted_iota(jnp.int32, square, 0) <= lanes(square)
    until = until.astype(jnp.bfloat16)
    slot = lax.broadcasted_iota(jnp.int32, (slots, count), 0).astype(jnp.float32)
    reads[0].wait()
    reads[1].wait()
    chosen = held_ids[...] == 0
    routed = jnp.max(chosen.astype(jnp.float32), axis=0, keepdims=True)
    weight = jnp.sum(jnp.where(chosen, held_share[...], 0.0), axis=0, keepdims=True)
    before = jnp.dot(
        jnp.broadcast_to(routed, (slots, count)).astype(jnp.bfloat16),
        until,
        preferred_element_type=jnp.float32,
    )
    place = jnp.where((before - 1.0 == slot) & (routed > 0.0), 1.0, 0.0)
    slot_weight = jnp.sum(place * weight, axis=1, keepdims=True)
    chooser[...] = place.astype(jnp.bfloat16)
    weights[...] = jnp.broadcast_to(slot_weight, weights.shape)
    writes = [
        pltpu.make_async_copy(chooser, chooser_ref, own_sems.at[0]),
        pltpu.make_async_copy(weights, slot_weight_ref, own_sems.at[1]),
    ]
    for write in writes:
        write.start()
    for part, held in enumerate((held_tokens, held_cot)):
        reads[2 + part].wait()
        rows = jnp.dot(chooser[...], held[...], preferred_element_type=jnp.float32)
        both[part] = (rows * slot_weight if part else rows).astype(jnp.bfloat16)
        for k in range(peers):
            writes.append(
                pltpu.make_async_copy(
                    both.at[part],
                    copies_ref.at[k, pl.ds(part * slots, slots), :],
                    out_sems.at[part, k],
                )
            )
            writes[-1].start()
    for write in writes:
        write.wait()


def route(ids, share, tokens, cot, peers):
    count, width = tokens.shape
    slots = count // 8
    top = ids.shape[1]
    return pl.pallas_call(
        route_kernel,
        out_shape=(
            jax.ShapeDtypeStruct((peers, 2 * slots, width), jnp.bfloat16),
            jax.ShapeDtypeStruct((slots, count), jnp.bfloat16),
            jax.ShapeDtypeStruct((slots, 128), jnp.float32),
        ),
        in_specs=[HBM] * 4,
        out_specs=(HBM,) * 3,
        scratch_shapes=[
            pltpu.VMEM((top, count), jnp.int32),
            pltpu.VMEM((top, count), jnp.float32),
            pltpu.VMEM((count, width), jnp.bfloat16),
            pltpu.VMEM((count, width), jnp.bfloat16),
            pltpu.VMEM((2, slots, width), jnp.bfloat16),
            pltpu.VMEM((slots, count), jnp.bfloat16),
            pltpu.VMEM((slots, 128), jnp.float32),
            pltpu.SemaphoreType.DMA((4,)),
            pltpu.SemaphoreType.DMA((2, peers)),
            pltpu.SemaphoreType.DMA((2,)),
        ],
        compiler_params=params(56),
        name="route",
    )(ids.T, share.T, tokens, cot)


def pack_kernel(own_ref, got_ref, packed_ref):
    rows, width = own_ref.shape[1:]
    low = lanes((rows, width)) < width // 2
    top = lax.axis_index("y") == 0

    def half_of(left, right):
        left, right = left.astype(jnp.float32), right.astype(jnp.float32)
        if_top = jnp.where(low, left, halves_swapped(right))
        return jnp.where(top, if_top, jnp.where(low, halves_swapped(left), right)).astype(jnp.bfloat16)

    mine = half_of(own_ref[0], own_ref[1])
    got = half_of(got_ref[0], got_ref[1])
    packed_ref[:rows, :] = jnp.where(top, mine, got)
    packed_ref[rows : 2 * rows, :] = jnp.where(top, got, mine)
    packed_ref[2 * rows : 3 * rows, :] = jnp.where(top, own_ref[2], got_ref[2])
    packed_ref[3 * rows :, :] = jnp.where(top, got_ref[2], own_ref[2])


def pack_shards(own, got):
    _, rows, width = own.shape
    return pl.pallas_call(
        pack_kernel,
        out_shape=jax.ShapeDtypeStruct((4 * rows, width), own.dtype),
        in_specs=whole(2),
        out_specs=whole(1)[0],
        compiler_params=params(2),
        name="pack_shards",
    )(own, got)


def expert_kernel(
    join_ref, both_ref, own_ref, got_ref, hidden_send_ref, hidden_keep_ref, down, send_ref, keep_ref,
    gate_up, terms, hiddens,
):
    chips, rows, width = own_ref.shape
    rows = rows // 4
    half = width // 2
    peers, slots = both_ref.shape[0], both_ref.shape[1] // 2
    depth = both_ref.shape[2]
    z, y, c = lax.axis_index("z"), lax.axis_index("y"), lax.axis_index("c")
    for core, ref in ((c, own_ref), (1 - c, got_ref)):
        for chip in range(chips):
            for k in range(2):
                at = pl.multiple_of((chip * 2 + k) * 2 * rows + core * rows, rows)
                gate_up[pl.ds(at, rows), :] = ref[chip, k * rows : (k + 1) * rows, :]
                down[pl.ds(at, rows), :] = ref[chip, (2 + k) * rows : (3 + k) * rows, :]
    total = peers * slots
    picked = both_ref[:, :slots, :].reshape(total, depth)
    dpicked = both_ref[:, slots:, :].reshape(total, depth)
    acts = jnp.dot(picked, gate_up[...], preferred_element_type=jnp.float32)
    turned = pltpu.roll(acts, half, 1)
    low = lanes(acts.shape) < half
    gate, up = jnp.where(low, acts, turned), jnp.where(low, turned, acts)
    sigma = jax.nn.sigmoid(gate)
    hidden = gate * sigma * up
    mine = (lanes(acts.shape) >= half) == (y == 1)
    hiddens[...] = jnp.where(mine, hidden, 0.0)
    group_rows = total // 2
    hidden_send_ref[...] = hiddens[pl.ds((1 - y) * group_rows, group_rows), :].astype(jnp.bfloat16)
    hidden_keep_ref[...] = hiddens[pl.ds(y * group_rows, group_rows), :].astype(jnp.bfloat16)
    dhidden = jnp.dot(dpicked, down[...], preferred_element_type=jnp.float32)
    dhidden = jnp.where(mine, dhidden, pltpu.roll(dhidden, half, 1))
    dgate = dhidden * up * sigma * (1.0 + gate * (1.0 - sigma))
    dup = dhidden * gate * sigma
    first = 1.0 - join_ref[(z * 2 + 0) * 2 + c].astype(jnp.float32)
    second = 1.0 - join_ref[(z * 2 + 1) * 2 + c].astype(jnp.float32)
    group = lax.broadcasted_iota(jnp.int32, acts.shape, 0) // group_rows
    active = jnp.where(group == 0, first, second)
    dacts = (jnp.where(low, dgate, dup) * active).astype(jnp.bfloat16)
    counted = (hidden.astype(jnp.bfloat16).astype(jnp.float32) * active).astype(jnp.bfloat16)
    terms[0] = lax.dot_general(picked, dacts, ROW_DIMS, preferred_element_type=jnp.float32)
    terms[1] = lax.dot_general(dpicked, counted, ROW_DIMS, preferred_element_type=jnp.float32)
    half_rows = rows // 2
    low = lanes((half_rows, width)) < half
    for chip in range(chips):
        for k in range(2):
            base = (chip * 2 + k) * 2 * rows
            for which, ref in ((c, keep_ref), (1 - c, send_ref)):
                at = pl.multiple_of(base + which * rows, rows)
                ref[chip, k, :rows, :] = terms[0, pl.ds(at, rows), :].astype(ref.dtype)
                packed = jnp.where(
                    low,
                    terms[1, pl.ds(at, half_rows), :],
                    terms[1, pl.ds(at + half_rows, half_rows), :],
                )
                ref[chip, k, rows:, :] = packed.astype(ref.dtype)


def expert(join, both, own, got):
    peers, doubled, depth = both.shape
    slots = doubled // 2
    chips, rows, width = own.shape
    chunk = (chips, 2, rows // 8 * 3, width)
    hidden = jax.ShapeDtypeStruct((peers * slots // 2, width), jnp.bfloat16)
    return pl.pallas_call(
        expert_kernel,
        out_shape=(
            hidden,
            hidden,
            jax.ShapeDtypeStruct((depth, width), jnp.bfloat16),
            jax.ShapeDtypeStruct(chunk, jnp.bfloat16),
            jax.ShapeDtypeStruct(chunk, jnp.float32),
        ),
        in_specs=[pl.BlockSpec(memory_space=pltpu.SMEM), *whole(3)],
        out_specs=tuple(whole(5)),
        scratch_shapes=[
            pltpu.VMEM((depth, width), jnp.bfloat16),
            pltpu.VMEM((2, depth, width), jnp.float32),
            pltpu.VMEM((peers * slots, width), jnp.float32),
        ],
        compiler_params=params(24),
        name="expert",
    )(join, both, own, got)


def partial_kernel(keep_ref, got_ref, down_ref, partial_0, partial_1, partial_2, partial_3, partials):
    partial = lax.dot_general(
        keep_ref[...] + got_ref[...], down_ref[...], LANE_DIMS, preferred_element_type=jnp.float32
    )
    partials[...] = partial.reshape(partials.shape)
    h, x = lax.axis_index("h"), lax.axis_index("x")
    for step, ref in enumerate((partial_0, partial_1, partial_2, partial_3)):
        for turn in range(2):
            peer = lax.rem(h + turn, 2) * 4 + lax.rem(x + step, 4)
            ref[turn] = partials[peer].astype(ref.dtype)


def partial_rows(keep, got, down, peers):
    slots, depth = keep.shape[0] // peers, down.shape[0]
    return pl.pallas_call(
        partial_kernel,
        out_shape=(jax.ShapeDtypeStruct((2, slots, depth), jnp.bfloat16),) * 4,
        in_specs=whole(3),
        out_specs=tuple(whole(4)),
        scratch_shapes=[pltpu.VMEM((peers, slots, depth), jnp.float32)],
        compiler_params=params(8),
        name="partial_rows",
    )(keep, got, down)


def add_kernel(own_ref, *refs):
    total = own_ref[...].astype(jnp.float32)
    for ref in refs[:3]:
        total += ref[...].astype(jnp.float32)
    for k, ref in enumerate(refs[3:]):
        ref[...] = total[k].astype(ref.dtype)


def add_turns(parts):
    turns, slots, depth = parts[0].shape
    return pl.pallas_call(
        add_kernel,
        out_shape=(jax.ShapeDtypeStruct((slots, depth), jnp.bfloat16),) * turns,
        in_specs=whole(4),
        out_specs=tuple(whole(turns)),
        compiler_params=params(8),
        name="add_turns",
    )(*parts)


def mix_kernel(own_ref, got_ref, chooser_ref, slot_weight_ref, mixed_ref):
    total = own_ref[...].astype(jnp.float32) + got_ref[...].astype(jnp.float32)
    weighted = (total * slot_weight_ref[:, :1]).astype(jnp.bfloat16)
    mixed_ref[...] = lax.dot_general(
        chooser_ref[...], weighted, ROW_DIMS, preferred_element_type=jnp.float32
    ).astype(jnp.bfloat16)


def mix(own, got, chooser, slot_weight):
    return pl.pallas_call(
        mix_kernel,
        out_shape=jax.ShapeDtypeStruct((chooser.shape[1], own.shape[1]), jnp.bfloat16),
        in_specs=whole(4),
        out_specs=whole(1)[0],
        compiler_params=params(8),
        name="mix",
    )(own, got, chooser, slot_weight)


def finish_kernel(blocks_ref, gate_ref, up_ref, down_ref):
    rows, width = gate_ref.shape
    half = width // 2
    sums = [blocks_ref[y].astype(jnp.float32) for y in range(2)]
    for k in range(2, blocks_ref.shape[0], 2):
        for y in range(2):
            sums[y] += blocks_ref[k + y].astype(jnp.float32)
    low = lanes(sums[0].shape) < half
    firsts = jnp.where(low, sums[0], pltpu.roll(sums[1], half, 1)).astype(jnp.bfloat16)
    seconds = jnp.where(low, pltpu.roll(sums[0], half, 1), sums[1]).astype(jnp.bfloat16)
    gate_ref[...] = firsts[:rows]
    up_ref[...] = seconds[:rows]
    down_ref[: rows // 2, :] = firsts[rows:]
    down_ref[rows // 2 :, :] = seconds[rows:]


def finish(blocks):
    _, packed_rows, width = blocks.shape
    shape = jax.ShapeDtypeStruct((packed_rows // 3 * 2, width), jnp.bfloat16)
    return pl.pallas_call(
        finish_kernel,
        out_shape=(shape,) * 3,
        in_specs=whole(1),
        out_specs=tuple(whole(3)),
        compiler_params=params(4),
        name="finish",
    )(blocks)


def spread(parts, axis):
    came = [
        lax.ppermute(part, axis, [(i, (i + k) % 4) for i in range(4)])
        for k, part in enumerate(parts)
        if k
    ]
    return [parts[0], *came]


def per_device(tokens, cotangent, expert_ids, route_weights, join_groups, w_gate, w_up, w_down):
    chips = lax.axis_size("z")
    own = jnp.stack([w_gate, w_up, w_down])
    got = lax.ppermute(own, "y", SWAP)
    copies, chooser, slot_weight = route(
        expert_ids, route_weights, tokens, cotangent, lax.axis_size(PLANE)
    )
    packed = pack_shards(own, got)
    packed, copies = lax.optimization_barrier((packed, copies))
    rows_in = lax.all_to_all(copies, PLANE, 0, 0, tiled=True)
    along = lax.all_gather(packed, "z", axis=0, tiled=False)
    other = lax.ppermute(along, "c", SWAP)
    hidden_send, hidden, down, send, keep = expert(join_groups, rows_in, along, other)
    from_core = lax.ppermute(send, "c", SWAP)
    hidden_got = lax.ppermute(hidden_send, "y", SWAP)
    chip_sum = (keep + from_core.astype(jnp.float32)).astype(jnp.bfloat16)
    chip_sum = chip_sum.reshape(chips * 2, *chip_sum.shape[2:])
    chip_sum, hidden_got = lax.optimization_barrier((chip_sum, hidden_got))
    pieces = lax.all_to_all(chip_sum, ("z", "y"), 0, 0, tiled=True)
    partials = partial_rows(hidden, hidden_got, down, lax.axis_size(("h", "x")))
    mine, theirs = add_turns(spread(partials, "x"))
    mixed = mix(mine, lax.ppermute(theirs, "h", SWAP), chooser, slot_weight)
    return (mixed, *finish(pieces))


def solution(mesh):
    experts = mesh.shape["expert"]
    split = Mesh(mesh.devices.reshape(-1, 2, 2, 2, experts // 2), AXES)
    dp = ("z", "y", "c")
    tok, weight = P(AXES, None), P(dp, ("h", "x"))
    return jax.shard_map(
        per_device,
        mesh=split,
        in_specs=(tok, tok, tok, tok, P(), weight, weight, weight),
        out_specs=(tok, weight, weight, weight),
        check_vma=False,
    )
```

```python
import jax
import jax.numpy as jnp
from jax import lax
from jax.experimental import pallas as pl
from jax.experimental.pallas import tpu as pltpu
from jax.sharding import Mesh
from jax.sharding import PartitionSpec as P

AXES = ("zh", "zl", "y", "c", "h", "x")
Z = ("zh", "zl")
PLANE = ("y", "h", "x")
HBM = pl.BlockSpec(memory_space=pltpu.HBM)
ROW_DIMS = (((0,), (0,)), ((), ()))
LANE_DIMS = (((1,), (1,)), ((), ()))


def whole(n):
    return [pl.BlockSpec(memory_space=pltpu.VMEM) for _ in range(n)]


def lanes(shape):
    return lax.broadcasted_iota(jnp.int32, shape, 1)


def halves_swapped(a):
    half = a.shape[1] // 2
    return pltpu.roll(a.astype(jnp.float32), half, 1)


def params(mib):
    return pltpu.CompilerParams(vmem_limit_bytes=mib * 1024 * 1024)


def route_kernel(
    ids_ref, share_ref, tokens_ref, cot_ref, copies_ref, chooser_ref, slot_weight_ref,
    held_ids, held_share, held_tokens, held_cot, both, chooser, weights, in_sems, out_sems, own_sems,
):
    count = ids_ref.shape[1]
    slots = chooser_ref.shape[0]
    peers = copies_ref.shape[0]
    pairs = (
        (ids_ref, held_ids), (share_ref, held_share), (tokens_ref, held_tokens), (cot_ref, held_cot)
    )
    reads = [
        pltpu.make_async_copy(src, dst, in_sems.at[k]) for k, (src, dst) in enumerate(pairs)
    ]
    for read in reads:
        read.start()
    square = (count, count)
    until = lax.broadcasted_iota(jnp.int32, square, 0) <= lanes(square)
    until = until.astype(jnp.bfloat16)
    slot = lax.broadcasted_iota(jnp.int32, (slots, count), 0).astype(jnp.float32)
    reads[0].wait()
    reads[1].wait()
    chosen = held_ids[...] == 0
    routed = jnp.max(chosen.astype(jnp.float32), axis=0, keepdims=True)
    weight = jnp.sum(jnp.where(chosen, held_share[...], 0.0), axis=0, keepdims=True)
    before = jnp.dot(
        jnp.broadcast_to(routed, (slots, count)).astype(jnp.bfloat16),
        until,
        preferred_element_type=jnp.float32,
    )
    place = jnp.where((before - 1.0 == slot) & (routed > 0.0), 1.0, 0.0)
    slot_weight = jnp.sum(place * weight, axis=1, keepdims=True)
    chooser[...] = place.astype(jnp.bfloat16)
    weights[...] = jnp.broadcast_to(slot_weight, weights.shape)
    writes = [
        pltpu.make_async_copy(chooser, chooser_ref, own_sems.at[0]),
        pltpu.make_async_copy(weights, slot_weight_ref, own_sems.at[1]),
    ]
    for write in writes:
        write.start()
    for part, held in enumerate((held_tokens, held_cot)):
        reads[2 + part].wait()
        rows = jnp.dot(chooser[...], held[...], preferred_element_type=jnp.float32)
        both[part] = (rows * slot_weight if part else rows).astype(jnp.bfloat16)
        for k in range(peers):
            writes.append(
                pltpu.make_async_copy(
                    both.at[part],
                    copies_ref.at[k, pl.ds(part * slots, slots), :],
                    out_sems.at[part, k],
                )
            )
            writes[-1].start()
    for write in writes:
        write.wait()


def route(ids, share, tokens, cot, peers):
    count, width = tokens.shape
    slots = count // 8
    top = ids.shape[1]
    return pl.pallas_call(
        route_kernel,
        out_shape=(
            jax.ShapeDtypeStruct((peers, 2 * slots, width), jnp.bfloat16),
            jax.ShapeDtypeStruct((slots, count), jnp.bfloat16),
            jax.ShapeDtypeStruct((slots, 128), jnp.float32),
        ),
        in_specs=[HBM] * 4,
        out_specs=(HBM,) * 3,
        scratch_shapes=[
            pltpu.VMEM((top, count), jnp.int32),
            pltpu.VMEM((top, count), jnp.float32),
            pltpu.VMEM((count, width), jnp.bfloat16),
            pltpu.VMEM((count, width), jnp.bfloat16),
            pltpu.VMEM((2, slots, width), jnp.bfloat16),
            pltpu.VMEM((slots, count), jnp.bfloat16),
            pltpu.VMEM((slots, 128), jnp.float32),
            pltpu.SemaphoreType.DMA((4,)),
            pltpu.SemaphoreType.DMA((2, peers)),
            pltpu.SemaphoreType.DMA((2,)),
        ],
        compiler_params=params(56),
        name="route",
    )(ids.T, share.T, tokens, cot)


def pack_kernel(own_ref, got_ref, packed_ref):
    rows, width = own_ref.shape[1:]
    low = lanes((rows, width)) < width // 2
    top = lax.axis_index("y") == 0

    def half_of(left, right):
        left, right = left.astype(jnp.float32), right.astype(jnp.float32)
        if_top = jnp.where(low, left, halves_swapped(right))
        return jnp.where(top, if_top, jnp.where(low, halves_swapped(left), right)).astype(jnp.bfloat16)

    mine = half_of(own_ref[0], own_ref[1])
    got = half_of(got_ref[0], got_ref[1])
    packed_ref[:rows, :] = jnp.where(top, mine, got)
    packed_ref[rows : 2 * rows, :] = jnp.where(top, got, mine)
    packed_ref[2 * rows : 3 * rows, :] = jnp.where(top, own_ref[2], got_ref[2])
    packed_ref[3 * rows :, :] = jnp.where(top, got_ref[2], own_ref[2])


def pack_shards(own, got):
    _, rows, width = own.shape
    return pl.pallas_call(
        pack_kernel,
        out_shape=jax.ShapeDtypeStruct((4 * rows, width), own.dtype),
        in_specs=whole(2),
        out_specs=whole(1)[0],
        compiler_params=params(2),
        name="pack_shards",
    )(own, got)


def expert_kernel(
    join_ref, both_ref, own_ref, got_ref, hidden_send_ref, hidden_keep_ref, down, send_ref, keep_ref,
    gate_up, terms, hiddens,
):
    chips, rows, width = own_ref.shape
    rows = rows // 4
    half = width // 2
    peers, slots = both_ref.shape[0], both_ref.shape[1] // 2
    depth = both_ref.shape[2]
    z, y, c = lax.axis_index(Z), lax.axis_index("y"), lax.axis_index("c")
    for core, ref in ((c, own_ref), (1 - c, got_ref)):
        for chip in range(chips):
            for k in range(2):
                at = pl.multiple_of((chip * 2 + k) * 2 * rows + core * rows, rows)
                gate_up[pl.ds(at, rows), :] = ref[chip, k * rows : (k + 1) * rows, :]
                down[pl.ds(at, rows), :] = ref[chip, (2 + k) * rows : (3 + k) * rows, :]
    total = peers * slots
    picked = both_ref[:, :slots, :].reshape(total, depth)
    dpicked = both_ref[:, slots:, :].reshape(total, depth)
    acts = jnp.dot(picked, gate_up[...], preferred_element_type=jnp.float32)
    turned = pltpu.roll(acts, half, 1)
    low = lanes(acts.shape) < half
    gate, up = jnp.where(low, acts, turned), jnp.where(low, turned, acts)
    sigma = jax.nn.sigmoid(gate)
    hidden = gate * sigma * up
    mine = (lanes(acts.shape) >= half) == (y == 1)
    hiddens[...] = jnp.where(mine, hidden, 0.0)
    group_rows = total // 2
    hidden_send_ref[...] = hiddens[pl.ds((1 - y) * group_rows, group_rows), :].astype(jnp.bfloat16)
    hidden_keep_ref[...] = hiddens[pl.ds(y * group_rows, group_rows), :].astype(jnp.bfloat16)
    dhidden = jnp.dot(dpicked, down[...], preferred_element_type=jnp.float32)
    dhidden = jnp.where(mine, dhidden, pltpu.roll(dhidden, half, 1))
    dgate = dhidden * up * sigma * (1.0 + gate * (1.0 - sigma))
    dup = dhidden * gate * sigma
    first = 1.0 - join_ref[(z * 2 + 0) * 2 + c].astype(jnp.float32)
    second = 1.0 - join_ref[(z * 2 + 1) * 2 + c].astype(jnp.float32)
    group = lax.broadcasted_iota(jnp.int32, acts.shape, 0) // group_rows
    active = jnp.where(group == 0, first, second)
    dacts = (jnp.where(low, dgate, dup) * active).astype(jnp.bfloat16)
    counted = (hidden.astype(jnp.bfloat16).astype(jnp.float32) * active).astype(jnp.bfloat16)
    terms[0] = lax.dot_general(picked, dacts, ROW_DIMS, preferred_element_type=jnp.float32)
    terms[1] = lax.dot_general(dpicked, counted, ROW_DIMS, preferred_element_type=jnp.float32)
    half_rows = rows // 2
    low = lanes((half_rows, width)) < half
    for chip in range(chips):
        for k in range(2):
            base = (chip * 2 + k) * 2 * rows
            away = jnp.bitwise_xor(chip % 2, lax.rem(z, 2))
            for which, ref in ((c, keep_ref), (1 - c, send_ref)):
                at = pl.multiple_of(base + which * rows, rows)
                ref[away, chip // 2, k, :rows, :] = terms[0, pl.ds(at, rows), :].astype(ref.dtype)
                packed = jnp.where(
                    low,
                    terms[1, pl.ds(at, half_rows), :],
                    terms[1, pl.ds(at + half_rows, half_rows), :],
                )
                ref[away, chip // 2, k, rows:, :] = packed.astype(ref.dtype)


def expert(join, both, own, got):
    peers, doubled, depth = both.shape
    slots = doubled // 2
    chips, rows, width = own.shape
    chunk = (2, chips // 2, 2, rows // 8 * 3, width)
    hidden = jax.ShapeDtypeStruct((peers * slots // 2, width), jnp.bfloat16)
    return pl.pallas_call(
        expert_kernel,
        out_shape=(
            hidden,
            hidden,
            jax.ShapeDtypeStruct((depth, width), jnp.bfloat16),
            jax.ShapeDtypeStruct(chunk, jnp.bfloat16),
            jax.ShapeDtypeStruct(chunk, jnp.float32),
        ),
        in_specs=[pl.BlockSpec(memory_space=pltpu.SMEM), *whole(3)],
        out_specs=tuple(whole(5)),
        scratch_shapes=[
            pltpu.VMEM((depth, width), jnp.bfloat16),
            pltpu.VMEM((2, depth, width), jnp.float32),
            pltpu.VMEM((peers * slots, width), jnp.float32),
        ],
        compiler_params=params(24),
        name="expert",
    )(join, both, own, got)


def partial_kernel(keep_ref, got_ref, down_ref, mine_ref, theirs_ref, partials):
    partial = lax.dot_general(
        keep_ref[...] + got_ref[...], down_ref[...], LANE_DIMS, preferred_element_type=jnp.float32
    )
    partials[...] = partial.reshape(partials.shape)
    h, x = lax.axis_index("h"), lax.axis_index("x")
    for low, ref in enumerate((mine_ref, theirs_ref)):
        for high in range(2):
            for row in range(2):
                peer = jnp.bitwise_xor(h, row) * 4 + jnp.bitwise_xor(x, 2 * high + low)
                ref[2 * high + row] = partials[peer].astype(ref.dtype)


def partial_rows(keep, got, down, peers):
    slots, depth = keep.shape[0] // peers, down.shape[0]
    return pl.pallas_call(
        partial_kernel,
        out_shape=(
            jax.ShapeDtypeStruct((peers // 2, slots, depth), jnp.float32),
            jax.ShapeDtypeStruct((peers // 2, slots, depth), jnp.bfloat16),
        ),
        in_specs=whole(3),
        out_specs=tuple(whole(2)),
        scratch_shapes=[pltpu.VMEM((peers, slots, depth), jnp.float32)],
        compiler_params=params(8),
        name="partial_rows",
    )(keep, got, down)


def add_kernel(keep_ref, got_ref, mine_ref, theirs_ref):
    half = mine_ref.shape[0]
    mine_ref[...] = keep_ref[:half] + got_ref[:half].astype(jnp.float32)
    theirs_ref[...] = (keep_ref[half:] + got_ref[half:].astype(jnp.float32)).astype(jnp.bfloat16)


def add_halves(keep, got):
    half = (keep.shape[0] // 2, *keep.shape[1:])
    return pl.pallas_call(
        add_kernel,
        out_shape=(
            jax.ShapeDtypeStruct(half, jnp.float32),
            jax.ShapeDtypeStruct(half, jnp.bfloat16),
        ),
        in_specs=whole(2),
        out_specs=tuple(whole(2)),
        compiler_params=params(8),
        name="add_halves",
    )(keep, got)


def mix_kernel(own_ref, got_ref, chooser_ref, slot_weight_ref, mixed_ref):
    total = own_ref[0] + got_ref[0].astype(jnp.float32)
    weighted = (total * slot_weight_ref[:, :1]).astype(jnp.bfloat16)
    mixed_ref[...] = lax.dot_general(
        chooser_ref[...], weighted, ROW_DIMS, preferred_element_type=jnp.float32
    ).astype(jnp.bfloat16)


def mix(own, got, chooser, slot_weight):
    return pl.pallas_call(
        mix_kernel,
        out_shape=jax.ShapeDtypeStruct((chooser.shape[1], own.shape[2]), jnp.bfloat16),
        in_specs=whole(4),
        out_specs=whole(1)[0],
        compiler_params=params(8),
        name="mix",
    )(own, got, chooser, slot_weight)


def finish_kernel(blocks_ref, gate_ref, up_ref, down_ref):
    rows, width = gate_ref.shape
    half = width // 2
    sums = [blocks_ref[y].astype(jnp.float32) for y in range(2)]
    for k in range(2, blocks_ref.shape[0], 2):
        for y in range(2):
            sums[y] += blocks_ref[k + y].astype(jnp.float32)
    low = lanes(sums[0].shape) < half
    firsts = jnp.where(low, sums[0], pltpu.roll(sums[1], half, 1)).astype(jnp.bfloat16)
    seconds = jnp.where(low, pltpu.roll(sums[0], half, 1), sums[1]).astype(jnp.bfloat16)
    gate_ref[...] = firsts[:rows]
    up_ref[...] = seconds[:rows]
    down_ref[: rows // 2, :] = firsts[rows:]
    down_ref[rows // 2 :, :] = seconds[rows:]


def finish(blocks):
    _, packed_rows, width = blocks.shape
    shape = jax.ShapeDtypeStruct((packed_rows // 3 * 2, width), jnp.bfloat16)
    return pl.pallas_call(
        finish_kernel,
        out_shape=(shape,) * 3,
        in_specs=whole(1),
        out_specs=tuple(whole(3)),
        compiler_params=params(4),
        name="finish",
    )(blocks)


def swapped(part, axis, distance=1):
    size = lax.axis_size(axis)
    return lax.ppermute(part, axis, [(i, i ^ distance) for i in range(size)])


def per_device(tokens, cotangent, expert_ids, route_weights, join_groups, w_gate, w_up, w_down):
    own = jnp.stack([w_gate, w_up, w_down])
    got = swapped(own, "y")
    copies, chooser, slot_weight = route(
        expert_ids, route_weights, tokens, cotangent, lax.axis_size(PLANE)
    )
    packed = pack_shards(own, got)
    packed, copies = lax.optimization_barrier((packed, copies))
    rows_in = lax.all_to_all(copies, PLANE, 0, 0, tiled=True)
    along = lax.all_gather(packed, Z, axis=0, tiled=False)
    along, rows_in = lax.optimization_barrier((along, rows_in))
    other = swapped(along, "c")
    hidden_send, hidden, down, send, keep = expert(join_groups, rows_in, along, other)
    from_core = swapped(send, "c")
    hidden_got = swapped(hidden_send, "y")
    keep, to_pair = add_halves(keep, from_core)
    from_pair = swapped(to_pair, "zl")
    partial, partial_send = partial_rows(hidden, hidden_got, down, lax.axis_size(("h", "x")))
    pair_sum = (keep + from_pair.astype(jnp.float32)).astype(jnp.bfloat16)
    pair_sum = pair_sum.reshape(-1, *pair_sum.shape[3:])
    pair_sum, partial_send = lax.optimization_barrier((pair_sum, partial_send))
    pieces = lax.all_to_all(pair_sum, ("zh", "y"), 0, 0, tiled=True)
    partial, partial_send = add_halves(partial, swapped(partial_send, "x"))
    partial, partial_send = add_halves(partial, swapped(partial_send, "x", 2))
    mixed = mix(partial, swapped(partial_send, "h"), chooser, slot_weight)
    return (mixed, *finish(pieces))


def solution(mesh):
    experts = mesh.shape["expert"]
    split = Mesh(mesh.devices.reshape(-1, 2, 2, 2, 2, experts // 2), AXES)
    dp = ("zh", "zl", "y", "c")
    tok, weight = P(AXES, None), P(dp, ("h", "x"))
    return jax.shard_map(
        per_device,
        mesh=split,
        in_specs=(tok, tok, tok, tok, P(), weight, weight, weight),
        out_specs=(tok, weight, weight, weight),
        check_vma=False,
    )
```

```python
import jax
import jax.numpy as jnp
from jax import lax
from jax.experimental import pallas as pl
from jax.experimental.pallas import tpu as pltpu
from jax.sharding import Mesh
from jax.sharding import PartitionSpec as P

AXES = ("zh", "zl", "y", "c", "h", "x")
Z = ("zh", "zl")
PLANE = ("y", "h", "x")
HBM = pl.BlockSpec(memory_space=pltpu.HBM)
ROW_DIMS = (((0,), (0,)), ((), ()))
LANE_DIMS = (((1,), (1,)), ((), ()))


def whole(n):
    return [pl.BlockSpec(memory_space=pltpu.VMEM) for _ in range(n)]


def lanes(shape):
    return lax.broadcasted_iota(jnp.int32, shape, 1)


def halves_swapped(a):
    half = a.shape[1] // 2
    return pltpu.roll(a.astype(jnp.float32), half, 1)


def params(mib):
    return pltpu.CompilerParams(vmem_limit_bytes=mib * 1024 * 1024)


def route_kernel(
    ids_ref, share_ref, tokens_ref, cot_ref, copies_ref, chooser_ref, slot_weight_ref,
    held_ids, held_share, held_tokens, held_cot, both, chooser, weights, in_sems, out_sems, own_sems,
):
    count = ids_ref.shape[1]
    slots = chooser_ref.shape[0]
    peers = copies_ref.shape[0]
    pairs = (
        (ids_ref, held_ids), (share_ref, held_share), (tokens_ref, held_tokens), (cot_ref, held_cot)
    )
    reads = [
        pltpu.make_async_copy(src, dst, in_sems.at[k]) for k, (src, dst) in enumerate(pairs)
    ]
    for read in reads:
        read.start()
    square = (count, count)
    until = lax.broadcasted_iota(jnp.int32, square, 0) <= lanes(square)
    until = until.astype(jnp.bfloat16)
    slot = lax.broadcasted_iota(jnp.int32, (slots, count), 0).astype(jnp.float32)
    reads[0].wait()
    reads[1].wait()
    chosen = held_ids[...] == 0
    routed = jnp.max(chosen.astype(jnp.float32), axis=0, keepdims=True)
    weight = jnp.sum(jnp.where(chosen, held_share[...], 0.0), axis=0, keepdims=True)
    before = jnp.dot(
        jnp.broadcast_to(routed, (slots, count)).astype(jnp.bfloat16),
        until,
        preferred_element_type=jnp.float32,
    )
    place = jnp.where((before - 1.0 == slot) & (routed > 0.0), 1.0, 0.0)
    slot_weight = jnp.sum(place * weight, axis=1, keepdims=True)
    chooser[...] = place.astype(jnp.bfloat16)
    weights[...] = jnp.broadcast_to(slot_weight, weights.shape)
    writes = [
        pltpu.make_async_copy(chooser, chooser_ref, own_sems.at[0]),
        pltpu.make_async_copy(weights, slot_weight_ref, own_sems.at[1]),
    ]
    for write in writes:
        write.start()
    for part, held in enumerate((held_tokens, held_cot)):
        reads[2 + part].wait()
        rows = jnp.dot(chooser[...], held[...], preferred_element_type=jnp.float32)
        both[part] = (rows * slot_weight if part else rows).astype(jnp.bfloat16)
        for k in range(peers):
            writes.append(
                pltpu.make_async_copy(
                    both.at[part],
                    copies_ref.at[k, pl.ds(part * slots, slots), :],
                    out_sems.at[part, k],
                )
            )
            writes[-1].start()
    for write in writes:
        write.wait()


def route(ids, share, tokens, cot, peers):
    count, width = tokens.shape
    slots = count // 8
    top = ids.shape[1]
    return pl.pallas_call(
        route_kernel,
        out_shape=(
            jax.ShapeDtypeStruct((peers, 2 * slots, width), jnp.bfloat16),
            jax.ShapeDtypeStruct((slots, count), jnp.bfloat16),
            jax.ShapeDtypeStruct((slots, 128), jnp.float32),
        ),
        in_specs=[HBM] * 4,
        out_specs=(HBM,) * 3,
        scratch_shapes=[
            pltpu.VMEM((top, count), jnp.int32),
            pltpu.VMEM((top, count), jnp.float32),
            pltpu.VMEM((count, width), jnp.bfloat16),
            pltpu.VMEM((count, width), jnp.bfloat16),
            pltpu.VMEM((2, slots, width), jnp.bfloat16),
            pltpu.VMEM((slots, count), jnp.bfloat16),
            pltpu.VMEM((slots, 128), jnp.float32),
            pltpu.SemaphoreType.DMA((4,)),
            pltpu.SemaphoreType.DMA((2, peers)),
            pltpu.SemaphoreType.DMA((2,)),
        ],
        compiler_params=params(56),
        name="route",
    )(ids.T, share.T, tokens, cot)


def pack_kernel(own_ref, got_ref, packed_ref):
    rows, width = own_ref.shape[1:]
    low = lanes((rows, width)) < width // 2
    top = lax.axis_index("y") == 0

    def half_of(left, right):
        left, right = left.astype(jnp.float32), right.astype(jnp.float32)
        if_top = jnp.where(low, left, halves_swapped(right))
        return jnp.where(top, if_top, jnp.where(low, halves_swapped(left), right)).astype(jnp.bfloat16)

    mine = half_of(own_ref[0], own_ref[1])
    got = half_of(got_ref[0], got_ref[1])
    packed_ref[:rows, :] = jnp.where(top, mine, got)
    packed_ref[rows : 2 * rows, :] = jnp.where(top, got, mine)
    packed_ref[2 * rows : 3 * rows, :] = jnp.where(top, own_ref[2], got_ref[2])
    packed_ref[3 * rows :, :] = jnp.where(top, got_ref[2], own_ref[2])


def pack_shards(own, got):
    _, rows, width = own.shape
    return pl.pallas_call(
        pack_kernel,
        out_shape=jax.ShapeDtypeStruct((4 * rows, width), own.dtype),
        in_specs=whole(2),
        out_specs=whole(1)[0],
        compiler_params=params(2),
        name="pack_shards",
    )(own, got)


def expert_kernel(
    join_ref, both_ref, own_ref, got_ref, hidden_send_ref, hidden_keep_ref, down, send_ref, keep_ref,
    gate_up, terms, hiddens,
):
    chips, rows, width = own_ref.shape
    rows = rows // 4
    half = width // 2
    peers, slots = both_ref.shape[0], both_ref.shape[1] // 2
    depth = both_ref.shape[2]
    z, y, c = lax.axis_index(Z), lax.axis_index("y"), lax.axis_index("c")
    for core, ref in ((c, own_ref), (1 - c, got_ref)):
        for chip in range(chips):
            for k in range(2):
                at = pl.multiple_of((chip * 2 + k) * 2 * rows + core * rows, rows)
                gate_up[pl.ds(at, rows), :] = ref[chip, k * rows : (k + 1) * rows, :]
                down[pl.ds(at, rows), :] = ref[chip, (2 + k) * rows : (3 + k) * rows, :]
    total = peers * slots
    picked = both_ref[:, :slots, :].reshape(total, depth)
    dpicked = both_ref[:, slots:, :].reshape(total, depth)
    acts = jnp.dot(picked, gate_up[...], preferred_element_type=jnp.float32)
    turned = pltpu.roll(acts, half, 1)
    low = lanes(acts.shape) < half
    gate, up = jnp.where(low, acts, turned), jnp.where(low, turned, acts)
    sigma = jax.nn.sigmoid(gate)
    hidden = gate * sigma * up
    mine = (lanes(acts.shape) >= half) == (y == 1)
    hiddens[...] = jnp.where(mine, hidden, 0.0)
    group_rows = total // 2
    hidden_send_ref[...] = hiddens[pl.ds((1 - y) * group_rows, group_rows), :].astype(jnp.bfloat16)
    hidden_keep_ref[...] = hiddens[pl.ds(y * group_rows, group_rows), :].astype(jnp.bfloat16)
    dhidden = jnp.dot(dpicked, down[...], preferred_element_type=jnp.float32)
    dhidden = jnp.where(mine, dhidden, pltpu.roll(dhidden, half, 1))
    dgate = dhidden * up * sigma * (1.0 + gate * (1.0 - sigma))
    dup = dhidden * gate * sigma
    first = 1.0 - join_ref[(z * 2 + 0) * 2 + c].astype(jnp.float32)
    second = 1.0 - join_ref[(z * 2 + 1) * 2 + c].astype(jnp.float32)
    group = lax.broadcasted_iota(jnp.int32, acts.shape, 0) // group_rows
    active = jnp.where(group == 0, first, second)
    dacts = (jnp.where(low, dgate, dup) * active).astype(jnp.bfloat16)
    counted = (hidden.astype(jnp.bfloat16).astype(jnp.float32) * active).astype(jnp.bfloat16)
    terms[0] = lax.dot_general(picked, dacts, ROW_DIMS, preferred_element_type=jnp.float32)
    terms[1] = lax.dot_general(dpicked, counted, ROW_DIMS, preferred_element_type=jnp.float32)
    half_rows = rows // 2
    low = lanes((half_rows, width)) < half
    for chip in range(chips):
        for k in range(2):
            base = (chip * 2 + k) * 2 * rows
            away = jnp.bitwise_xor(chip % 2, lax.rem(z, 2))
            for which, ref in ((c, keep_ref), (1 - c, send_ref)):
                at = pl.multiple_of(base + which * rows, rows)
                ref[away, chip // 2, k, :rows, :] = terms[0, pl.ds(at, rows), :].astype(ref.dtype)
                packed = jnp.where(
                    low,
                    terms[1, pl.ds(at, half_rows), :],
                    terms[1, pl.ds(at + half_rows, half_rows), :],
                )
                ref[away, chip // 2, k, rows:, :] = packed.astype(ref.dtype)


def expert(join, both, own, got):
    peers, doubled, depth = both.shape
    slots = doubled // 2
    chips, rows, width = own.shape
    chunk = (2, chips // 2, 2, rows // 8 * 3, width)
    hidden = jax.ShapeDtypeStruct((peers * slots // 2, width), jnp.bfloat16)
    return pl.pallas_call(
        expert_kernel,
        out_shape=(
            hidden,
            hidden,
            jax.ShapeDtypeStruct((depth, width), jnp.bfloat16),
            jax.ShapeDtypeStruct(chunk, jnp.bfloat16),
            jax.ShapeDtypeStruct(chunk, jnp.float32),
        ),
        in_specs=[pl.BlockSpec(memory_space=pltpu.SMEM), *whole(3)],
        out_specs=tuple(whole(5)),
        scratch_shapes=[
            pltpu.VMEM((depth, width), jnp.bfloat16),
            pltpu.VMEM((2, depth, width), jnp.float32),
            pltpu.VMEM((peers * slots, width), jnp.float32),
        ],
        compiler_params=params(24),
        name="expert",
    )(join, both, own, got)


def partial_kernel(keep_ref, got_ref, down_ref, mine_ref, theirs_ref, partials):
    partial = lax.dot_general(
        keep_ref[...] + got_ref[...], down_ref[...], LANE_DIMS, preferred_element_type=jnp.float32
    )
    partials[...] = partial.reshape(partials.shape)
    h, x = lax.axis_index("h"), lax.axis_index("x")
    for low, ref in enumerate((mine_ref, theirs_ref)):
        for high in range(2):
            for row in range(2):
                peer = jnp.bitwise_xor(h, row) * 4 + jnp.bitwise_xor(x, 2 * high + low)
                ref[2 * high + row] = partials[peer].astype(ref.dtype)


def partial_rows(keep, got, down, peers):
    slots, depth = keep.shape[0] // peers, down.shape[0]
    return pl.pallas_call(
        partial_kernel,
        out_shape=(
            jax.ShapeDtypeStruct((peers // 2, slots, depth), jnp.float32),
            jax.ShapeDtypeStruct((peers // 2, slots, depth), jnp.bfloat16),
        ),
        in_specs=whole(3),
        out_specs=tuple(whole(2)),
        scratch_shapes=[pltpu.VMEM((peers, slots, depth), jnp.float32)],
        compiler_params=params(8),
        name="partial_rows",
    )(keep, got, down)


def add_kernel(keep_ref, got_ref, mine_ref, theirs_ref):
    half = mine_ref.shape[0]
    mine_ref[...] = keep_ref[:half] + got_ref[:half].astype(jnp.float32)
    theirs_ref[...] = (keep_ref[half:] + got_ref[half:].astype(jnp.float32)).astype(jnp.bfloat16)


def add_halves(keep, got):
    half = (keep.shape[0] // 2, *keep.shape[1:])
    return pl.pallas_call(
        add_kernel,
        out_shape=(
            jax.ShapeDtypeStruct(half, jnp.float32),
            jax.ShapeDtypeStruct(half, jnp.bfloat16),
        ),
        in_specs=whole(2),
        out_specs=tuple(whole(2)),
        compiler_params=params(8),
        name="add_halves",
    )(keep, got)


def mix_kernel(own_ref, got_ref, chooser_ref, slot_weight_ref, mixed_ref):
    total = own_ref[0] + got_ref[0].astype(jnp.float32)
    weighted = (total * slot_weight_ref[:, :1]).astype(jnp.bfloat16)
    mixed_ref[...] = lax.dot_general(
        chooser_ref[...], weighted, ROW_DIMS, preferred_element_type=jnp.float32
    ).astype(jnp.bfloat16)


def mix(own, got, chooser, slot_weight):
    return pl.pallas_call(
        mix_kernel,
        out_shape=jax.ShapeDtypeStruct((chooser.shape[1], own.shape[2]), jnp.bfloat16),
        in_specs=whole(4),
        out_specs=whole(1)[0],
        compiler_params=params(8),
        name="mix",
    )(own, got, chooser, slot_weight)


def finish_kernel(blocks_ref, gate_ref, up_ref, down_ref):
    rows, width = gate_ref.shape
    half = width // 2
    sums = [blocks_ref[y].astype(jnp.float32) for y in range(2)]
    for k in range(2, blocks_ref.shape[0], 2):
        for y in range(2):
            sums[y] += blocks_ref[k + y].astype(jnp.float32)
    low = lanes(sums[0].shape) < half
    firsts = jnp.where(low, sums[0], pltpu.roll(sums[1], half, 1)).astype(jnp.bfloat16)
    seconds = jnp.where(low, pltpu.roll(sums[0], half, 1), sums[1]).astype(jnp.bfloat16)
    gate_ref[...] = firsts[:rows]
    up_ref[...] = seconds[:rows]
    down_ref[: rows // 2, :] = firsts[rows:]
    down_ref[rows // 2 :, :] = seconds[rows:]


def finish(blocks):
    _, packed_rows, width = blocks.shape
    shape = jax.ShapeDtypeStruct((packed_rows // 3 * 2, width), jnp.bfloat16)
    return pl.pallas_call(
        finish_kernel,
        out_shape=(shape,) * 3,
        in_specs=whole(1),
        out_specs=tuple(whole(3)),
        compiler_params=params(4),
        name="finish",
    )(blocks)


def swapped(part, axis, distance=1):
    size = lax.axis_size(axis)
    return lax.ppermute(part, axis, [(i, i ^ distance) for i in range(size)])


def per_device(tokens, cotangent, expert_ids, route_weights, join_groups, w_gate, w_up, w_down):
    own = jnp.stack([w_gate, w_up, w_down])
    got = swapped(own, "y")
    copies, chooser, slot_weight = route(
        expert_ids, route_weights, tokens, cotangent, lax.axis_size(PLANE)
    )
    packed = pack_shards(own, got)
    packed, copies = lax.optimization_barrier((packed, copies))
    rows_in = lax.all_to_all(copies, PLANE, 0, 0, tiled=True)
    along = lax.all_gather(packed, Z, axis=0, tiled=False)
    along, rows_in = lax.optimization_barrier((along, rows_in))
    other = swapped(along, "c")
    hidden_send, hidden, down, send, keep = expert(join_groups, rows_in, along, other)
    hidden_got = swapped(hidden_send, "y")
    from_core = swapped(send, "c")
    partial, partial_send = partial_rows(hidden, hidden_got, down, lax.axis_size(("h", "x")))
    from_core, partial_send = lax.optimization_barrier((from_core, partial_send))
    partial_got = swapped(partial_send, "x")
    keep, to_pair = add_halves(keep, from_core)
    from_pair = swapped(to_pair, "zl")
    pair_sum = (keep + from_pair.astype(jnp.float32)).astype(jnp.bfloat16)
    pair_sum = pair_sum.reshape(-1, *pair_sum.shape[3:])
    pair_sum, partial_got = lax.optimization_barrier((pair_sum, partial_got))
    pieces = lax.all_to_all(pair_sum, ("zh", "y"), 0, 0, tiled=True)
    partial, partial_send = add_halves(partial, partial_got)
    partial, partial_send = add_halves(partial, swapped(partial_send, "x", 2))
    mixed = mix(partial, swapped(partial_send, "h"), chooser, slot_weight)
    return (mixed, *finish(pieces))


def solution(mesh):
    experts = mesh.shape["expert"]
    split = Mesh(mesh.devices.reshape(-1, 2, 2, 2, 2, experts // 2), AXES)
    dp = ("zh", "zl", "y", "c")
    tok, weight = P(AXES, None), P(dp, ("h", "x"))
    return jax.shard_map(
        per_device,
        mesh=split,
        in_specs=(tok, tok, tok, tok, P(), weight, weight, weight),
        out_specs=(tok, weight, weight, weight),
        check_vma=False,
    )
```

```python
import jax
import jax.numpy as jnp
from jax import lax
from jax.experimental import pallas as pl
from jax.experimental.pallas import tpu as pltpu
from jax.sharding import Mesh
from jax.sharding import PartitionSpec as P

AXES = ("zh", "zl", "y", "c", "h", "x")
Z = ("zh", "zl")
PLANE = ("y", "h", "x")
HBM = pl.BlockSpec(memory_space=pltpu.HBM)
ROW_DIMS = (((0,), (0,)), ((), ()))
LANE_DIMS = (((1,), (1,)), ((), ()))


def whole(n):
    return [pl.BlockSpec(memory_space=pltpu.VMEM) for _ in range(n)]


def lanes(shape):
    return lax.broadcasted_iota(jnp.int32, shape, 1)


def halves_swapped(a):
    half = a.shape[1] // 2
    return pltpu.roll(a.astype(jnp.float32), half, 1)


def params(mib):
    return pltpu.CompilerParams(vmem_limit_bytes=mib * 1024 * 1024)


def cost(microseconds):
    return pl.CostEstimate(flops=int(1.1e9 * microseconds), transcendentals=0, bytes_accessed=int(3.7e6 * microseconds))


def route_kernel(
    ids_ref, share_ref, tokens_ref, cot_ref, copies_ref, chooser_ref, slot_weight_ref,
    held_ids, held_share, held_tokens, held_cot, both, chooser, weights, in_sems, out_sems, own_sems,
):
    count = ids_ref.shape[1]
    slots = chooser_ref.shape[0]
    peers = copies_ref.shape[0]
    pairs = (
        (ids_ref, held_ids), (share_ref, held_share), (tokens_ref, held_tokens), (cot_ref, held_cot)
    )
    reads = [
        pltpu.make_async_copy(src, dst, in_sems.at[k]) for k, (src, dst) in enumerate(pairs)
    ]
    for read in reads:
        read.start()
    square = (count, count)
    until = lax.broadcasted_iota(jnp.int32, square, 0) <= lanes(square)
    until = until.astype(jnp.bfloat16)
    slot = lax.broadcasted_iota(jnp.int32, (slots, count), 0).astype(jnp.float32)
    reads[0].wait()
    reads[1].wait()
    chosen = held_ids[...] == 0
    routed = jnp.max(chosen.astype(jnp.float32), axis=0, keepdims=True)
    weight = jnp.sum(jnp.where(chosen, held_share[...], 0.0), axis=0, keepdims=True)
    before = jnp.dot(
        jnp.broadcast_to(routed, (slots, count)).astype(jnp.bfloat16),
        until,
        preferred_element_type=jnp.float32,
    )
    place = jnp.where((before - 1.0 == slot) & (routed > 0.0), 1.0, 0.0)
    slot_weight = jnp.sum(place * weight, axis=1, keepdims=True)
    chooser[...] = place.astype(jnp.bfloat16)
    weights[...] = jnp.broadcast_to(slot_weight, weights.shape)
    writes = [
        pltpu.make_async_copy(chooser, chooser_ref, own_sems.at[0]),
        pltpu.make_async_copy(weights, slot_weight_ref, own_sems.at[1]),
    ]
    for write in writes:
        write.start()
    for part, held in enumerate((held_tokens, held_cot)):
        reads[2 + part].wait()
        rows = jnp.dot(chooser[...], held[...], preferred_element_type=jnp.float32)
        both[part] = (rows * slot_weight if part else rows).astype(jnp.bfloat16)
        for k in range(peers):
            writes.append(
                pltpu.make_async_copy(
                    both.at[part],
                    copies_ref.at[k, pl.ds(part * slots, slots), :],
                    out_sems.at[part, k],
                )
            )
            writes[-1].start()
    for write in writes:
        write.wait()


def route(ids, share, tokens, cot, peers):
    count, width = tokens.shape
    slots = count // 8
    top = ids.shape[1]
    return pl.pallas_call(
        route_kernel,
        out_shape=(
            jax.ShapeDtypeStruct((peers, 2 * slots, width), jnp.bfloat16),
            jax.ShapeDtypeStruct((slots, count), jnp.bfloat16),
            jax.ShapeDtypeStruct((slots, 128), jnp.float32),
        ),
        in_specs=[HBM] * 4,
        out_specs=(HBM,) * 3,
        scratch_shapes=[
            pltpu.VMEM((top, count), jnp.int32),
            pltpu.VMEM((top, count), jnp.float32),
            pltpu.VMEM((count, width), jnp.bfloat16),
            pltpu.VMEM((count, width), jnp.bfloat16),
            pltpu.VMEM((2, slots, width), jnp.bfloat16),
            pltpu.VMEM((slots, count), jnp.bfloat16),
            pltpu.VMEM((slots, 128), jnp.float32),
            pltpu.SemaphoreType.DMA((4,)),
            pltpu.SemaphoreType.DMA((2, peers)),
            pltpu.SemaphoreType.DMA((2,)),
        ],
        compiler_params=params(56),
        name="route",
    )(ids.T, share.T, tokens, cot)


def pack_kernel(own_ref, got_ref, packed_ref):
    rows, width = own_ref.shape[1:]
    low = lanes((rows, width)) < width // 2
    top = lax.axis_index("y") == 0

    def half_of(left, right):
        left, right = left.astype(jnp.float32), right.astype(jnp.float32)
        if_top = jnp.where(low, left, halves_swapped(right))
        return jnp.where(top, if_top, jnp.where(low, halves_swapped(left), right)).astype(jnp.bfloat16)

    mine = half_of(own_ref[0], own_ref[1])
    got = half_of(got_ref[0], got_ref[1])
    packed_ref[:rows, :] = jnp.where(top, mine, got)
    packed_ref[rows : 2 * rows, :] = jnp.where(top, got, mine)
    packed_ref[2 * rows : 3 * rows, :] = jnp.where(top, own_ref[2], got_ref[2])
    packed_ref[3 * rows :, :] = jnp.where(top, got_ref[2], own_ref[2])


def pack_shards(own, got):
    _, rows, width = own.shape
    return pl.pallas_call(
        pack_kernel,
        out_shape=jax.ShapeDtypeStruct((4 * rows, width), own.dtype),
        in_specs=whole(2),
        out_specs=whole(1)[0],
        compiler_params=params(2),
        name="pack_shards",
    )(own, got)


def forward_kernel(
    both_ref, own_ref, got_ref, hidden_send_ref, hidden_keep_ref, acts_ref, down, gate_up, hiddens
):
    chips, rows, width = own_ref.shape
    rows = rows // 4
    half = width // 2
    peers, slots = both_ref.shape[0], both_ref.shape[1] // 2
    y, c = lax.axis_index("y"), lax.axis_index("c")
    for core, ref in ((c, own_ref), (1 - c, got_ref)):
        for chip in range(chips):
            for k in range(2):
                at = pl.multiple_of((chip * 2 + k) * 2 * rows + core * rows, rows)
                gate_up[pl.ds(at, rows), :] = ref[chip, k * rows : (k + 1) * rows, :]
                down[pl.ds(at, rows), :] = ref[chip, (2 + k) * rows : (3 + k) * rows, :]
    total = peers * slots
    picked = both_ref[:, :slots, :].reshape(total, both_ref.shape[2])
    acts = jnp.dot(picked, gate_up[...], preferred_element_type=jnp.float32)
    acts_ref[...] = acts
    gate, up, _ = gate_and_up(acts)
    hidden = gate * jax.nn.sigmoid(gate) * up
    mine = (lanes(acts.shape) >= half) == (y == 1)
    hiddens[...] = jnp.where(mine, hidden, 0.0)
    group_rows = total // 2
    hidden_send_ref[...] = hiddens[pl.ds((1 - y) * group_rows, group_rows), :].astype(jnp.bfloat16)
    hidden_keep_ref[...] = hiddens[pl.ds(y * group_rows, group_rows), :].astype(jnp.bfloat16)


def gate_and_up(acts):
    half = acts.shape[1] // 2
    turned = pltpu.roll(acts, half, 1)
    low = lanes(acts.shape) < half
    return jnp.where(low, acts, turned), jnp.where(low, turned, acts), low


def forward(both, own, got):
    peers, doubled, depth = both.shape
    rows = peers * doubled // 2
    width = own.shape[2]
    hidden = jax.ShapeDtypeStruct((rows // 2, width), jnp.bfloat16)
    return pl.pallas_call(
        forward_kernel,
        out_shape=(
            hidden,
            hidden,
            jax.ShapeDtypeStruct((rows, width), jnp.float32),
            jax.ShapeDtypeStruct((depth, width), jnp.bfloat16),
        ),
        in_specs=whole(3),
        out_specs=tuple(whole(4)),
        scratch_shapes=[
            pltpu.VMEM((depth, width), jnp.bfloat16),
            pltpu.VMEM((rows, width), jnp.float32),
        ],
        compiler_params=params(12),
        name="forward",
    )(both, own, got)


def backward_kernel(join_ref, both_ref, acts_ref, down, send_ref, keep_ref, terms):
    peers, slots = both_ref.shape[0], both_ref.shape[1] // 2
    depth = both_ref.shape[2]
    total, width = acts_ref.shape
    half = width // 2
    chips = send_ref.shape[0] * send_ref.shape[1]
    rows = send_ref.shape[3] // 3 * 2
    z, y, c = lax.axis_index(Z), lax.axis_index("y"), lax.axis_index("c")
    picked = both_ref[:, :slots, :].reshape(total, depth)
    dpicked = both_ref[:, slots:, :].reshape(total, depth)
    gate, up, low = gate_and_up(acts_ref[...])
    sigma = jax.nn.sigmoid(gate)
    hidden = gate * sigma * up
    mine = (lanes(gate.shape) >= half) == (y == 1)
    dhidden = jnp.dot(dpicked, down[...], preferred_element_type=jnp.float32)
    dhidden = jnp.where(mine, dhidden, pltpu.roll(dhidden, half, 1))
    dgate = dhidden * up * sigma * (1.0 + gate * (1.0 - sigma))
    dup = dhidden * gate * sigma
    first = 1.0 - join_ref[(z * 2 + 0) * 2 + c].astype(jnp.float32)
    second = 1.0 - join_ref[(z * 2 + 1) * 2 + c].astype(jnp.float32)
    group = lax.broadcasted_iota(jnp.int32, gate.shape, 0) // (total // 2)
    active = jnp.where(group == 0, first, second)
    dacts = (jnp.where(low, dgate, dup) * active).astype(jnp.bfloat16)
    counted = (hidden.astype(jnp.bfloat16).astype(jnp.float32) * active).astype(jnp.bfloat16)
    terms[0] = lax.dot_general(picked, dacts, ROW_DIMS, preferred_element_type=jnp.float32)
    terms[1] = lax.dot_general(dpicked, counted, ROW_DIMS, preferred_element_type=jnp.float32)
    half_rows = rows // 2
    low = lanes((half_rows, width)) < half
    for chip in range(chips):
        for k in range(2):
            base = (chip * 2 + k) * 2 * rows
            away = jnp.bitwise_xor(chip % 2, lax.rem(z, 2))
            for which, ref in ((c, keep_ref), (1 - c, send_ref)):
                at = pl.multiple_of(base + which * rows, rows)
                ref[away, chip // 2, k, :rows, :] = terms[0, pl.ds(at, rows), :].astype(ref.dtype)
                packed = jnp.where(
                    low,
                    terms[1, pl.ds(at, half_rows), :],
                    terms[1, pl.ds(at + half_rows, half_rows), :],
                )
                ref[away, chip // 2, k, rows:, :] = packed.astype(ref.dtype)


def backward(join, both, acts, down, chips):
    depth, width = down.shape
    rows = depth // chips // 4
    chunk = (2, chips // 2, 2, rows // 2 * 3, width)
    return pl.pallas_call(
        backward_kernel,
        out_shape=(
            jax.ShapeDtypeStruct(chunk, jnp.bfloat16),
            jax.ShapeDtypeStruct(chunk, jnp.float32),
        ),
        in_specs=[pl.BlockSpec(memory_space=pltpu.SMEM), *whole(3)],
        out_specs=tuple(whole(2)),
        scratch_shapes=[pltpu.VMEM((2, depth, width), jnp.float32)],
        compiler_params=params(16),
        cost_estimate=cost(8),
        name="backward",
    )(join, both, acts, down)


def partial_kernel(keep_ref, got_ref, down_ref, mine_ref, theirs_ref, partials):
    partial = lax.dot_general(
        keep_ref[...] + got_ref[...], down_ref[...], LANE_DIMS, preferred_element_type=jnp.float32
    )
    partials[...] = partial.reshape(partials.shape)
    h, x = lax.axis_index("h"), lax.axis_index("x")
    for low, ref in enumerate((mine_ref, theirs_ref)):
        for high in range(2):
            for row in range(2):
                peer = jnp.bitwise_xor(h, row) * 4 + jnp.bitwise_xor(x, 2 * high + low)
                ref[2 * high + row] = partials[peer].astype(ref.dtype)


def partial_rows(keep, got, down, peers):
    slots, depth = keep.shape[0] // peers, down.shape[0]
    return pl.pallas_call(
        partial_kernel,
        out_shape=(
            jax.ShapeDtypeStruct((peers // 2, slots, depth), jnp.float32),
            jax.ShapeDtypeStruct((peers // 2, slots, depth), jnp.bfloat16),
        ),
        in_specs=whole(3),
        out_specs=tuple(whole(2)),
        scratch_shapes=[pltpu.VMEM((peers, slots, depth), jnp.float32)],
        compiler_params=params(8),
        cost_estimate=cost(5),
        name="partial_rows",
    )(keep, got, down)


def add_kernel(keep_ref, got_ref, mine_ref, theirs_ref):
    half = mine_ref.shape[0]
    mine_ref[...] = keep_ref[:half] + got_ref[:half].astype(jnp.float32)
    theirs_ref[...] = (keep_ref[half:] + got_ref[half:].astype(jnp.float32)).astype(jnp.bfloat16)


def add_halves(keep, got, lasts):
    half = (keep.shape[0] // 2, *keep.shape[1:])
    return pl.pallas_call(
        add_kernel,
        out_shape=(
            jax.ShapeDtypeStruct(half, jnp.float32),
            jax.ShapeDtypeStruct(half, jnp.bfloat16),
        ),
        in_specs=whole(2),
        out_specs=tuple(whole(2)),
        compiler_params=params(8),
        cost_estimate=cost(lasts),
        name="add_halves",
    )(keep, got)


def mix_kernel(own_ref, got_ref, chooser_ref, slot_weight_ref, mixed_ref):
    total = own_ref[0] + got_ref[0].astype(jnp.float32)
    weighted = (total * slot_weight_ref[:, :1]).astype(jnp.bfloat16)
    mixed_ref[...] = lax.dot_general(
        chooser_ref[...], weighted, ROW_DIMS, preferred_element_type=jnp.float32
    ).astype(jnp.bfloat16)


def mix(own, got, chooser, slot_weight):
    return pl.pallas_call(
        mix_kernel,
        out_shape=jax.ShapeDtypeStruct((chooser.shape[1], own.shape[2]), jnp.bfloat16),
        in_specs=whole(4),
        out_specs=whole(1)[0],
        compiler_params=params(8),
        cost_estimate=cost(1),
        name="mix",
    )(own, got, chooser, slot_weight)


def finish_kernel(blocks_ref, gate_ref, up_ref, down_ref):
    rows, width = gate_ref.shape
    half = width // 2
    sums = [blocks_ref[y].astype(jnp.float32) for y in range(2)]
    for k in range(2, blocks_ref.shape[0], 2):
        for y in range(2):
            sums[y] += blocks_ref[k + y].astype(jnp.float32)
    low = lanes(sums[0].shape) < half
    firsts = jnp.where(low, sums[0], pltpu.roll(sums[1], half, 1)).astype(jnp.bfloat16)
    seconds = jnp.where(low, pltpu.roll(sums[0], half, 1), sums[1]).astype(jnp.bfloat16)
    gate_ref[...] = firsts[:rows]
    up_ref[...] = seconds[:rows]
    down_ref[: rows // 2, :] = firsts[rows:]
    down_ref[rows // 2 :, :] = seconds[rows:]


def finish(blocks):
    _, packed_rows, width = blocks.shape
    shape = jax.ShapeDtypeStruct((packed_rows // 3 * 2, width), jnp.bfloat16)
    return pl.pallas_call(
        finish_kernel,
        out_shape=(shape,) * 3,
        in_specs=whole(1),
        out_specs=tuple(whole(3)),
        compiler_params=params(4),
        name="finish",
    )(blocks)


def swapped(part, axis, distance=1):
    size = lax.axis_size(axis)
    return lax.ppermute(part, axis, [(i, i ^ distance) for i in range(size)])


def per_device(tokens, cotangent, expert_ids, route_weights, join_groups, w_gate, w_up, w_down):
    own = jnp.stack([w_gate, w_up, w_down])
    got = swapped(own, "y")
    copies, chooser, slot_weight = route(
        expert_ids, route_weights, tokens, cotangent, lax.axis_size(PLANE)
    )
    packed = pack_shards(own, got)
    packed, copies = lax.optimization_barrier((packed, copies))
    rows_in = lax.all_to_all(copies, PLANE, 0, 0, tiled=True)
    along = lax.all_gather(packed, Z, axis=0, tiled=False)
    along, rows_in = lax.optimization_barrier((along, rows_in))
    other = swapped(along, "c")
    hidden_send, hidden, acts, down = forward(rows_in, along, other)
    hidden_got = swapped(hidden_send, "y")
    send, keep = backward(join_groups, rows_in, acts, down, lax.axis_size(Z))
    from_core = swapped(send, "c")
    partial, partial_send = partial_rows(hidden, hidden_got, down, lax.axis_size(("h", "x")))
    partial_got = swapped(partial_send, "x")
    from_core, _ = lax.optimization_barrier((from_core, partial_send))
    keep, to_pair = add_halves(keep, from_core, 0.4)
    from_pair = swapped(to_pair, "zl")
    pair_sum = (keep + from_pair.astype(jnp.float32)).astype(jnp.bfloat16)
    pair_sum = pair_sum.reshape(-1, *pair_sum.shape[3:])
    pieces = lax.all_to_all(pair_sum, ("zh", "y"), 0, 0, tiled=True)
    partial, partial_send = add_halves(partial, partial_got, 2)
    partial, partial_send = add_halves(partial, swapped(partial_send, "x", 2), 1)
    mixed = mix(partial, swapped(partial_send, "h"), chooser, slot_weight)
    return (mixed, *finish(pieces))


def solution(mesh):
    experts = mesh.shape["expert"]
    split = Mesh(mesh.devices.reshape(-1, 2, 2, 2, 2, experts // 2), AXES)
    dp = ("zh", "zl", "y", "c")
    tok, weight = P(AXES, None), P(dp, ("h", "x"))
    return jax.shard_map(
        per_device,
        mesh=split,
        in_specs=(tok, tok, tok, tok, P(), weight, weight, weight),
        out_specs=(tok, weight, weight, weight),
        check_vma=False,
    )
```

```python
import jax
import jax.numpy as jnp
from jax import lax
from jax.experimental import pallas as pl
from jax.experimental.pallas import tpu as pltpu
from jax.sharding import Mesh
from jax.sharding import PartitionSpec as P

AXES = ("zh", "zl", "y", "c", "h", "x")
Z = ("zh", "zl")
PLANE = ("y", "h", "x")
HBM = pl.BlockSpec(memory_space=pltpu.HBM)
ROW_DIMS = (((0,), (0,)), ((), ()))
LANE_DIMS = (((1,), (1,)), ((), ()))


def whole(n):
    return [pl.BlockSpec(memory_space=pltpu.VMEM) for _ in range(n)]


def lanes(shape):
    return lax.broadcasted_iota(jnp.int32, shape, 1)


def halves_swapped(a):
    half = a.shape[1] // 2
    return pltpu.roll(a.astype(jnp.float32), half, 1)


def params(mib):
    return pltpu.CompilerParams(vmem_limit_bytes=mib * 1024 * 1024)


def cost(microseconds):
    return pl.CostEstimate(flops=int(1.1e9 * microseconds), transcendentals=0, bytes_accessed=int(3.7e6 * microseconds))


def route_kernel(
    ids_ref, share_ref, tokens_ref, cot_ref, copies_ref, chooser_ref, slot_weight_ref,
    held_ids, held_share, held_tokens, held_cot, both, chooser, weights, in_sems, out_sems, own_sems,
):
    count = ids_ref.shape[1]
    slots = chooser_ref.shape[0]
    peers = copies_ref.shape[0]
    pairs = (
        (ids_ref, held_ids), (share_ref, held_share), (tokens_ref, held_tokens), (cot_ref, held_cot)
    )
    reads = [
        pltpu.make_async_copy(src, dst, in_sems.at[k]) for k, (src, dst) in enumerate(pairs)
    ]
    for read in reads:
        read.start()
    square = (count, count)
    until = lax.broadcasted_iota(jnp.int32, square, 0) <= lanes(square)
    until = until.astype(jnp.bfloat16)
    slot = lax.broadcasted_iota(jnp.int32, (slots, count), 0).astype(jnp.float32)
    reads[0].wait()
    reads[1].wait()
    chosen = held_ids[...] == 0
    routed = jnp.max(chosen.astype(jnp.float32), axis=0, keepdims=True)
    weight = jnp.sum(jnp.where(chosen, held_share[...], 0.0), axis=0, keepdims=True)
    before = jnp.dot(
        jnp.broadcast_to(routed, (slots, count)).astype(jnp.bfloat16),
        until,
        preferred_element_type=jnp.float32,
    )
    place = jnp.where((before - 1.0 == slot) & (routed > 0.0), 1.0, 0.0)
    slot_weight = jnp.sum(place * weight, axis=1, keepdims=True)
    chooser[...] = place.astype(jnp.bfloat16)
    weights[...] = jnp.broadcast_to(slot_weight, weights.shape)
    writes = [
        pltpu.make_async_copy(chooser, chooser_ref, own_sems.at[0]),
        pltpu.make_async_copy(weights, slot_weight_ref, own_sems.at[1]),
    ]
    for write in writes:
        write.start()
    for part, held in enumerate((held_tokens, held_cot)):
        reads[2 + part].wait()
        rows = jnp.dot(chooser[...], held[...], preferred_element_type=jnp.float32)
        both[part] = (rows * slot_weight if part else rows).astype(jnp.bfloat16)
        for k in range(peers):
            writes.append(
                pltpu.make_async_copy(
                    both.at[part],
                    copies_ref.at[k, pl.ds(part * slots, slots), :],
                    out_sems.at[part, k],
                )
            )
            writes[-1].start()
    for write in writes:
        write.wait()


def route(ids, share, tokens, cot, peers):
    count, width = tokens.shape
    slots = count // 8
    top = ids.shape[1]
    return pl.pallas_call(
        route_kernel,
        out_shape=(
            jax.ShapeDtypeStruct((peers, 2 * slots, width), jnp.bfloat16),
            jax.ShapeDtypeStruct((slots, count), jnp.bfloat16),
            jax.ShapeDtypeStruct((slots, 128), jnp.float32),
        ),
        in_specs=[HBM] * 4,
        out_specs=(HBM,) * 3,
        scratch_shapes=[
            pltpu.VMEM((top, count), jnp.int32),
            pltpu.VMEM((top, count), jnp.float32),
            pltpu.VMEM((count, width), jnp.bfloat16),
            pltpu.VMEM((count, width), jnp.bfloat16),
            pltpu.VMEM((2, slots, width), jnp.bfloat16),
            pltpu.VMEM((slots, count), jnp.bfloat16),
            pltpu.VMEM((slots, 128), jnp.float32),
            pltpu.SemaphoreType.DMA((4,)),
            pltpu.SemaphoreType.DMA((2, peers)),
            pltpu.SemaphoreType.DMA((2,)),
        ],
        compiler_params=params(56),
        name="route",
    )(ids.T, share.T, tokens, cot)


def pack_kernel(own_ref, got_ref, packed_ref):
    rows, width = own_ref.shape[1:]
    low = lanes((rows, width)) < width // 2
    top = lax.axis_index("y") == 0

    def half_of(left, right):
        left, right = left.astype(jnp.float32), right.astype(jnp.float32)
        if_top = jnp.where(low, left, halves_swapped(right))
        return jnp.where(top, if_top, jnp.where(low, halves_swapped(left), right)).astype(jnp.bfloat16)

    mine = half_of(own_ref[0], own_ref[1])
    got = half_of(got_ref[0], got_ref[1])
    packed_ref[:rows, :] = jnp.where(top, mine, got)
    packed_ref[rows : 2 * rows, :] = jnp.where(top, got, mine)
    packed_ref[2 * rows : 3 * rows, :] = jnp.where(top, own_ref[2], got_ref[2])
    packed_ref[3 * rows :, :] = jnp.where(top, got_ref[2], own_ref[2])


def pack_shards(own, got):
    _, rows, width = own.shape
    return pl.pallas_call(
        pack_kernel,
        out_shape=jax.ShapeDtypeStruct((4 * rows, width), own.dtype),
        in_specs=whole(2),
        out_specs=whole(1)[0],
        compiler_params=params(2),
        name="pack_shards",
    )(own, got)


def forward_kernel(
    both_ref, own_ref, got_ref, hidden_send_ref, hidden_keep_ref, acts_ref, down, gate_up, hiddens
):
    chips, rows, width = own_ref.shape
    rows = rows // 4
    half = width // 2
    peers, slots = both_ref.shape[0], both_ref.shape[1] // 2
    y, c = lax.axis_index("y"), lax.axis_index("c")
    for core, ref in ((c, own_ref), (1 - c, got_ref)):
        for chip in range(chips):
            for k in range(2):
                at = pl.multiple_of((chip * 2 + k) * 2 * rows + core * rows, rows)
                gate_up[pl.ds(at, rows), :] = ref[chip, k * rows : (k + 1) * rows, :]
                down[pl.ds(at, rows), :] = ref[chip, (2 + k) * rows : (3 + k) * rows, :]
    total = peers * slots
    picked = both_ref[:, :slots, :].reshape(total, both_ref.shape[2])
    acts = jnp.dot(picked, gate_up[...], preferred_element_type=jnp.float32)
    acts_ref[...] = acts
    gate, up, _ = gate_and_up(acts)
    hidden = gate * jax.nn.sigmoid(gate) * up
    mine = (lanes(acts.shape) >= half) == (y == 1)
    hiddens[...] = jnp.where(mine, hidden, 0.0)
    group_rows = total // 2
    hidden_send_ref[...] = hiddens[pl.ds((1 - y) * group_rows, group_rows), :].astype(jnp.bfloat16)
    hidden_keep_ref[...] = hiddens[pl.ds(y * group_rows, group_rows), :].astype(jnp.bfloat16)


def gate_and_up(acts):
    half = acts.shape[1] // 2
    turned = pltpu.roll(acts, half, 1)
    low = lanes(acts.shape) < half
    return jnp.where(low, acts, turned), jnp.where(low, turned, acts), low


def forward(both, own, got):
    peers, doubled, depth = both.shape
    rows = peers * doubled // 2
    width = own.shape[2]
    hidden = jax.ShapeDtypeStruct((rows // 2, width), jnp.bfloat16)
    return pl.pallas_call(
        forward_kernel,
        out_shape=(
            hidden,
            hidden,
            jax.ShapeDtypeStruct((rows, width), jnp.float32),
            jax.ShapeDtypeStruct((depth, width), jnp.bfloat16),
        ),
        in_specs=whole(3),
        out_specs=tuple(whole(4)),
        scratch_shapes=[
            pltpu.VMEM((depth, width), jnp.bfloat16),
            pltpu.VMEM((rows, width), jnp.float32),
        ],
        compiler_params=params(12),
        name="forward",
    )(both, own, got)


def backward_kernel(join_ref, both_ref, acts_ref, down, send_ref, keep_ref, terms):
    peers, slots = both_ref.shape[0], both_ref.shape[1] // 2
    depth = both_ref.shape[2]
    total, width = acts_ref.shape
    half = width // 2
    chips = send_ref.shape[0] * send_ref.shape[1]
    rows = send_ref.shape[3] // 3 * 2
    z, y, c = lax.axis_index(Z), lax.axis_index("y"), lax.axis_index("c")
    picked = both_ref[:, :slots, :].reshape(total, depth)
    dpicked = both_ref[:, slots:, :].reshape(total, depth)
    gate, up, low = gate_and_up(acts_ref[...])
    sigma = jax.nn.sigmoid(gate)
    hidden = gate * sigma * up
    mine = (lanes(gate.shape) >= half) == (y == 1)
    dhidden = jnp.dot(dpicked, down[...], preferred_element_type=jnp.float32)
    dhidden = jnp.where(mine, dhidden, pltpu.roll(dhidden, half, 1))
    dgate = dhidden * up * sigma * (1.0 + gate * (1.0 - sigma))
    dup = dhidden * gate * sigma
    first = 1.0 - join_ref[(z * 2 + 0) * 2 + c].astype(jnp.float32)
    second = 1.0 - join_ref[(z * 2 + 1) * 2 + c].astype(jnp.float32)
    group = lax.broadcasted_iota(jnp.int32, gate.shape, 0) // (total // 2)
    active = jnp.where(group == 0, first, second)
    dacts = (jnp.where(low, dgate, dup) * active).astype(jnp.bfloat16)
    counted = (hidden.astype(jnp.bfloat16).astype(jnp.float32) * active).astype(jnp.bfloat16)
    terms[0] = lax.dot_general(picked, dacts, ROW_DIMS, preferred_element_type=jnp.float32)
    terms[1] = lax.dot_general(dpicked, counted, ROW_DIMS, preferred_element_type=jnp.float32)
    half_rows = rows // 2
    low = lanes((half_rows, width)) < half
    for chip in range(chips):
        for k in range(2):
            base = (chip * 2 + k) * 2 * rows
            away = jnp.bitwise_xor(chip % 2, lax.rem(z, 2))
            for which, ref in ((c, keep_ref), (1 - c, send_ref)):
                at = pl.multiple_of(base + which * rows, rows)
                ref[away, chip // 2, k, :rows, :] = terms[0, pl.ds(at, rows), :].astype(ref.dtype)
                packed = jnp.where(
                    low,
                    terms[1, pl.ds(at, half_rows), :],
                    terms[1, pl.ds(at + half_rows, half_rows), :],
                )
                ref[away, chip // 2, k, rows:, :] = packed.astype(ref.dtype)


def backward(join, both, acts, down, chips):
    depth, width = down.shape
    rows = depth // chips // 4
    chunk = (2, chips // 2, 2, rows // 2 * 3, width)
    return pl.pallas_call(
        backward_kernel,
        out_shape=(
            jax.ShapeDtypeStruct(chunk, jnp.bfloat16),
            jax.ShapeDtypeStruct(chunk, jnp.float32),
        ),
        in_specs=[pl.BlockSpec(memory_space=pltpu.SMEM), *whole(3)],
        out_specs=tuple(whole(2)),
        scratch_shapes=[pltpu.VMEM((2, depth, width), jnp.float32)],
        compiler_params=params(16),
        cost_estimate=cost(8),
        name="backward",
    )(join, both, acts, down)


def partial_kernel(keep_ref, got_ref, down_ref, mine_ref, theirs_ref, partials):
    partial = lax.dot_general(
        keep_ref[...] + got_ref[...], down_ref[...], LANE_DIMS, preferred_element_type=jnp.float32
    )
    partials[...] = partial.reshape(partials.shape)
    h, x = lax.axis_index("h"), lax.axis_index("x")
    for high, ref in enumerate((mine_ref, theirs_ref)):
        for low in range(2):
            for row in range(2):
                peer = jnp.bitwise_xor(h, row) * 4 + jnp.bitwise_xor(x, 2 * high + low)
                ref[2 * low + row] = partials[peer].astype(ref.dtype)


def partial_rows(keep, got, down, peers):
    slots, depth = keep.shape[0] // peers, down.shape[0]
    return pl.pallas_call(
        partial_kernel,
        out_shape=(
            jax.ShapeDtypeStruct((peers // 2, slots, depth), jnp.float32),
            jax.ShapeDtypeStruct((peers // 2, slots, depth), jnp.bfloat16),
        ),
        in_specs=whole(3),
        out_specs=tuple(whole(2)),
        scratch_shapes=[pltpu.VMEM((peers, slots, depth), jnp.float32)],
        compiler_params=params(8),
        cost_estimate=cost(5),
        name="partial_rows",
    )(keep, got, down)


def add_kernel(keep_ref, got_ref, mine_ref, theirs_ref):
    half = mine_ref.shape[0]
    mine_ref[...] = keep_ref[:half] + got_ref[:half].astype(jnp.float32)
    theirs_ref[...] = (keep_ref[half:] + got_ref[half:].astype(jnp.float32)).astype(jnp.bfloat16)


def add_halves(keep, got, lasts):
    half = (keep.shape[0] // 2, *keep.shape[1:])
    return pl.pallas_call(
        add_kernel,
        out_shape=(
            jax.ShapeDtypeStruct(half, jnp.float32),
            jax.ShapeDtypeStruct(half, jnp.bfloat16),
        ),
        in_specs=whole(2),
        out_specs=tuple(whole(2)),
        compiler_params=params(8),
        cost_estimate=cost(lasts),
        name="add_halves",
    )(keep, got)


def mix_kernel(own_ref, got_ref, chooser_ref, slot_weight_ref, mixed_ref):
    total = own_ref[0] + got_ref[0].astype(jnp.float32)
    weighted = (total * slot_weight_ref[:, :1]).astype(jnp.bfloat16)
    mixed_ref[...] = lax.dot_general(
        chooser_ref[...], weighted, ROW_DIMS, preferred_element_type=jnp.float32
    ).astype(jnp.bfloat16)


def mix(own, got, chooser, slot_weight):
    return pl.pallas_call(
        mix_kernel,
        out_shape=jax.ShapeDtypeStruct((chooser.shape[1], own.shape[2]), jnp.bfloat16),
        in_specs=whole(4),
        out_specs=whole(1)[0],
        compiler_params=params(8),
        cost_estimate=cost(1),
        name="mix",
    )(own, got, chooser, slot_weight)


def finish_kernel(blocks_ref, gate_ref, up_ref, down_ref):
    rows, width = gate_ref.shape
    half = width // 2
    sums = [blocks_ref[y].astype(jnp.float32) for y in range(2)]
    for k in range(2, blocks_ref.shape[0], 2):
        for y in range(2):
            sums[y] += blocks_ref[k + y].astype(jnp.float32)
    low = lanes(sums[0].shape) < half
    firsts = jnp.where(low, sums[0], pltpu.roll(sums[1], half, 1)).astype(jnp.bfloat16)
    seconds = jnp.where(low, pltpu.roll(sums[0], half, 1), sums[1]).astype(jnp.bfloat16)
    gate_ref[...] = firsts[:rows]
    up_ref[...] = seconds[:rows]
    down_ref[: rows // 2, :] = firsts[rows:]
    down_ref[rows // 2 :, :] = seconds[rows:]


def finish(blocks):
    _, packed_rows, width = blocks.shape
    shape = jax.ShapeDtypeStruct((packed_rows // 3 * 2, width), jnp.bfloat16)
    return pl.pallas_call(
        finish_kernel,
        out_shape=(shape,) * 3,
        in_specs=whole(1),
        out_specs=tuple(whole(3)),
        compiler_params=params(4),
        name="finish",
    )(blocks)


def swapped(part, axis, distance=1):
    size = lax.axis_size(axis)
    return lax.ppermute(part, axis, [(i, i ^ distance) for i in range(size)])


def per_device(tokens, cotangent, expert_ids, route_weights, join_groups, w_gate, w_up, w_down):
    own = jnp.stack([w_gate, w_up, w_down])
    got = swapped(own, "y")
    copies, chooser, slot_weight = route(
        expert_ids, route_weights, tokens, cotangent, lax.axis_size(PLANE)
    )
    packed = pack_shards(own, got)
    packed, copies = lax.optimization_barrier((packed, copies))
    rows_in = lax.all_to_all(copies, PLANE, 0, 0, tiled=True)
    along = lax.all_gather(packed, Z, axis=0, tiled=False)
    along, rows_in = lax.optimization_barrier((along, rows_in))
    other = swapped(along, "c")
    hidden_send, hidden, acts, down = forward(rows_in, along, other)
    hidden_got = swapped(hidden_send, "y")
    send, keep = backward(join_groups, rows_in, acts, down, lax.axis_size(Z))
    from_core = swapped(send, "c")
    partial, partial_send = partial_rows(hidden, hidden_got, down, lax.axis_size(("h", "x")))
    partial_got = swapped(partial_send, "x", 2)
    from_core, _ = lax.optimization_barrier((from_core, partial_send))
    keep, to_pair = add_halves(keep, from_core, 0.4)
    from_pair = swapped(to_pair, "zl")
    pair_sum = (keep + from_pair.astype(jnp.float32)).astype(jnp.bfloat16)
    pair_sum = pair_sum.reshape(-1, *pair_sum.shape[3:])
    pieces = lax.all_to_all(pair_sum, ("zh", "y"), 0, 0, tiled=True)
    partial, partial_send = add_halves(partial, partial_got, 2)
    partial, partial_send = add_halves(partial, swapped(partial_send, "x"), 1)
    mixed = mix(partial, swapped(partial_send, "h"), chooser, slot_weight)
    return (mixed, *finish(pieces))


def solution(mesh):
    experts = mesh.shape["expert"]
    split = Mesh(mesh.devices.reshape(-1, 2, 2, 2, 2, experts // 2), AXES)
    dp = ("zh", "zl", "y", "c")
    tok, weight = P(AXES, None), P(dp, ("h", "x"))
    return jax.shard_map(
        per_device,
        mesh=split,
        in_specs=(tok, tok, tok, tok, P(), weight, weight, weight),
        out_specs=(tok, weight, weight, weight),
        check_vma=False,
    )
```

```python
import jax
import jax.numpy as jnp
from jax import lax
from jax.experimental import pallas as pl
from jax.experimental.pallas import tpu as pltpu
from jax.sharding import Mesh
from jax.sharding import PartitionSpec as P

AXES = ("zh", "zm", "zl", "y", "c", "h", "x")
Z = ("zh", "zm", "zl")
PLANE = ("y", "h", "x")
HBM = pl.BlockSpec(memory_space=pltpu.HBM)
ROW_DIMS = (((0,), (0,)), ((), ()))
LANE_DIMS = (((1,), (1,)), ((), ()))


def whole(n):
    return [pl.BlockSpec(memory_space=pltpu.VMEM) for _ in range(n)]


def lanes(shape):
    return lax.broadcasted_iota(jnp.int32, shape, 1)


def halves_swapped(a):
    half = a.shape[1] // 2
    return pltpu.roll(a.astype(jnp.float32), half, 1)


def params(mib):
    return pltpu.CompilerParams(vmem_limit_bytes=mib * 1024 * 1024)


def cost(microseconds):
    return pl.CostEstimate(flops=int(1.1e9 * microseconds), transcendentals=0, bytes_accessed=int(3.7e6 * microseconds))


def route_kernel(
    ids_ref, share_ref, tokens_ref, cot_ref, copies_ref, chooser_ref, slot_weight_ref,
    held_ids, held_share, held_tokens, held_cot, both, chooser, weights, in_sems, out_sems, own_sems,
):
    count = ids_ref.shape[1]
    slots = chooser_ref.shape[0]
    peers = copies_ref.shape[0]
    pairs = (
        (ids_ref, held_ids), (share_ref, held_share), (tokens_ref, held_tokens), (cot_ref, held_cot)
    )
    reads = [
        pltpu.make_async_copy(src, dst, in_sems.at[k]) for k, (src, dst) in enumerate(pairs)
    ]
    for read in reads:
        read.start()
    square = (count, count)
    until = lax.broadcasted_iota(jnp.int32, square, 0) <= lanes(square)
    until = until.astype(jnp.bfloat16)
    slot = lax.broadcasted_iota(jnp.int32, (slots, count), 0).astype(jnp.float32)
    reads[0].wait()
    reads[1].wait()
    chosen = held_ids[...] == 0
    routed = jnp.max(chosen.astype(jnp.float32), axis=0, keepdims=True)
    weight = jnp.sum(jnp.where(chosen, held_share[...], 0.0), axis=0, keepdims=True)
    before = jnp.dot(
        jnp.broadcast_to(routed, (slots, count)).astype(jnp.bfloat16),
        until,
        preferred_element_type=jnp.float32,
    )
    place = jnp.where((before - 1.0 == slot) & (routed > 0.0), 1.0, 0.0)
    slot_weight = jnp.sum(place * weight, axis=1, keepdims=True)
    chooser[...] = place.astype(jnp.bfloat16)
    weights[...] = jnp.broadcast_to(slot_weight, weights.shape)
    writes = [
        pltpu.make_async_copy(chooser, chooser_ref, own_sems.at[0]),
        pltpu.make_async_copy(weights, slot_weight_ref, own_sems.at[1]),
    ]
    for write in writes:
        write.start()
    for part, held in enumerate((held_tokens, held_cot)):
        reads[2 + part].wait()
        rows = jnp.dot(chooser[...], held[...], preferred_element_type=jnp.float32)
        both[part] = (rows * slot_weight if part else rows).astype(jnp.bfloat16)
        for k in range(peers):
            writes.append(
                pltpu.make_async_copy(
                    both.at[part],
                    copies_ref.at[k, pl.ds(part * slots, slots), :],
                    out_sems.at[part, k],
                )
            )
            writes[-1].start()
    for write in writes:
        write.wait()


def route(ids, share, tokens, cot, peers):
    count, width = tokens.shape
    slots = count // 8
    top = ids.shape[1]
    return pl.pallas_call(
        route_kernel,
        out_shape=(
            jax.ShapeDtypeStruct((peers, 2 * slots, width), jnp.bfloat16),
            jax.ShapeDtypeStruct((slots, count), jnp.bfloat16),
            jax.ShapeDtypeStruct((slots, 128), jnp.float32),
        ),
        in_specs=[HBM] * 4,
        out_specs=(HBM,) * 3,
        scratch_shapes=[
            pltpu.VMEM((top, count), jnp.int32),
            pltpu.VMEM((top, count), jnp.float32),
            pltpu.VMEM((count, width), jnp.bfloat16),
            pltpu.VMEM((count, width), jnp.bfloat16),
            pltpu.VMEM((2, slots, width), jnp.bfloat16),
            pltpu.VMEM((slots, count), jnp.bfloat16),
            pltpu.VMEM((slots, 128), jnp.float32),
            pltpu.SemaphoreType.DMA((4,)),
            pltpu.SemaphoreType.DMA((2, peers)),
            pltpu.SemaphoreType.DMA((2,)),
        ],
        compiler_params=params(56),
        name="route",
    )(ids.T, share.T, tokens, cot)


def pack_kernel(own_ref, got_ref, packed_ref):
    rows, width = own_ref.shape[1:]
    low = lanes((rows, width)) < width // 2
    top = lax.axis_index("y") == 0

    def half_of(left, right):
        left, right = left.astype(jnp.float32), right.astype(jnp.float32)
        if_top = jnp.where(low, left, halves_swapped(right))
        return jnp.where(top, if_top, jnp.where(low, halves_swapped(left), right)).astype(jnp.bfloat16)

    mine = half_of(own_ref[0], own_ref[1])
    got = half_of(got_ref[0], got_ref[1])
    packed_ref[:rows, :] = jnp.where(top, mine, got)
    packed_ref[rows : 2 * rows, :] = jnp.where(top, got, mine)
    packed_ref[2 * rows : 3 * rows, :] = jnp.where(top, own_ref[2], got_ref[2])
    packed_ref[3 * rows :, :] = jnp.where(top, got_ref[2], own_ref[2])


def pack_shards(own, got):
    _, rows, width = own.shape
    return pl.pallas_call(
        pack_kernel,
        out_shape=jax.ShapeDtypeStruct((4 * rows, width), own.dtype),
        in_specs=whole(2),
        out_specs=whole(1)[0],
        compiler_params=params(2),
        name="pack_shards",
    )(own, got)


def forward_kernel(
    both_ref, own_ref, got_ref, hidden_send_ref, hidden_keep_ref, acts_ref, down, gate_up, hiddens
):
    chips, rows, width = own_ref.shape
    rows = rows // 4
    half = width // 2
    peers, slots = both_ref.shape[0], both_ref.shape[1] // 2
    y, c = lax.axis_index("y"), lax.axis_index("c")
    for core, ref in ((c, own_ref), (1 - c, got_ref)):
        for chip in range(chips):
            for k in range(2):
                at = pl.multiple_of((chip * 2 + k) * 2 * rows + core * rows, rows)
                gate_up[pl.ds(at, rows), :] = ref[chip, k * rows : (k + 1) * rows, :]
                down[pl.ds(at, rows), :] = ref[chip, (2 + k) * rows : (3 + k) * rows, :]
    total = peers * slots
    picked = both_ref[:, :slots, :].reshape(total, both_ref.shape[2])
    acts = jnp.dot(picked, gate_up[...], preferred_element_type=jnp.float32)
    acts_ref[...] = acts
    gate, up, _ = gate_and_up(acts)
    hidden = gate * jax.nn.sigmoid(gate) * up
    mine = (lanes(acts.shape) >= half) == (y == 1)
    hiddens[...] = jnp.where(mine, hidden, 0.0)
    group_rows = total // 2
    hidden_send_ref[...] = hiddens[pl.ds((1 - y) * group_rows, group_rows), :].astype(jnp.bfloat16)
    hidden_keep_ref[...] = hiddens[pl.ds(y * group_rows, group_rows), :].astype(jnp.bfloat16)


def gate_and_up(acts):
    half = acts.shape[1] // 2
    turned = pltpu.roll(acts, half, 1)
    low = lanes(acts.shape) < half
    return jnp.where(low, acts, turned), jnp.where(low, turned, acts), low


def forward(both, own, got):
    peers, doubled, depth = both.shape
    rows = peers * doubled // 2
    width = own.shape[2]
    hidden = jax.ShapeDtypeStruct((rows // 2, width), jnp.bfloat16)
    return pl.pallas_call(
        forward_kernel,
        out_shape=(
            hidden,
            hidden,
            jax.ShapeDtypeStruct((rows, width), jnp.float32),
            jax.ShapeDtypeStruct((depth, width), jnp.bfloat16),
        ),
        in_specs=whole(3),
        out_specs=tuple(whole(4)),
        scratch_shapes=[
            pltpu.VMEM((depth, width), jnp.bfloat16),
            pltpu.VMEM((rows, width), jnp.float32),
        ],
        compiler_params=params(12),
        name="forward",
    )(both, own, got)


def backward_kernel(join_ref, both_ref, acts_ref, down, send_ref, keep_ref, terms):
    peers, slots = both_ref.shape[0], both_ref.shape[1] // 2
    depth = both_ref.shape[2]
    total, width = acts_ref.shape
    half = width // 2
    chips = send_ref.shape[0] * send_ref.shape[1]
    rows = send_ref.shape[3] // 3 * 2
    z, y, c = lax.axis_index(Z), lax.axis_index("y"), lax.axis_index("c")
    picked = both_ref[:, :slots, :].reshape(total, depth)
    dpicked = both_ref[:, slots:, :].reshape(total, depth)
    gate, up, low = gate_and_up(acts_ref[...])
    sigma = jax.nn.sigmoid(gate)
    hidden = gate * sigma * up
    mine = (lanes(gate.shape) >= half) == (y == 1)
    dhidden = jnp.dot(dpicked, down[...], preferred_element_type=jnp.float32)
    dhidden = jnp.where(mine, dhidden, pltpu.roll(dhidden, half, 1))
    dgate = dhidden * up * sigma * (1.0 + gate * (1.0 - sigma))
    dup = dhidden * gate * sigma
    first = 1.0 - join_ref[(z * 2 + 0) * 2 + c].astype(jnp.float32)
    second = 1.0 - join_ref[(z * 2 + 1) * 2 + c].astype(jnp.float32)
    group = lax.broadcasted_iota(jnp.int32, gate.shape, 0) // (total // 2)
    active = jnp.where(group == 0, first, second)
    dacts = (jnp.where(low, dgate, dup) * active).astype(jnp.bfloat16)
    counted = (hidden.astype(jnp.bfloat16).astype(jnp.float32) * active).astype(jnp.bfloat16)
    terms[0] = lax.dot_general(picked, dacts, ROW_DIMS, preferred_element_type=jnp.float32)
    terms[1] = lax.dot_general(dpicked, counted, ROW_DIMS, preferred_element_type=jnp.float32)
    half_rows = rows // 2
    low = lanes((half_rows, width)) < half
    for chip in range(chips):
        for k in range(2):
            base = (chip * 2 + k) * 2 * rows
            away = jnp.bitwise_xor(chip % 2, lax.rem(z, 2)) * 2
            away += jnp.bitwise_xor(chip // 2 % 2, lax.rem(z // 2, 2))
            for which, ref in ((c, keep_ref), (1 - c, send_ref)):
                at = pl.multiple_of(base + which * rows, rows)
                ref[away, chip // 4, k, :rows, :] = terms[0, pl.ds(at, rows), :].astype(ref.dtype)
                packed = jnp.where(
                    low,
                    terms[1, pl.ds(at, half_rows), :],
                    terms[1, pl.ds(at + half_rows, half_rows), :],
                )
                ref[away, chip // 4, k, rows:, :] = packed.astype(ref.dtype)


def backward(join, both, acts, down, chips):
    depth, width = down.shape
    rows = depth // chips // 4
    chunk = (4, chips // 4, 2, rows // 2 * 3, width)
    return pl.pallas_call(
        backward_kernel,
        out_shape=(
            jax.ShapeDtypeStruct(chunk, jnp.bfloat16),
            jax.ShapeDtypeStruct(chunk, jnp.float32),
        ),
        in_specs=[pl.BlockSpec(memory_space=pltpu.SMEM), *whole(3)],
        out_specs=tuple(whole(2)),
        scratch_shapes=[pltpu.VMEM((2, depth, width), jnp.float32)],
        compiler_params=params(16),
        cost_estimate=cost(0.5),
        name="backward",
    )(join, both, acts, down)


def partial_kernel(keep_ref, got_ref, down_ref, mine_ref, theirs_ref, partials):
    partial = lax.dot_general(
        keep_ref[...] + got_ref[...], down_ref[...], LANE_DIMS, preferred_element_type=jnp.float32
    )
    partials[...] = partial.reshape(partials.shape)
    h, x = lax.axis_index("h"), lax.axis_index("x")
    for high, ref in enumerate((mine_ref, theirs_ref)):
        for low in range(2):
            for row in range(2):
                peer = jnp.bitwise_xor(h, row) * 4 + jnp.bitwise_xor(x, 2 * high + low)
                ref[2 * low + row] = partials[peer].astype(ref.dtype)


def partial_rows(keep, got, down, peers):
    slots, depth = keep.shape[0] // peers, down.shape[0]
    return pl.pallas_call(
        partial_kernel,
        out_shape=(
            jax.ShapeDtypeStruct((peers // 2, slots, depth), jnp.float32),
            jax.ShapeDtypeStruct((peers // 2, slots, depth), jnp.bfloat16),
        ),
        in_specs=whole(3),
        out_specs=tuple(whole(2)),
        scratch_shapes=[pltpu.VMEM((peers, slots, depth), jnp.float32)],
        compiler_params=params(8),
        cost_estimate=cost(0.5),
        name="partial_rows",
    )(keep, got, down)


def add_kernel(keep_ref, got_ref, mine_ref, theirs_ref):
    half = mine_ref.shape[0]
    mine_ref[...] = keep_ref[:half] + got_ref[:half].astype(jnp.float32)
    theirs_ref[...] = (keep_ref[half:] + got_ref[half:].astype(jnp.float32)).astype(jnp.bfloat16)


def add_halves(keep, got):
    half = (keep.shape[0] // 2, *keep.shape[1:])
    return pl.pallas_call(
        add_kernel,
        out_shape=(
            jax.ShapeDtypeStruct(half, jnp.float32),
            jax.ShapeDtypeStruct(half, jnp.bfloat16),
        ),
        in_specs=whole(2),
        out_specs=tuple(whole(2)),
        compiler_params=params(8),
        cost_estimate=cost(0.5),
        name="add_halves",
    )(keep, got)


def mix_kernel(own_ref, got_ref, chooser_ref, slot_weight_ref, mixed_ref):
    total = own_ref[0] + got_ref[0].astype(jnp.float32)
    weighted = (total * slot_weight_ref[:, :1]).astype(jnp.bfloat16)
    mixed_ref[...] = lax.dot_general(
        chooser_ref[...], weighted, ROW_DIMS, preferred_element_type=jnp.float32
    ).astype(jnp.bfloat16)


def mix(own, got, chooser, slot_weight):
    return pl.pallas_call(
        mix_kernel,
        out_shape=jax.ShapeDtypeStruct((chooser.shape[1], own.shape[2]), jnp.bfloat16),
        in_specs=whole(4),
        out_specs=whole(1)[0],
        compiler_params=params(8),
        cost_estimate=cost(0.5),
        name="mix",
    )(own, got, chooser, slot_weight)


def finish_kernel(blocks_ref, gate_ref, up_ref, down_ref):
    rows, width = gate_ref.shape
    half = width // 2
    sums = [blocks_ref[y].astype(jnp.float32) for y in range(2)]
    for k in range(2, blocks_ref.shape[0], 2):
        for y in range(2):
            sums[y] += blocks_ref[k + y].astype(jnp.float32)
    low = lanes(sums[0].shape) < half
    firsts = jnp.where(low, sums[0], pltpu.roll(sums[1], half, 1)).astype(jnp.bfloat16)
    seconds = jnp.where(low, pltpu.roll(sums[0], half, 1), sums[1]).astype(jnp.bfloat16)
    gate_ref[...] = firsts[:rows]
    up_ref[...] = seconds[:rows]
    down_ref[: rows // 2, :] = firsts[rows:]
    down_ref[rows // 2 :, :] = seconds[rows:]


def finish(blocks):
    _, packed_rows, width = blocks.shape
    shape = jax.ShapeDtypeStruct((packed_rows // 3 * 2, width), jnp.bfloat16)
    return pl.pallas_call(
        finish_kernel,
        out_shape=(shape,) * 3,
        in_specs=whole(1),
        out_specs=tuple(whole(3)),
        compiler_params=params(4),
        name="finish",
    )(blocks)


def swapped(part, axis, distance=1):
    size = lax.axis_size(axis)
    return lax.ppermute(part, axis, [(i, i ^ distance) for i in range(size)])


def per_device(tokens, cotangent, expert_ids, route_weights, join_groups, w_gate, w_up, w_down):
    own = jnp.stack([w_gate, w_up, w_down])
    got = swapped(own, "y")
    copies, chooser, slot_weight = route(
        expert_ids, route_weights, tokens, cotangent, lax.axis_size(PLANE)
    )
    packed = pack_shards(own, got)
    packed, copies = lax.optimization_barrier((packed, copies))
    rows_in = lax.all_to_all(copies, PLANE, 0, 0, tiled=True)
    along = lax.all_gather(packed, Z, axis=0, tiled=False)
    along, rows_in = lax.optimization_barrier((along, rows_in))
    other = swapped(along, "c")
    hidden_send, hidden, acts, down = forward(rows_in, along, other)
    hidden_got = swapped(hidden_send, "y")
    send, keep = backward(join_groups, rows_in, acts, down, lax.axis_size(Z))
    from_core = swapped(send, "c")
    partial, partial_send = partial_rows(hidden, hidden_got, down, lax.axis_size(("h", "x")))
    partial_got = swapped(partial_send, "x", 2)
    keep, to_pair = add_halves(keep, from_core)
    from_pair = swapped(to_pair, "zl")
    from_pair, _ = lax.optimization_barrier((from_pair, partial_send))
    keep, to_far = add_halves(keep, from_pair)
    from_far = swapped(to_far, "zm")
    pair_sum = (keep + from_far.astype(jnp.float32)).astype(jnp.bfloat16)
    pair_sum = pair_sum.reshape(-1, *pair_sum.shape[3:])
    pieces = lax.all_to_all(pair_sum, ("zh", "y"), 0, 0, tiled=True)
    partial, partial_send = add_halves(partial, partial_got)
    partial, partial_send = add_halves(partial, swapped(partial_send, "x"))
    mixed = mix(partial, swapped(partial_send, "h"), chooser, slot_weight)
    return (mixed, *finish(pieces))


def solution(mesh):
    experts = mesh.shape["expert"]
    split = Mesh(mesh.devices.reshape(-1, 2, 2, 2, 2, 2, experts // 2), AXES)
    dp = (*Z, "y", "c")
    tok, weight = P(AXES, None), P(dp, ("h", "x"))
    return jax.shard_map(
        per_device,
        mesh=split,
        in_specs=(tok, tok, tok, tok, P(), weight, weight, weight),
        out_specs=(tok, weight, weight, weight),
        check_vma=False,
    )
```

```python
import jax
import jax.numpy as jnp
from jax import lax
from jax.experimental import pallas as pl
from jax.experimental.pallas import tpu as pltpu
from jax.sharding import Mesh
from jax.sharding import PartitionSpec as P

AXES = ("zh", "zl", "y", "c", "h", "x")
Z = ("zh", "zl")
PLANE = ("y", "h", "x")
HBM = pl.BlockSpec(memory_space=pltpu.HBM)
ROW_DIMS = (((0,), (0,)), ((), ()))
LANE_DIMS = (((1,), (1,)), ((), ()))


def whole(n):
    return [pl.BlockSpec(memory_space=pltpu.VMEM) for _ in range(n)]


def lanes(shape):
    return lax.broadcasted_iota(jnp.int32, shape, 1)


def halves_swapped(a):
    half = a.shape[1] // 2
    return pltpu.roll(a.astype(jnp.float32), half, 1)


def params(mib):
    return pltpu.CompilerParams(vmem_limit_bytes=mib * 1024 * 1024)


def cost(microseconds):
    return pl.CostEstimate(flops=int(1.1e9 * microseconds), transcendentals=0, bytes_accessed=int(3.7e6 * microseconds))


def route_kernel(
    ids_ref, share_ref, tokens_ref, cot_ref, copies_ref, chooser_ref, slot_weight_ref,
    held_ids, held_share, held_tokens, held_cot, both, chooser, weights, in_sems, out_sems, own_sems,
):
    count = ids_ref.shape[1]
    slots = chooser_ref.shape[0]
    peers = copies_ref.shape[0]
    pairs = (
        (ids_ref, held_ids), (share_ref, held_share), (tokens_ref, held_tokens), (cot_ref, held_cot)
    )
    reads = [
        pltpu.make_async_copy(src, dst, in_sems.at[k]) for k, (src, dst) in enumerate(pairs)
    ]
    for read in reads:
        read.start()
    square = (count, count)
    until = lax.broadcasted_iota(jnp.int32, square, 0) <= lanes(square)
    until = until.astype(jnp.bfloat16)
    slot = lax.broadcasted_iota(jnp.int32, (slots, count), 0).astype(jnp.float32)
    reads[0].wait()
    reads[1].wait()
    chosen = held_ids[...] == 0
    routed = jnp.max(chosen.astype(jnp.float32), axis=0, keepdims=True)
    weight = jnp.sum(jnp.where(chosen, held_share[...], 0.0), axis=0, keepdims=True)
    before = jnp.dot(
        jnp.broadcast_to(routed, (slots, count)).astype(jnp.bfloat16),
        until,
        preferred_element_type=jnp.float32,
    )
    place = jnp.where((before - 1.0 == slot) & (routed > 0.0), 1.0, 0.0)
    slot_weight = jnp.sum(place * weight, axis=1, keepdims=True)
    chooser[...] = place.astype(jnp.bfloat16)
    weights[...] = jnp.broadcast_to(slot_weight, weights.shape)
    writes = [
        pltpu.make_async_copy(chooser, chooser_ref, own_sems.at[0]),
        pltpu.make_async_copy(weights, slot_weight_ref, own_sems.at[1]),
    ]
    for write in writes:
        write.start()
    for part, held in enumerate((held_tokens, held_cot)):
        reads[2 + part].wait()
        rows = jnp.dot(chooser[...], held[...], preferred_element_type=jnp.float32)
        both[part] = (rows * slot_weight if part else rows).astype(jnp.bfloat16)
        for k in range(peers):
            writes.append(
                pltpu.make_async_copy(
                    both.at[part],
                    copies_ref.at[k, pl.ds(part * slots, slots), :],
                    out_sems.at[part, k],
                )
            )
            writes[-1].start()
    for write in writes:
        write.wait()


def route(ids, share, tokens, cot, peers):
    count, width = tokens.shape
    slots = count // 8
    top = ids.shape[1]
    return pl.pallas_call(
        route_kernel,
        out_shape=(
            jax.ShapeDtypeStruct((peers, 2 * slots, width), jnp.bfloat16),
            jax.ShapeDtypeStruct((slots, count), jnp.bfloat16),
            jax.ShapeDtypeStruct((slots, 128), jnp.float32),
        ),
        in_specs=[HBM] * 4,
        out_specs=(HBM,) * 3,
        scratch_shapes=[
            pltpu.VMEM((top, count), jnp.int32),
            pltpu.VMEM((top, count), jnp.float32),
            pltpu.VMEM((count, width), jnp.bfloat16),
            pltpu.VMEM((count, width), jnp.bfloat16),
            pltpu.VMEM((2, slots, width), jnp.bfloat16),
            pltpu.VMEM((slots, count), jnp.bfloat16),
            pltpu.VMEM((slots, 128), jnp.float32),
            pltpu.SemaphoreType.DMA((4,)),
            pltpu.SemaphoreType.DMA((2, peers)),
            pltpu.SemaphoreType.DMA((2,)),
        ],
        compiler_params=params(56),
        name="route",
    )(ids.T, share.T, tokens, cot)


def pack_kernel(own_ref, got_ref, packed_ref):
    rows, width = own_ref.shape[1:]
    low = lanes((rows, width)) < width // 2
    top = lax.axis_index("y") == 0

    def halves_of(ref):
        left, right = ref[0].astype(jnp.float32), ref[1].astype(jnp.float32)
        firsts = jnp.where(low, left, halves_swapped(right)).astype(jnp.bfloat16)
        seconds = jnp.where(low, halves_swapped(left), right).astype(jnp.bfloat16)
        return jnp.where(top, firsts, seconds), jnp.where(top, seconds, firsts)

    for k, (own, got) in enumerate(
        (*zip(halves_of(own_ref), halves_of(got_ref), strict=True), (own_ref[2], got_ref[2]))
    ):
        at = 2 * k * rows
        packed_ref[at : at + rows, :] = jnp.where(top, own, got)
        packed_ref[at + rows : at + 2 * rows, :] = jnp.where(top, got, own)


def pack_shards(own, got):
    _, rows, width = own.shape
    return pl.pallas_call(
        pack_kernel,
        out_shape=jax.ShapeDtypeStruct((6 * rows, width), own.dtype),
        in_specs=whole(2),
        out_specs=whole(1)[0],
        compiler_params=params(2),
        name="pack_shards",
    )(own, got)


def forward_kernel(
    both_ref, own_ref, got_ref, mine_ref, theirs_ref, acts_ref, down, gate_up, others, hiddens, partials
):
    chips, rows, width = own_ref.shape
    rows = rows // 6
    half = width // 2
    peers, slots = both_ref.shape[0], both_ref.shape[1] // 2
    depth = both_ref.shape[2]
    y, c = lax.axis_index("y"), lax.axis_index("c")
    for core, ref in ((c, own_ref), (1 - c, got_ref)):
        for chip in range(chips):
            for k in range(2):
                at = pl.multiple_of((chip * 2 + k) * 2 * rows + core * rows, rows)
                for part, target in enumerate((gate_up, others, down)):
                    first = (2 * part + k) * rows
                    target[pl.ds(at, rows), :] = ref[chip, first : first + rows, :]
    total = peers * slots
    picked = both_ref[:, :slots, :].reshape(total, depth)
    acts = jnp.dot(picked, gate_up[...], preferred_element_type=jnp.float32)
    acts_ref[...] = acts
    gate, up, _ = gate_and_up(acts)
    hiddens[...] = gate * jax.nn.sigmoid(gate) * up
    group_rows = total // 2
    group = both_ref[pl.ds(y * (peers // 2), peers // 2), :slots, :].reshape(group_rows, depth)
    gate, up, _ = gate_and_up(jnp.dot(group, others[...], preferred_element_type=jnp.float32))
    hidden = gate * jax.nn.sigmoid(gate) * up
    mine = (lanes(hidden.shape) >= half) == (y == 1)
    hidden = jnp.where(mine, hiddens[pl.ds(y * group_rows, group_rows), :], hidden)
    partial = lax.dot_general(
        hidden.astype(jnp.bfloat16), down[...], LANE_DIMS, preferred_element_type=jnp.float32
    )
    partials[...] = partial.reshape(partials.shape)
    h, x = lax.axis_index("h"), lax.axis_index("x")
    for high, ref in enumerate((mine_ref, theirs_ref)):
        for low in range(2):
            for row in range(2):
                peer = jnp.bitwise_xor(h, row) * 4 + jnp.bitwise_xor(x, 2 * high + low)
                ref[2 * low + row] = partials[peer].astype(ref.dtype)


def gate_and_up(acts):
    half = acts.shape[1] // 2
    turned = pltpu.roll(acts, half, 1)
    low = lanes(acts.shape) < half
    return jnp.where(low, acts, turned), jnp.where(low, turned, acts), low


def forward(both, own, got):
    peers, doubled, depth = both.shape
    slots = doubled // 2
    rows = peers * slots
    width = own.shape[2]
    return pl.pallas_call(
        forward_kernel,
        out_shape=(
            jax.ShapeDtypeStruct((peers // 4, slots, depth), jnp.float32),
            jax.ShapeDtypeStruct((peers // 4, slots, depth), jnp.bfloat16),
            jax.ShapeDtypeStruct((rows, width), jnp.float32),
            jax.ShapeDtypeStruct((depth, width), jnp.bfloat16),
        ),
        in_specs=whole(3),
        out_specs=tuple(whole(4)),
        scratch_shapes=[
            pltpu.VMEM((depth, width), jnp.bfloat16),
            pltpu.VMEM((depth, width), jnp.bfloat16),
            pltpu.VMEM((rows, width), jnp.float32),
            pltpu.VMEM((peers // 2, slots, depth), jnp.float32),
        ],
        compiler_params=params(16),
        name="forward",
    )(both, own, got)


def backward_kernel(join_ref, both_ref, acts_ref, down, send_ref, keep_ref, terms):
    peers, slots = both_ref.shape[0], both_ref.shape[1] // 2
    depth = both_ref.shape[2]
    total, width = acts_ref.shape
    half = width // 2
    chips = send_ref.shape[0] * send_ref.shape[1]
    rows = send_ref.shape[3] // 3 * 2
    z, y, c = lax.axis_index(Z), lax.axis_index("y"), lax.axis_index("c")
    picked = both_ref[:, :slots, :].reshape(total, depth)
    dpicked = both_ref[:, slots:, :].reshape(total, depth)
    gate, up, low = gate_and_up(acts_ref[...])
    sigma = jax.nn.sigmoid(gate)
    hidden = gate * sigma * up
    mine = (lanes(gate.shape) >= half) == (y == 1)
    dhidden = jnp.dot(dpicked, down[...], preferred_element_type=jnp.float32)
    dhidden = jnp.where(mine, dhidden, pltpu.roll(dhidden, half, 1))
    dgate = dhidden * up * sigma * (1.0 + gate * (1.0 - sigma))
    dup = dhidden * gate * sigma
    first = 1.0 - join_ref[(z * 2 + 0) * 2 + c].astype(jnp.float32)
    second = 1.0 - join_ref[(z * 2 + 1) * 2 + c].astype(jnp.float32)
    group = lax.broadcasted_iota(jnp.int32, gate.shape, 0) // (total // 2)
    active = jnp.where(group == 0, first, second)
    dacts = (jnp.where(low, dgate, dup) * active).astype(jnp.bfloat16)
    counted = (hidden.astype(jnp.bfloat16).astype(jnp.float32) * active).astype(jnp.bfloat16)
    terms[0] = lax.dot_general(picked, dacts, ROW_DIMS, preferred_element_type=jnp.float32)
    terms[1] = lax.dot_general(dpicked, counted, ROW_DIMS, preferred_element_type=jnp.float32)
    half_rows = rows // 2
    low = lanes((half_rows, width)) < half
    for chip in range(chips):
        for k in range(2):
            base = (chip * 2 + k) * 2 * rows
            away = jnp.bitwise_xor(chip % 2, lax.rem(z, 2))
            for which, ref in ((c, keep_ref), (1 - c, send_ref)):
                at = pl.multiple_of(base + which * rows, rows)
                ref[away, chip // 2, k, :rows, :] = terms[0, pl.ds(at, rows), :].astype(ref.dtype)
                packed = jnp.where(
                    low,
                    terms[1, pl.ds(at, half_rows), :],
                    terms[1, pl.ds(at + half_rows, half_rows), :],
                )
                ref[away, chip // 2, k, rows:, :] = packed.astype(ref.dtype)


def backward(join, both, acts, down, chips):
    depth, width = down.shape
    rows = depth // chips // 4
    chunk = (2, chips // 2, 2, rows // 2 * 3, width)
    return pl.pallas_call(
        backward_kernel,
        out_shape=(
            jax.ShapeDtypeStruct(chunk, jnp.bfloat16),
            jax.ShapeDtypeStruct(chunk, jnp.float32),
        ),
        in_specs=[pl.BlockSpec(memory_space=pltpu.SMEM), *whole(3)],
        out_specs=tuple(whole(2)),
        scratch_shapes=[pltpu.VMEM((2, depth, width), jnp.float32)],
        compiler_params=params(16),
        cost_estimate=cost(8),
        name="backward",
    )(join, both, acts, down)


def add_kernel(keep_ref, got_ref, mine_ref, theirs_ref):
    half = mine_ref.shape[0]
    mine_ref[...] = keep_ref[:half] + got_ref[:half].astype(jnp.float32)
    theirs_ref[...] = (keep_ref[half:] + got_ref[half:].astype(jnp.float32)).astype(jnp.bfloat16)


def add_halves(keep, got, lasts):
    half = (keep.shape[0] // 2, *keep.shape[1:])
    return pl.pallas_call(
        add_kernel,
        out_shape=(
            jax.ShapeDtypeStruct(half, jnp.float32),
            jax.ShapeDtypeStruct(half, jnp.bfloat16),
        ),
        in_specs=whole(2),
        out_specs=tuple(whole(2)),
        compiler_params=params(8),
        cost_estimate=cost(lasts),
        name="add_halves",
    )(keep, got)


def mix_kernel(own_ref, got_ref, chooser_ref, slot_weight_ref, mixed_ref):
    total = own_ref[0] + got_ref[0].astype(jnp.float32)
    weighted = (total * slot_weight_ref[:, :1]).astype(jnp.bfloat16)
    mixed_ref[...] = lax.dot_general(
        chooser_ref[...], weighted, ROW_DIMS, preferred_element_type=jnp.float32
    ).astype(jnp.bfloat16)


def mix(own, got, chooser, slot_weight):
    return pl.pallas_call(
        mix_kernel,
        out_shape=jax.ShapeDtypeStruct((chooser.shape[1], own.shape[2]), jnp.bfloat16),
        in_specs=whole(4),
        out_specs=whole(1)[0],
        compiler_params=params(8),
        cost_estimate=cost(1),
        name="mix",
    )(own, got, chooser, slot_weight)


def finish_kernel(blocks_ref, gate_ref, up_ref, down_ref):
    rows, width = gate_ref.shape
    half = width // 2
    sums = [blocks_ref[y].astype(jnp.float32) for y in range(2)]
    for k in range(2, blocks_ref.shape[0], 2):
        for y in range(2):
            sums[y] += blocks_ref[k + y].astype(jnp.float32)
    low = lanes(sums[0].shape) < half
    firsts = jnp.where(low, sums[0], pltpu.roll(sums[1], half, 1)).astype(jnp.bfloat16)
    seconds = jnp.where(low, pltpu.roll(sums[0], half, 1), sums[1]).astype(jnp.bfloat16)
    gate_ref[...] = firsts[:rows]
    up_ref[...] = seconds[:rows]
    down_ref[: rows // 2, :] = firsts[rows:]
    down_ref[rows // 2 :, :] = seconds[rows:]


def finish(blocks):
    _, packed_rows, width = blocks.shape
    shape = jax.ShapeDtypeStruct((packed_rows // 3 * 2, width), jnp.bfloat16)
    return pl.pallas_call(
        finish_kernel,
        out_shape=(shape,) * 3,
        in_specs=whole(1),
        out_specs=tuple(whole(3)),
        compiler_params=params(4),
        name="finish",
    )(blocks)


def swapped(part, axis, distance=1):
    size = lax.axis_size(axis)
    return lax.ppermute(part, axis, [(i, i ^ distance) for i in range(size)])


def per_device(tokens, cotangent, expert_ids, route_weights, join_groups, w_gate, w_up, w_down):
    own = jnp.stack([w_gate, w_up, w_down])
    got = swapped(own, "y")
    copies, chooser, slot_weight = route(
        expert_ids, route_weights, tokens, cotangent, lax.axis_size(PLANE)
    )
    packed = pack_shards(own, got)
    packed, copies = lax.optimization_barrier((packed, copies))
    rows_in = lax.all_to_all(copies, PLANE, 0, 0, tiled=True)
    along = lax.all_gather(packed, Z, axis=0, tiled=False)
    along, rows_in = lax.optimization_barrier((along, rows_in))
    other = swapped(along, "c")
    partial, partial_send, acts, down = forward(rows_in, along, other)
    partial_got = swapped(partial_send, "x", 2)
    send, keep = backward(join_groups, rows_in, acts, down, lax.axis_size(Z))
    keep, to_pair = add_halves(keep, swapped(send, "c"), 0.4)
    from_pair = swapped(to_pair, "zl")
    pair_sum = (keep + from_pair.astype(jnp.float32)).astype(jnp.bfloat16)
    pair_sum = pair_sum.reshape(-1, *pair_sum.shape[3:])
    pieces = lax.all_to_all(pair_sum, ("zh", "y"), 0, 0, tiled=True)
    partial, partial_send = add_halves(partial, partial_got, 2)
    partial, partial_send = add_halves(partial, swapped(partial_send, "x"), 1)
    mixed = mix(partial, swapped(partial_send, "h"), chooser, slot_weight)
    return (mixed, *finish(pieces))


def solution(mesh):
    experts = mesh.shape["expert"]
    split = Mesh(mesh.devices.reshape(-1, 2, 2, 2, 2, experts // 2), AXES)
    dp = ("zh", "zl", "y", "c")
    tok, weight = P(AXES, None), P(dp, ("h", "x"))
    return jax.shard_map(
        per_device,
        mesh=split,
        in_specs=(tok, tok, tok, tok, P(), weight, weight, weight),
        out_specs=(tok, weight, weight, weight),
        check_vma=False,
    )
```

```python
import jax
import jax.numpy as jnp
from jax import lax
from jax.experimental import pallas as pl
from jax.experimental.pallas import tpu as pltpu
from jax.sharding import Mesh
from jax.sharding import PartitionSpec as P

AXES = ("zh", "zl", "y", "c", "h", "x")
Z = ("zh", "zl")
PLANE = ("y", "h", "x")
HBM = pl.BlockSpec(memory_space=pltpu.HBM)
ROW_DIMS = (((0,), (0,)), ((), ()))
LANE_DIMS = (((1,), (1,)), ((), ()))


def whole(n):
    return [pl.BlockSpec(memory_space=pltpu.VMEM) for _ in range(n)]


def lanes(shape):
    return lax.broadcasted_iota(jnp.int32, shape, 1)


def halves_swapped(a):
    half = a.shape[1] // 2
    return pltpu.roll(a.astype(jnp.float32), half, 1)


def params(mib):
    return pltpu.CompilerParams(vmem_limit_bytes=mib * 1024 * 1024)


def cost(microseconds):
    return pl.CostEstimate(flops=int(1.1e9 * microseconds), transcendentals=0, bytes_accessed=int(3.7e6 * microseconds))


def route_kernel(
    ids_ref, share_ref, tokens_ref, cot_ref, copies_ref, chooser_ref, slot_weight_ref,
    held_ids, held_share, held_tokens, held_cot, both, chooser, weights, in_sems, out_sems, own_sems,
):
    count = ids_ref.shape[1]
    slots = chooser_ref.shape[0]
    peers = copies_ref.shape[0]
    pairs = (
        (ids_ref, held_ids), (share_ref, held_share), (tokens_ref, held_tokens), (cot_ref, held_cot)
    )
    reads = [
        pltpu.make_async_copy(src, dst, in_sems.at[k]) for k, (src, dst) in enumerate(pairs)
    ]
    for read in reads:
        read.start()
    square = (count, count)
    until = lax.broadcasted_iota(jnp.int32, square, 0) <= lanes(square)
    until = until.astype(jnp.bfloat16)
    slot = lax.broadcasted_iota(jnp.int32, (slots, count), 0).astype(jnp.float32)
    reads[0].wait()
    reads[1].wait()
    chosen = held_ids[...] == 0
    routed = jnp.max(chosen.astype(jnp.float32), axis=0, keepdims=True)
    weight = jnp.sum(jnp.where(chosen, held_share[...], 0.0), axis=0, keepdims=True)
    before = jnp.dot(
        jnp.broadcast_to(routed, (slots, count)).astype(jnp.bfloat16),
        until,
        preferred_element_type=jnp.float32,
    )
    place = jnp.where((before - 1.0 == slot) & (routed > 0.0), 1.0, 0.0)
    slot_weight = jnp.sum(place * weight, axis=1, keepdims=True)
    chooser[...] = place.astype(jnp.bfloat16)
    weights[...] = jnp.broadcast_to(slot_weight, weights.shape)
    writes = [
        pltpu.make_async_copy(chooser, chooser_ref, own_sems.at[0]),
        pltpu.make_async_copy(weights, slot_weight_ref, own_sems.at[1]),
    ]
    for write in writes:
        write.start()
    for part, held in enumerate((held_tokens, held_cot)):
        reads[2 + part].wait()
        rows = jnp.dot(chooser[...], held[...], preferred_element_type=jnp.float32)
        both[part] = (rows * slot_weight if part else rows).astype(jnp.bfloat16)
        for k in range(peers):
            writes.append(
                pltpu.make_async_copy(
                    both.at[part],
                    copies_ref.at[k, pl.ds(part * slots, slots), :],
                    out_sems.at[part, k],
                )
            )
            writes[-1].start()
    for write in writes:
        write.wait()


def route(ids, share, tokens, cot, peers):
    count, width = tokens.shape
    slots = count // 8
    top = ids.shape[1]
    return pl.pallas_call(
        route_kernel,
        out_shape=(
            jax.ShapeDtypeStruct((peers, 2 * slots, width), jnp.bfloat16),
            jax.ShapeDtypeStruct((slots, count), jnp.bfloat16),
            jax.ShapeDtypeStruct((slots, 128), jnp.float32),
        ),
        in_specs=[HBM] * 4,
        out_specs=(HBM,) * 3,
        scratch_shapes=[
            pltpu.VMEM((top, count), jnp.int32),
            pltpu.VMEM((top, count), jnp.float32),
            pltpu.VMEM((count, width), jnp.bfloat16),
            pltpu.VMEM((count, width), jnp.bfloat16),
            pltpu.VMEM((2, slots, width), jnp.bfloat16),
            pltpu.VMEM((slots, count), jnp.bfloat16),
            pltpu.VMEM((slots, 128), jnp.float32),
            pltpu.SemaphoreType.DMA((4,)),
            pltpu.SemaphoreType.DMA((2, peers)),
            pltpu.SemaphoreType.DMA((2,)),
        ],
        compiler_params=params(56),
        name="route",
    )(ids.T, share.T, tokens, cot)


def pack_kernel(own_ref, got_ref, packed_ref):
    rows, width = own_ref.shape[1:]
    low = lanes((rows, width)) < width // 2
    top = lax.axis_index("y") == 0

    def halves_of(ref):
        left, right = ref[0].astype(jnp.float32), ref[1].astype(jnp.float32)
        firsts = jnp.where(low, left, halves_swapped(right)).astype(jnp.bfloat16)
        seconds = jnp.where(low, halves_swapped(left), right).astype(jnp.bfloat16)
        return jnp.where(top, firsts, seconds), jnp.where(top, seconds, firsts)

    for k, (own, got) in enumerate(
        (*zip(halves_of(own_ref), halves_of(got_ref), strict=True), (own_ref[2], got_ref[2]))
    ):
        at = 2 * k * rows
        packed_ref[at : at + rows, :] = jnp.where(top, own, got)
        packed_ref[at + rows : at + 2 * rows, :] = jnp.where(top, got, own)


def pack_shards(own, got):
    _, rows, width = own.shape
    return pl.pallas_call(
        pack_kernel,
        out_shape=jax.ShapeDtypeStruct((6 * rows, width), own.dtype),
        in_specs=whole(2),
        out_specs=whole(1)[0],
        compiler_params=params(2),
        name="pack_shards",
    )(own, got)


def lay_out(own_ref, got_ref, part, target):
    chips, rows, _ = own_ref.shape
    rows = rows // 6
    c = lax.axis_index("c")
    for core, ref in ((c, own_ref), (1 - c, got_ref)):
        for chip in range(chips):
            for k in range(2):
                at = pl.multiple_of((chip * 2 + k) * 2 * rows + core * rows, rows)
                first = (2 * part + k) * rows
                target[pl.ds(at, rows), :] = ref[chip, first : first + rows, :]


def forward_kernel(both_ref, own_ref, got_ref, acts_ref, down, gate_up):
    peers, slots = both_ref.shape[0], both_ref.shape[1] // 2
    lay_out(own_ref, got_ref, 0, gate_up)
    lay_out(own_ref, got_ref, 2, down)
    picked = both_ref[:, :slots, :].reshape(peers * slots, both_ref.shape[2])
    acts_ref[...] = jnp.dot(picked, gate_up[...], preferred_element_type=jnp.float32)


def partial_kernel(
    both_ref, own_ref, got_ref, acts_ref, down_ref, mine_ref, theirs_ref, others, partials
):
    group_rows, width = acts_ref.shape[0] // 2, acts_ref.shape[1]
    peers, slots = both_ref.shape[0] // 2, both_ref.shape[1] // 2
    y, h, x = lax.axis_index("y"), lax.axis_index("h"), lax.axis_index("x")
    lay_out(own_ref, got_ref, 1, others)
    group = both_ref[pl.ds(y * peers, peers), :slots, :].reshape(group_rows, both_ref.shape[2])
    theirs = jnp.dot(group, others[...], preferred_element_type=jnp.float32)
    mine = acts_ref[pl.ds(pl.multiple_of(y * group_rows, group_rows), group_rows), :]
    (gate, up, low), (their_gate, their_up, _) = gate_and_up(mine), gate_and_up(theirs)
    here = jnp.logical_not(low) == (y == 1)
    gate, up = jnp.where(here, gate, their_gate), jnp.where(here, up, their_up)
    hidden = (gate * jax.nn.sigmoid(gate) * up).astype(jnp.bfloat16)
    partial = lax.dot_general(
        hidden, down_ref[...], LANE_DIMS, preferred_element_type=jnp.float32
    )
    partials[...] = partial.reshape(partials.shape)
    for high, ref in enumerate((mine_ref, theirs_ref)):
        for low_bit in range(2):
            for row in range(2):
                peer = jnp.bitwise_xor(h, row) * 4 + jnp.bitwise_xor(x, 2 * high + low_bit)
                ref[2 * low_bit + row] = partials[peer].astype(ref.dtype)


def partial_rows(both, own, got, acts, down):
    peers, doubled, depth = both.shape
    peers, slots = peers // 2, doubled // 2
    return pl.pallas_call(
        partial_kernel,
        out_shape=(
            jax.ShapeDtypeStruct((peers // 2, slots, depth), jnp.float32),
            jax.ShapeDtypeStruct((peers // 2, slots, depth), jnp.bfloat16),
        ),
        in_specs=whole(5),
        out_specs=tuple(whole(2)),
        scratch_shapes=[
            pltpu.VMEM(down.shape, jnp.bfloat16),
            pltpu.VMEM((peers, slots, depth), jnp.float32),
        ],
        compiler_params=params(12),
        cost_estimate=cost(4),
        name="partial_rows",
    )(both, own, got, acts, down)


def gate_and_up(acts):
    half = acts.shape[1] // 2
    turned = pltpu.roll(acts, half, 1)
    low = lanes(acts.shape) < half
    return jnp.where(low, acts, turned), jnp.where(low, turned, acts), low


def forward(both, own, got):
    peers, doubled, depth = both.shape
    width = own.shape[2]
    return pl.pallas_call(
        forward_kernel,
        out_shape=(
            jax.ShapeDtypeStruct((peers * doubled // 2, width), jnp.float32),
            jax.ShapeDtypeStruct((depth, width), jnp.bfloat16),
        ),
        in_specs=whole(3),
        out_specs=tuple(whole(2)),
        scratch_shapes=[pltpu.VMEM((depth, width), jnp.bfloat16)],
        compiler_params=params(12),
        name="forward",
    )(both, own, got)


def backward_kernel(join_ref, both_ref, acts_ref, down, send_ref, keep_ref, terms):
    peers, slots = both_ref.shape[0], both_ref.shape[1] // 2
    depth = both_ref.shape[2]
    total, width = acts_ref.shape
    half = width // 2
    chips = send_ref.shape[0] * send_ref.shape[1]
    rows = send_ref.shape[3] // 3 * 2
    z, y, c = lax.axis_index(Z), lax.axis_index("y"), lax.axis_index("c")
    picked = both_ref[:, :slots, :].reshape(total, depth)
    dpicked = both_ref[:, slots:, :].reshape(total, depth)
    gate, up, low = gate_and_up(acts_ref[...])
    sigma = jax.nn.sigmoid(gate)
    hidden = gate * sigma * up
    mine = (lanes(gate.shape) >= half) == (y == 1)
    dhidden = jnp.dot(dpicked, down[...], preferred_element_type=jnp.float32)
    dhidden = jnp.where(mine, dhidden, pltpu.roll(dhidden, half, 1))
    dgate = dhidden * up * sigma * (1.0 + gate * (1.0 - sigma))
    dup = dhidden * gate * sigma
    first = 1.0 - join_ref[(z * 2 + 0) * 2 + c].astype(jnp.float32)
    second = 1.0 - join_ref[(z * 2 + 1) * 2 + c].astype(jnp.float32)
    group = lax.broadcasted_iota(jnp.int32, gate.shape, 0) // (total // 2)
    active = jnp.where(group == 0, first, second)
    dacts = (jnp.where(low, dgate, dup) * active).astype(jnp.bfloat16)
    counted = (hidden.astype(jnp.bfloat16).astype(jnp.float32) * active).astype(jnp.bfloat16)
    terms[0] = lax.dot_general(picked, dacts, ROW_DIMS, preferred_element_type=jnp.float32)
    terms[1] = lax.dot_general(dpicked, counted, ROW_DIMS, preferred_element_type=jnp.float32)
    half_rows = rows // 2
    low = lanes((half_rows, width)) < half
    for chip in range(chips):
        for k in range(2):
            base = (chip * 2 + k) * 2 * rows
            away = jnp.bitwise_xor(chip % 2, lax.rem(z, 2))
            for which, ref in ((c, keep_ref), (1 - c, send_ref)):
                at = pl.multiple_of(base + which * rows, rows)
                ref[away, chip // 2, k, :rows, :] = terms[0, pl.ds(at, rows), :].astype(ref.dtype)
                packed = jnp.where(
                    low,
                    terms[1, pl.ds(at, half_rows), :],
                    terms[1, pl.ds(at + half_rows, half_rows), :],
                )
                ref[away, chip // 2, k, rows:, :] = packed.astype(ref.dtype)


def backward(join, both, acts, down, chips):
    depth, width = down.shape
    rows = depth // chips // 4
    chunk = (2, chips // 2, 2, rows // 2 * 3, width)
    return pl.pallas_call(
        backward_kernel,
        out_shape=(
            jax.ShapeDtypeStruct(chunk, jnp.bfloat16),
            jax.ShapeDtypeStruct(chunk, jnp.float32),
        ),
        in_specs=[pl.BlockSpec(memory_space=pltpu.SMEM), *whole(3)],
        out_specs=tuple(whole(2)),
        scratch_shapes=[pltpu.VMEM((2, depth, width), jnp.float32)],
        compiler_params=params(16),
        cost_estimate=cost(8),
        name="backward",
    )(join, both, acts, down)


def add_kernel(keep_ref, got_ref, mine_ref, theirs_ref):
    half = mine_ref.shape[0]
    mine_ref[...] = keep_ref[:half] + got_ref[:half].astype(jnp.float32)
    theirs_ref[...] = (keep_ref[half:] + got_ref[half:].astype(jnp.float32)).astype(jnp.bfloat16)


def add_halves(keep, got, lasts):
    half = (keep.shape[0] // 2, *keep.shape[1:])
    return pl.pallas_call(
        add_kernel,
        out_shape=(
            jax.ShapeDtypeStruct(half, jnp.float32),
            jax.ShapeDtypeStruct(half, jnp.bfloat16),
        ),
        in_specs=whole(2),
        out_specs=tuple(whole(2)),
        compiler_params=params(8),
        cost_estimate=cost(lasts),
        name="add_halves",
    )(keep, got)


def mix_kernel(own_ref, got_ref, chooser_ref, slot_weight_ref, mixed_ref):
    total = own_ref[0] + got_ref[0].astype(jnp.float32)
    weighted = (total * slot_weight_ref[:, :1]).astype(jnp.bfloat16)
    mixed_ref[...] = lax.dot_general(
        chooser_ref[...], weighted, ROW_DIMS, preferred_element_type=jnp.float32
    ).astype(jnp.bfloat16)


def mix(own, got, chooser, slot_weight):
    return pl.pallas_call(
        mix_kernel,
        out_shape=jax.ShapeDtypeStruct((chooser.shape[1], own.shape[2]), jnp.bfloat16),
        in_specs=whole(4),
        out_specs=whole(1)[0],
        compiler_params=params(8),
        cost_estimate=cost(1),
        name="mix",
    )(own, got, chooser, slot_weight)


def finish_kernel(blocks_ref, gate_ref, up_ref, down_ref):
    rows, width = gate_ref.shape
    half = width // 2
    sums = [blocks_ref[y].astype(jnp.float32) for y in range(2)]
    for k in range(2, blocks_ref.shape[0], 2):
        for y in range(2):
            sums[y] += blocks_ref[k + y].astype(jnp.float32)
    low = lanes(sums[0].shape) < half
    firsts = jnp.where(low, sums[0], pltpu.roll(sums[1], half, 1)).astype(jnp.bfloat16)
    seconds = jnp.where(low, pltpu.roll(sums[0], half, 1), sums[1]).astype(jnp.bfloat16)
    gate_ref[...] = firsts[:rows]
    up_ref[...] = seconds[:rows]
    down_ref[: rows // 2, :] = firsts[rows:]
    down_ref[rows // 2 :, :] = seconds[rows:]


def finish(blocks):
    _, packed_rows, width = blocks.shape
    shape = jax.ShapeDtypeStruct((packed_rows // 3 * 2, width), jnp.bfloat16)
    return pl.pallas_call(
        finish_kernel,
        out_shape=(shape,) * 3,
        in_specs=whole(1),
        out_specs=tuple(whole(3)),
        compiler_params=params(4),
        name="finish",
    )(blocks)


def swapped(part, axis, distance=1):
    size = lax.axis_size(axis)
    return lax.ppermute(part, axis, [(i, i ^ distance) for i in range(size)])


def per_device(tokens, cotangent, expert_ids, route_weights, join_groups, w_gate, w_up, w_down):
    own = jnp.stack([w_gate, w_up, w_down])
    got = swapped(own, "y")
    copies, chooser, slot_weight = route(
        expert_ids, route_weights, tokens, cotangent, lax.axis_size(PLANE)
    )
    packed = pack_shards(own, got)
    packed, copies = lax.optimization_barrier((packed, copies))
    rows_in = lax.all_to_all(copies, PLANE, 0, 0, tiled=True)
    along = lax.all_gather(packed, Z, axis=0, tiled=False)
    along, rows_in = lax.optimization_barrier((along, rows_in))
    other = swapped(along, "c")
    acts, down = forward(rows_in, along, other)
    send, keep = backward(join_groups, rows_in, acts, down, lax.axis_size(Z))
    acts, keep = lax.optimization_barrier((acts, keep))
    partial, partial_send = partial_rows(rows_in, along, other, acts, down)
    partial_got = swapped(partial_send, "x", 2)
    from_core = swapped(send, "c")
    from_core, _ = lax.optimization_barrier((from_core, partial_send))
    keep, to_pair = add_halves(keep, from_core, 0.4)
    from_pair = swapped(to_pair, "zl")
    pair_sum = (keep + from_pair.astype(jnp.float32)).astype(jnp.bfloat16)
    pair_sum = pair_sum.reshape(-1, *pair_sum.shape[3:])
    pieces = lax.all_to_all(pair_sum, ("zh", "y"), 0, 0, tiled=True)
    partial, partial_send = add_halves(partial, partial_got, 2)
    partial, partial_send = add_halves(partial, swapped(partial_send, "x"), 1)
    mixed = mix(partial, swapped(partial_send, "h"), chooser, slot_weight)
    return (mixed, *finish(pieces))


def solution(mesh):
    experts = mesh.shape["expert"]
    split = Mesh(mesh.devices.reshape(-1, 2, 2, 2, 2, experts // 2), AXES)
    dp = ("zh", "zl", "y", "c")
    tok, weight = P(AXES, None), P(dp, ("h", "x"))
    return jax.shard_map(
        per_device,
        mesh=split,
        in_specs=(tok, tok, tok, tok, P(), weight, weight, weight),
        out_specs=(tok, weight, weight, weight),
        check_vma=False,
    )
```

```python
import jax
import jax.numpy as jnp
from jax import lax
from jax.experimental import pallas as pl
from jax.experimental.pallas import tpu as pltpu
from jax.sharding import Mesh
from jax.sharding import PartitionSpec as P

AXES = ("zh", "zl", "y", "c", "h", "x")
Z = ("zh", "zl")
PLANE = ("y", "h", "x")
HBM = pl.BlockSpec(memory_space=pltpu.HBM)
ROW_DIMS = (((0,), (0,)), ((), ()))
LANE_DIMS = (((1,), (1,)), ((), ()))


def whole(n):
    return [pl.BlockSpec(memory_space=pltpu.VMEM) for _ in range(n)]


def lanes(shape):
    return lax.broadcasted_iota(jnp.int32, shape, 1)


def halves_swapped(a):
    half = a.shape[1] // 2
    return pltpu.roll(a.astype(jnp.float32), half, 1)


def params(mib):
    return pltpu.CompilerParams(vmem_limit_bytes=mib * 1024 * 1024)


def cost(microseconds):
    return pl.CostEstimate(flops=int(1.1e9 * microseconds), transcendentals=0, bytes_accessed=int(3.7e6 * microseconds))


def route_kernel(
    ids_ref, share_ref, tokens_ref, cot_ref, copies_ref, chooser_ref, slot_weight_ref,
    held_ids, held_share, held_tokens, held_cot, both, chooser, weights, in_sems, out_sems, own_sems,
):
    count = ids_ref.shape[1]
    slots = chooser_ref.shape[0]
    peers = copies_ref.shape[0]
    pairs = (
        (ids_ref, held_ids), (share_ref, held_share), (tokens_ref, held_tokens), (cot_ref, held_cot)
    )
    reads = [
        pltpu.make_async_copy(src, dst, in_sems.at[k]) for k, (src, dst) in enumerate(pairs)
    ]
    for read in reads:
        read.start()
    square = (count, count)
    until = lax.broadcasted_iota(jnp.int32, square, 0) <= lanes(square)
    until = until.astype(jnp.bfloat16)
    slot = lax.broadcasted_iota(jnp.int32, (slots, count), 0).astype(jnp.float32)
    reads[0].wait()
    reads[1].wait()
    chosen = held_ids[...] == 0
    routed = jnp.max(chosen.astype(jnp.float32), axis=0, keepdims=True)
    weight = jnp.sum(jnp.where(chosen, held_share[...], 0.0), axis=0, keepdims=True)
    before = jnp.dot(
        jnp.broadcast_to(routed, (slots, count)).astype(jnp.bfloat16),
        until,
        preferred_element_type=jnp.float32,
    )
    place = jnp.where((before - 1.0 == slot) & (routed > 0.0), 1.0, 0.0)
    slot_weight = jnp.sum(place * weight, axis=1, keepdims=True)
    chooser[...] = place.astype(jnp.bfloat16)
    weights[...] = jnp.broadcast_to(slot_weight, weights.shape)
    writes = [
        pltpu.make_async_copy(chooser, chooser_ref, own_sems.at[0]),
        pltpu.make_async_copy(weights, slot_weight_ref, own_sems.at[1]),
    ]
    for write in writes:
        write.start()
    for part, held in enumerate((held_tokens, held_cot)):
        reads[2 + part].wait()
        rows = jnp.dot(chooser[...], held[...], preferred_element_type=jnp.float32)
        both[part] = (rows * slot_weight if part else rows).astype(jnp.bfloat16)
        for k in range(peers):
            writes.append(
                pltpu.make_async_copy(
                    both.at[part],
                    copies_ref.at[k, pl.ds(part * slots, slots), :],
                    out_sems.at[part, k],
                )
            )
            writes[-1].start()
    for write in writes:
        write.wait()


def route(ids, share, tokens, cot, peers):
    count, width = tokens.shape
    slots = count // 8
    top = ids.shape[1]
    return pl.pallas_call(
        route_kernel,
        out_shape=(
            jax.ShapeDtypeStruct((peers, 2 * slots, width), jnp.bfloat16),
            jax.ShapeDtypeStruct((slots, count), jnp.bfloat16),
            jax.ShapeDtypeStruct((slots, 128), jnp.float32),
        ),
        in_specs=[HBM] * 4,
        out_specs=(HBM,) * 3,
        scratch_shapes=[
            pltpu.VMEM((top, count), jnp.int32),
            pltpu.VMEM((top, count), jnp.float32),
            pltpu.VMEM((count, width), jnp.bfloat16),
            pltpu.VMEM((count, width), jnp.bfloat16),
            pltpu.VMEM((2, slots, width), jnp.bfloat16),
            pltpu.VMEM((slots, count), jnp.bfloat16),
            pltpu.VMEM((slots, 128), jnp.float32),
            pltpu.SemaphoreType.DMA((4,)),
            pltpu.SemaphoreType.DMA((2, peers)),
            pltpu.SemaphoreType.DMA((2,)),
        ],
        compiler_params=params(56),
        name="route",
    )(ids.T, share.T, tokens, cot)


def pack_kernel(own_ref, got_ref, packed_ref):
    rows, width = own_ref.shape[1:]
    low = lanes((rows, width)) < width // 2
    top = lax.axis_index("y") == 0

    def halves_of(ref):
        left, right = ref[0].astype(jnp.float32), ref[1].astype(jnp.float32)
        firsts = jnp.where(low, left, halves_swapped(right)).astype(jnp.bfloat16)
        seconds = jnp.where(low, halves_swapped(left), right).astype(jnp.bfloat16)
        return jnp.where(top, firsts, seconds), jnp.where(top, seconds, firsts)

    for k, (own, got) in enumerate(
        (*zip(halves_of(own_ref), halves_of(got_ref), strict=True), (own_ref[2], got_ref[2]))
    ):
        at = 2 * k * rows
        packed_ref[at : at + rows, :] = jnp.where(top, own, got)
        packed_ref[at + rows : at + 2 * rows, :] = jnp.where(top, got, own)


def pack_shards(own, got):
    _, rows, width = own.shape
    return pl.pallas_call(
        pack_kernel,
        out_shape=jax.ShapeDtypeStruct((6 * rows, width), own.dtype),
        in_specs=whole(2),
        out_specs=whole(1)[0],
        compiler_params=params(2),
        name="pack_shards",
    )(own, got)


def lay_out(own_ref, got_ref, part, target):
    chips, rows, _ = own_ref.shape
    rows = rows // 6
    c = lax.axis_index("c")
    for core, ref in ((c, own_ref), (1 - c, got_ref)):
        for chip in range(chips):
            for k in range(2):
                at = pl.multiple_of((chip * 2 + k) * 2 * rows + core * rows, rows)
                first = (2 * part + k) * rows
                target[pl.ds(at, rows), :] = ref[chip, first : first + rows, :]


def forward_kernel(both_ref, own_ref, got_ref, acts_ref, down, gate_up):
    peers, slots = both_ref.shape[0], both_ref.shape[1] // 2
    lay_out(own_ref, got_ref, 0, gate_up)
    lay_out(own_ref, got_ref, 2, down)
    picked = both_ref[:, :slots, :].reshape(peers * slots, both_ref.shape[2])
    acts_ref[...] = jnp.dot(picked, gate_up[...], preferred_element_type=jnp.float32)


def partial_kernel(
    both_ref, own_ref, got_ref, acts_ref, down_ref, mine_ref, theirs_ref, others, partials
):
    group_rows, width = acts_ref.shape[0] // 2, acts_ref.shape[1]
    peers, slots = both_ref.shape[0] // 2, both_ref.shape[1] // 2
    y, h, x = lax.axis_index("y"), lax.axis_index("h"), lax.axis_index("x")
    lay_out(own_ref, got_ref, 1, others)
    group = both_ref[pl.ds(y * peers, peers), :slots, :].reshape(group_rows, both_ref.shape[2])
    theirs = jnp.dot(group, others[...], preferred_element_type=jnp.float32)
    mine = acts_ref[pl.ds(pl.multiple_of(y * group_rows, group_rows), group_rows), :]
    (gate, up, low), (their_gate, their_up, _) = gate_and_up(mine), gate_and_up(theirs)
    here = jnp.logical_not(low) == (y == 1)
    gate, up = jnp.where(here, gate, their_gate), jnp.where(here, up, their_up)
    hidden = (gate * jax.nn.sigmoid(gate) * up).astype(jnp.bfloat16)
    partial = lax.dot_general(
        hidden, down_ref[...], LANE_DIMS, preferred_element_type=jnp.float32
    )
    partials[...] = partial.reshape(partials.shape)
    for high, ref in enumerate((mine_ref, theirs_ref)):
        for low_bit in range(2):
            for row in range(2):
                peer = jnp.bitwise_xor(h, row) * 4 + jnp.bitwise_xor(x, 2 * high + low_bit)
                ref[2 * low_bit + row] = partials[peer].astype(ref.dtype)


def partial_rows(both, own, got, acts, down):
    peers, doubled, depth = both.shape
    peers, slots = peers // 2, doubled // 2
    return pl.pallas_call(
        partial_kernel,
        out_shape=(
            jax.ShapeDtypeStruct((peers // 2, slots, depth), jnp.bfloat16),
            jax.ShapeDtypeStruct((peers // 2, slots, depth), jnp.bfloat16),
        ),
        in_specs=whole(5),
        out_specs=tuple(whole(2)),
        scratch_shapes=[
            pltpu.VMEM(down.shape, jnp.bfloat16),
            pltpu.VMEM((peers, slots, depth), jnp.float32),
        ],
        compiler_params=params(12),
        cost_estimate=cost(4),
        name="partial_rows",
    )(both, own, got, acts, down)


def gate_and_up(acts):
    half = acts.shape[1] // 2
    turned = pltpu.roll(acts, half, 1)
    low = lanes(acts.shape) < half
    return jnp.where(low, acts, turned), jnp.where(low, turned, acts), low


def forward(both, own, got):
    peers, doubled, depth = both.shape
    width = own.shape[2]
    return pl.pallas_call(
        forward_kernel,
        out_shape=(
            jax.ShapeDtypeStruct((peers * doubled // 2, width), jnp.float32),
            jax.ShapeDtypeStruct((depth, width), jnp.bfloat16),
        ),
        in_specs=whole(3),
        out_specs=tuple(whole(2)),
        scratch_shapes=[pltpu.VMEM((depth, width), jnp.bfloat16)],
        compiler_params=params(12),
        name="forward",
    )(both, own, got)


def backward_kernel(join_ref, both_ref, acts_ref, down, send_ref, keep_ref, terms):
    peers, slots = both_ref.shape[0], both_ref.shape[1] // 2
    depth = both_ref.shape[2]
    total, width = acts_ref.shape
    half = width // 2
    chips = send_ref.shape[0] * send_ref.shape[1]
    rows = send_ref.shape[3] // 3 * 2
    z, y, c = lax.axis_index(Z), lax.axis_index("y"), lax.axis_index("c")
    picked = both_ref[:, :slots, :].reshape(total, depth)
    dpicked = both_ref[:, slots:, :].reshape(total, depth)
    gate, up, low = gate_and_up(acts_ref[...])
    sigma = jax.nn.sigmoid(gate)
    hidden = gate * sigma * up
    mine = (lanes(gate.shape) >= half) == (y == 1)
    dhidden = jnp.dot(dpicked, down[...], preferred_element_type=jnp.float32)
    dhidden = jnp.where(mine, dhidden, pltpu.roll(dhidden, half, 1))
    dgate = dhidden * up * sigma * (1.0 + gate * (1.0 - sigma))
    dup = dhidden * gate * sigma
    first = 1.0 - join_ref[(z * 2 + 0) * 2 + c].astype(jnp.float32)
    second = 1.0 - join_ref[(z * 2 + 1) * 2 + c].astype(jnp.float32)
    group = lax.broadcasted_iota(jnp.int32, gate.shape, 0) // (total // 2)
    active = jnp.where(group == 0, first, second)
    dacts = (jnp.where(low, dgate, dup) * active).astype(jnp.bfloat16)
    counted = (hidden.astype(jnp.bfloat16).astype(jnp.float32) * active).astype(jnp.bfloat16)
    terms[0] = lax.dot_general(picked, dacts, ROW_DIMS, preferred_element_type=jnp.float32)
    terms[1] = lax.dot_general(dpicked, counted, ROW_DIMS, preferred_element_type=jnp.float32)
    half_rows = rows // 2
    low = lanes((half_rows, width)) < half
    for chip in range(chips):
        for k in range(2):
            base = (chip * 2 + k) * 2 * rows
            away = jnp.bitwise_xor(chip % 2, lax.rem(z, 2))
            for which, ref in ((c, keep_ref), (1 - c, send_ref)):
                at = pl.multiple_of(base + which * rows, rows)
                ref[away, chip // 2, k, :rows, :] = terms[0, pl.ds(at, rows), :].astype(ref.dtype)
                packed = jnp.where(
                    low,
                    terms[1, pl.ds(at, half_rows), :],
                    terms[1, pl.ds(at + half_rows, half_rows), :],
                )
                ref[away, chip // 2, k, rows:, :] = packed.astype(ref.dtype)


def backward(join, both, acts, down, chips):
    depth, width = down.shape
    rows = depth // chips // 4
    chunk = (2, chips // 2, 2, rows // 2 * 3, width)
    return pl.pallas_call(
        backward_kernel,
        out_shape=(
            jax.ShapeDtypeStruct(chunk, jnp.bfloat16),
            jax.ShapeDtypeStruct(chunk, jnp.float32),
        ),
        in_specs=[pl.BlockSpec(memory_space=pltpu.SMEM), *whole(3)],
        out_specs=tuple(whole(2)),
        scratch_shapes=[pltpu.VMEM((2, depth, width), jnp.float32)],
        compiler_params=params(16),
        cost_estimate=cost(8),
        name="backward",
    )(join, both, acts, down)


def add_kernel(keep_ref, got_ref, mine_ref, theirs_ref):
    half = mine_ref.shape[0]
    mine_ref[...] = keep_ref[:half] + got_ref[:half].astype(jnp.float32)
    theirs_ref[...] = (keep_ref[half:] + got_ref[half:].astype(jnp.float32)).astype(jnp.bfloat16)


def add_halves(keep, got, lasts):
    half = (keep.shape[0] // 2, *keep.shape[1:])
    return pl.pallas_call(
        add_kernel,
        out_shape=(
            jax.ShapeDtypeStruct(half, jnp.float32),
            jax.ShapeDtypeStruct(half, jnp.bfloat16),
        ),
        in_specs=whole(2),
        out_specs=tuple(whole(2)),
        compiler_params=params(8),
        cost_estimate=cost(lasts),
        name="add_halves",
    )(keep, got)


def mix_kernel(own_ref, got_ref, chooser_ref, slot_weight_ref, mixed_ref):
    total = own_ref[0] + got_ref[0].astype(jnp.float32)
    weighted = (total * slot_weight_ref[:, :1]).astype(jnp.bfloat16)
    mixed_ref[...] = lax.dot_general(
        chooser_ref[...], weighted, ROW_DIMS, preferred_element_type=jnp.float32
    ).astype(jnp.bfloat16)


def mix(own, got, chooser, slot_weight):
    return pl.pallas_call(
        mix_kernel,
        out_shape=jax.ShapeDtypeStruct((chooser.shape[1], own.shape[2]), jnp.bfloat16),
        in_specs=whole(4),
        out_specs=whole(1)[0],
        compiler_params=params(8),
        cost_estimate=cost(1),
        name="mix",
    )(own, got, chooser, slot_weight)


def finish_kernel(blocks_ref, gate_ref, up_ref, down_ref):
    rows, width = gate_ref.shape
    half = width // 2
    sums = [blocks_ref[y].astype(jnp.float32) for y in range(2)]
    for k in range(2, blocks_ref.shape[0], 2):
        for y in range(2):
            sums[y] += blocks_ref[k + y].astype(jnp.float32)
    low = lanes(sums[0].shape) < half
    firsts = jnp.where(low, sums[0], pltpu.roll(sums[1], half, 1)).astype(jnp.bfloat16)
    seconds = jnp.where(low, pltpu.roll(sums[0], half, 1), sums[1]).astype(jnp.bfloat16)
    gate_ref[...] = firsts[:rows]
    up_ref[...] = seconds[:rows]
    down_ref[: rows // 2, :] = firsts[rows:]
    down_ref[rows // 2 :, :] = seconds[rows:]


def finish(blocks):
    _, packed_rows, width = blocks.shape
    shape = jax.ShapeDtypeStruct((packed_rows // 3 * 2, width), jnp.bfloat16)
    return pl.pallas_call(
        finish_kernel,
        out_shape=(shape,) * 3,
        in_specs=whole(1),
        out_specs=tuple(whole(3)),
        compiler_params=params(4),
        name="finish",
    )(blocks)


def swapped(part, axis, distance=1):
    size = lax.axis_size(axis)
    return lax.ppermute(part, axis, [(i, i ^ distance) for i in range(size)])


def per_device(tokens, cotangent, expert_ids, route_weights, join_groups, w_gate, w_up, w_down):
    own = jnp.stack([w_gate, w_up, w_down])
    got = swapped(own, "y")
    copies, chooser, slot_weight = route(
        expert_ids, route_weights, tokens, cotangent, lax.axis_size(PLANE)
    )
    packed = pack_shards(own, got)
    packed, copies = lax.optimization_barrier((packed, copies))
    rows_in = lax.all_to_all(copies, PLANE, 0, 0, tiled=True)
    along = lax.all_gather(packed, Z, axis=0, tiled=False)
    along, rows_in = lax.optimization_barrier((along, rows_in))
    other = swapped(along, "c")
    acts, down = forward(rows_in, along, other)
    send, keep = backward(join_groups, rows_in, acts, down, lax.axis_size(Z))
    acts, keep = lax.optimization_barrier((acts, keep))
    partial, partial_send = partial_rows(rows_in, along, other, acts, down)
    partial_got = swapped(partial_send, "x", 2)
    from_core = swapped(send, "c")
    from_core, _ = lax.optimization_barrier((from_core, partial_send))
    keep, to_pair = add_halves(keep, from_core, 0.4)
    from_pair = swapped(to_pair, "zl")
    pair_sum = (keep + from_pair.astype(jnp.float32)).astype(jnp.bfloat16)
    pair_sum = pair_sum.reshape(-1, *pair_sum.shape[3:])
    pieces = lax.all_to_all(pair_sum, ("zh", "y"), 0, 0, tiled=True)
    partial, partial_send = add_halves(partial, partial_got, 2)
    partial, partial_send = add_halves(partial, swapped(partial_send, "x"), 1)
    mixed = mix(partial, swapped(partial_send, "h"), chooser, slot_weight)
    return (mixed, *finish(pieces))


def solution(mesh):
    experts = mesh.shape["expert"]
    split = Mesh(mesh.devices.reshape(-1, 2, 2, 2, 2, experts // 2), AXES)
    dp = ("zh", "zl", "y", "c")
    tok, weight = P(AXES, None), P(dp, ("h", "x"))
    return jax.shard_map(
        per_device,
        mesh=split,
        in_specs=(tok, tok, tok, tok, P(), weight, weight, weight),
        out_specs=(tok, weight, weight, weight),
        check_vma=False,
    )
```
